512 devices in a mesh: gx: 64 (over y, z), gy: 8 (over x, core).
Axes of the slice: x: 4, y: 8, z: 8, core: 2. Of those that a mesh axis runs over, the one named last changes fastest.
Arguments:
- pressure_rhs: float32 [512, 64, 256], P('gx', 'gy'), may hold values from -6 to 6
- accumulation: float32 [512, 64, 256], P('gx', 'gy'), may hold values from 0.02 to 0.2
- trans_x: float32 [512, 64, 256], P('gx', 'gy'), may hold values from 0.2 to 1.5
- trans_y: float32 [512, 64, 256], P('gx', 'gy'), may hold values from 0.2 to 1.5
- trans_z: float32 [512, 64, 256], P('gx', 'gy'), may hold values from 0.2 to 1.5
- well_cells: int32 [2048], P(('gx', 'gy')), may hold values from 0 to 8388607, as said below
- well_flags: int32 [2048], P(('gx', 'gy')), may hold values 0 or 1
- well_rates: float32 [2048], P(('gx', 'gy')), may hold values from 1 to 8
- well_index: float32 [2048], P(('gx', 'gy')), may hold values from 0.5 to 4
- block_map: int32 [128, 16, 64], P('gx', 'gy'), may hold values from 0 to 15
- block_inverses: float32 [16, 64, 64], replicated, may hold values from -0.006 to 0.075
Outputs:
- pressure: float32 [512, 64, 256], P('gx', 'gy')
- residual_out: float32 [512, 64, 256], P('gx', 'gy')
The draws below stay inside these ranges and needn't reach their ends.
Inputs may be any that keep to these rules, and one draw needn't show every extreme that they name: `well_cells`: entry w is a flat index (x * 64 + y) * 256 + z with x in [bx * 8, (bx + 1) * 8) and y in [by * 8, (by + 1) * 8), where b = w // 4, bx = b // 8, by = b % 8.
All inputs are finite; a program needn't handle non-finite values. No bound on the sum of `well_flags` on one device may be relied on, other than what follows from the above.
Results may differ from the reference program's by a relative error of at most 0.0003.
Values sent between devices are 32-bit elements; how exact they have to be, the bound alone decides.
A program may use at most 64 MiB of HBM per device.

```python
import math
import jax
import jax.numpy as jnp
from jax import lax

CX = 8
CY = 8
NB = 16
WELLS_DEV = 4
NX = 512
NY = 64
NZ = 256
WELLS = 2048


def draw_well_cells(key, part):
    key = jax.random.fold_in(key, 11)
    key_x, key_y, key_z = jax.random.split(key, 3)
    blocks_y = NY // CY
    well_total = WELLS_DEV * (NX // CX) * blocks_y
    slot_ids = jnp.arange(well_total, dtype=jnp.int32)
    owner_ids = slot_ids // WELLS_DEV
    block_x = owner_ids // blocks_y
    block_y = owner_ids % blocks_y
    pos_x = block_x * CX + jax.random.randint(key_x, (well_total,), 0, CX, dtype=jnp.int32)
    pos_y = block_y * CY + jax.random.randint(key_y, (well_total,), 0, CY, dtype=jnp.int32)
    pos_z = jax.random.randint(key_z, (well_total,), 0, NZ, dtype=jnp.int32)
    pos_x = jnp.where(slot_ids == 0, 0, jnp.where(slot_ids == well_total - 1, NX - 1, pos_x))
    pos_y = jnp.where(slot_ids == 0, 0, jnp.where(slot_ids == well_total - 1, NY - 1, pos_y))
    pos_z = jnp.where(slot_ids == 0, 0, jnp.where(slot_ids == well_total - 1, NZ - 1, pos_z))
    return ((pos_x * NY + pos_y) * NZ + pos_z).astype(jnp.int32)


def draw_block_inverses(key, part):
    key = jax.random.fold_in(key, 23)
    key_off, key_gain = jax.random.split(key, 2)
    spread = jnp.clip(jax.random.normal(key_off, (NB, 64, 64), jnp.float32), -4.0, 4.0) * 0.0015
    diag_gain = jax.random.uniform(key_gain, (NB, 64), jnp.float32, 0.75, 1.25)
    row_ids = jax.lax.broadcasted_iota(jnp.int32, (NB, 64, 64), 1)
    col_ids = jax.lax.broadcasted_iota(jnp.int32, (NB, 64, 64), 2)
    on_diag = row_ids == col_ids
    return jnp.where(on_diag, 0.06 * diag_gain[:, :, None], spread).astype(jnp.float32)


def set_ends(values, stream_key, smallest, top_value):
    shape = values.shape
    spot = [jax.random.randint(jax.random.fold_in(stream_key, axis), (), 0, shape[axis]) for axis in range(len(shape))]
    values = values.at[tuple(spot)].set(smallest)
    longest = shape.index(max(shape))
    spot[longest] = (spot[longest] + 1) % shape[longest]
    return values.at[tuple(spot)].set(top_value)


def steps_of(rng, dims, pieces, low, largest):
    factor_of = 1.0
    for dim, parts in pieces:
        steps = jax.random.uniform(jax.random.fold_in(jax.random.fold_in(rng, 6), dim), (parts,), jnp.float32, low / len(pieces), largest / len(pieces))
        factor_of = factor_of * jnp.repeat(jnp.exp(steps), dims[dim] // parts).reshape((-1,) + (1,) * (len(dims) - 1 - dim))
    return factor_of


def normal_values(own_key, extent, width, most, cuts=(), kind=jnp.bfloat16):
    entries = jax.random.normal(own_key, extent, jnp.float32) * width
    if len(cuts) > 0:
        entries = steps_of(own_key, extent, cuts, -0.22, 0.18) * entries
    return jnp.clip(entries, min=-most, max=most).astype(kind)


def setup_inputs(seed: int = 0) -> dict:
    key_of = jax.random.split(jax.random.key(seed), 12)
    pressure_rhs = normal_values(key_of[0], (NX, NY, NZ), 1.0, 6.0, ((0, 64), (1, 8)), jnp.float32)
    accumulation = jnp.clip(jnp.exp(math.log(0.2) - 2.3025851 * jax.random.uniform(key_of[1], (NX, NY, NZ), jnp.float32) ** steps_of(key_of[1], (NX, NY, NZ), ((0, 64), (1, 8)), -0.2, 0.2)), 0.02, 0.2)
    trans_x = jnp.clip(jnp.exp(math.log(1.5) - 2.014903 * jax.random.uniform(key_of[2], (NX, NY, NZ), jnp.float32) ** steps_of(key_of[2], (NX, NY, NZ), ((0, 64), (1, 8)), -0.2, 0.2)), 0.2, 1.5)
    trans_y = jnp.clip(jnp.exp(math.log(1.5) - 2.014903 * jax.random.uniform(key_of[3], (NX, NY, NZ), jnp.float32) ** steps_of(key_of[3], (NX, NY, NZ), ((0, 64), (1, 8)), -0.2, 0.2)), 0.2, 1.5)
    trans_z = jnp.clip(jnp.exp(math.log(1.5) - 2.014903 * jax.random.uniform(key_of[4], (NX, NY, NZ), jnp.float32) ** steps_of(key_of[4], (NX, NY, NZ), ((0, 64), (1, 8)), -0.2, 0.2)), 0.2, 1.5)
    well_cells = draw_well_cells(jax.random.fold_in(key_of[11], 71), 0)
    well_flags = set_ends((jax.random.randint(key_of[6], (WELLS,), 0, 2) < 1).astype(jnp.int32), jax.random.fold_in(key_of[6], 1), 0, 1)
    well_rates = jnp.clip(jnp.exp(math.log(8.0) - 2.0794415 * jax.random.uniform(key_of[7], (WELLS,), jnp.float32) ** steps_of(key_of[7], (WELLS,), ((0, 512),), -0.2, 0.2)), 1.0, 8.0)
    well_index = jnp.clip(jnp.exp(math.log(4.0) - 2.0794415 * jax.random.uniform(key_of[8], (WELLS,), jnp.float32) ** steps_of(key_of[8], (WELLS,), ((0, 512),), -0.2, 0.2)), 0.5, 4.0)
    block_map = set_ends(jax.random.randint(key_of[9], (NX // 4, NY // 4, NZ // 4), 0, NB), jax.random.fold_in(key_of[9], 1), 0, NB - 1).astype(jnp.int32)
    block_inverses = draw_block_inverses(jax.random.fold_in(key_of[11], 71), 0)
    return dict(pressure_rhs=pressure_rhs, accumulation=accumulation, trans_x=trans_x, trans_y=trans_y, trans_z=trans_z, well_cells=well_cells, well_flags=well_flags, well_rates=well_rates, well_index=well_index, block_map=block_map, block_inverses=block_inverses)


OMEGA_FINE = 0.8
OMEGA_COARSE = 0.8
HIGHEST_PREC = lax.Precision.HIGHEST

def step_up(array_in, dimension):
    widths = [(0, 0)] * array_in.ndim
    widths[dimension] = (0, 1)
    return lax.slice_in_dim(jnp.pad(array_in, widths), 1, array_in.shape[dimension] + 1, axis=dimension)

def step_down(array_in, dimension):
    widths = [(0, 0)] * array_in.ndim
    widths[dimension] = (1, 0)
    return lax.slice_in_dim(jnp.pad(array_in, widths), 0, array_in.shape[dimension], axis=dimension)

def agg_sum(values):
    size_x, size_y, size_z = values.shape
    return values.reshape(size_x // 4, 4, size_y // 4, 4, size_z // 4, 4).sum(axis=(1, 3, 5))

def pair_sum(values):
    size_x, size_y, size_z = values.shape
    return values.reshape(size_x // 2, 2, size_y, size_z // 2, 2).sum(axis=(1, 4))

def prolong_pair(values):
    return jnp.repeat(jnp.repeat(values, 2, axis=0), 2, axis=2)

def prolong_agg(values):
    return jnp.repeat(jnp.repeat(jnp.repeat(values, 4, axis=0), 4, axis=1), 4, axis=2)

def to_columns(values):
    size_x, size_y, size_z = values.shape
    blocks = values.reshape(size_x // 4, 4, size_y // 4, 4, size_z // 4, 4)
    return blocks.transpose(1, 3, 5, 0, 2, 4).reshape(64, -1)

def from_columns(columns, dims_all):
    size_x, size_y, size_z = dims_all
    blocks = columns.reshape(4, 4, 4, size_x // 4, size_y // 4, size_z // 4)
    return blocks.transpose(3, 0, 4, 1, 5, 2).reshape(size_x, size_y, size_z)

def block_smooth(resid_in, block_map, block_inverses):
    columns = to_columns(resid_in)
    kind_ids = block_map.reshape(1, -1)

    def add_kind(kind_index, running):
        product = jnp.dot(block_inverses[kind_index], columns, precision=HIGHEST_PREC)
        return running + jnp.where(kind_ids == kind_index, product, 0.0)
    chosen = lax.fori_loop(0, block_inverses.shape[0], add_kind, jnp.zeros_like(columns))
    return from_columns(chosen, resid_in.shape)

def fine_apply(field_in, diag_total, masked_x, masked_y, masked_z):
    result = diag_total * field_in
    result = result + masked_x * (field_in - step_up(field_in, 0)) + step_down(masked_x, 0) * (field_in - step_down(field_in, 0))
    result = result + masked_y * (field_in - step_up(field_in, 1)) + step_down(masked_y, 1) * (field_in - step_down(field_in, 1))
    result = result + masked_z * (field_in - step_up(field_in, 2)) + step_down(masked_z, 2) * (field_in - step_down(field_in, 2))
    return result

def level_one(diag_total, trans_x, trans_y, trans_z):
    size_x, size_y, size_z = diag_total.shape
    base_diag = agg_sum(diag_total)
    coarse_x = trans_x[3::4].reshape(size_x // 4, size_y // 4, 4, size_z // 4, 4).sum(axis=(2, 4))
    coarse_y = trans_y[:, 3::4].reshape(size_x // 4, 4, size_y // 4, size_z // 4, 4).sum(axis=(1, 4))
    coarse_z = trans_z[:, :, 3::4].reshape(size_x // 4, 4, size_y // 4, 4, size_z // 4).sum(axis=(1, 3))
    return (base_diag, coarse_x, coarse_y, coarse_z)

def pair_level(operators):
    base_diag, coarse_x, coarse_y, coarse_z = operators
    size_x, size_y, size_z = base_diag.shape
    next_x = coarse_x[1::2].reshape(size_x // 2, size_y, size_z // 2, 2).sum(axis=3)
    next_z = coarse_z[:, :, 1::2].reshape(size_x // 2, 2, size_y, size_z // 2).sum(axis=1)
    return (pair_sum(base_diag), next_x, pair_sum(coarse_y), next_z)

def level_terms(trans_x, trans_y, trans_z, group_x, group_y):
    row_iota = lax.broadcasted_iota(jnp.int32, trans_x.shape, 0)
    col_iota = lax.broadcasted_iota(jnp.int32, trans_x.shape, 1)
    depth_iota = lax.broadcasted_iota(jnp.int32, trans_x.shape, 2)
    masked_x = jnp.where((row_iota + 1) % group_x != 0, trans_x, 0.0)
    masked_y = jnp.where((col_iota + 1) % group_y != 0, trans_y, 0.0)
    masked_z = jnp.where(depth_iota + 1 < trans_z.shape[2], trans_z, 0.0)
    return (masked_x, masked_y, masked_z)

def level_diag(base_diag, masked):
    masked_x, masked_y, masked_z = masked
    return base_diag + masked_x + step_down(masked_x, 0) + masked_y + step_down(masked_y, 1) + masked_z + step_down(masked_z, 2)

def level_apply(field_in, base_diag, masked):
    return fine_apply(field_in, base_diag, masked[0], masked[1], masked[2])

def descend(resid_in, operators, group_x, group_y):
    masked = level_terms(operators[1], operators[2], operators[3], group_x, group_y)
    diag_cell = level_diag(operators[0], masked)
    correction = OMEGA_COARSE * resid_in / diag_cell
    correction = correction + OMEGA_COARSE * (resid_in - level_apply(correction, operators[0], masked)) / diag_cell
    leftover = resid_in - level_apply(correction, operators[0], masked)
    return (correction, pair_sum(leftover))

def dense_solve(resid_in, diag_cell, masked_x, masked_y, masked_z):
    size_x, size_y, size_z = resid_in.shape
    count_all = size_x * size_y * size_z
    matrix = jnp.diag(diag_cell.reshape(-1))
    for values, offset in ((masked_z, 1), (masked_y, size_z), (masked_x, size_y * size_z)):
        if offset < count_all:
            band_vals = values.reshape(-1)[:count_all - offset]
            matrix = matrix - jnp.diag(band_vals, offset) - jnp.diag(band_vals, -offset)
    factor = jnp.linalg.cholesky(matrix)
    solved = jax.scipy.linalg.cho_solve((factor, True), resid_in.reshape(-1))
    return solved.reshape(resid_in.shape)

def group_solve(resid_in, operators, group_x, group_y):
    masked = level_terms(operators[1], operators[2], operators[3], group_x, group_y)
    diag_cell = level_diag(operators[0], masked)
    size_x, size_y, size_z = resid_in.shape

    def to_groups(values):
        return values.reshape(size_x // group_x, group_x, size_y // group_y, group_y, size_z).transpose(0, 2, 1, 3, 4).reshape(-1, group_x, group_y, size_z)
    solved = jax.vmap(dense_solve)(to_groups(resid_in), to_groups(diag_cell), to_groups(masked[0]), to_groups(masked[1]), to_groups(masked[2]))
    return solved.reshape(size_x // group_x, size_y // group_y, group_x, group_y, size_z).transpose(0, 2, 1, 3, 4).reshape(resid_in.shape)

def reference(pressure_rhs, accumulation, trans_x, trans_y, trans_z, well_cells, well_flags, well_rates, well_index, block_map, block_inverses):
    dims_all = pressure_rhs.shape
    cell_count = dims_all[0] * dims_all[1] * dims_all[2]
    well_diag = jnp.zeros((cell_count,), jnp.float32).at[well_cells].add(well_index).reshape(dims_all)
    signed_rates = jnp.where(well_flags == 1, well_rates, -well_rates)
    well_source = jnp.zeros((cell_count,), jnp.float32).at[well_cells].add(signed_rates).reshape(dims_all)
    diag_total = accumulation + well_diag
    source = pressure_rhs + well_source
    row_iota = lax.broadcasted_iota(jnp.int32, dims_all, 0)
    col_iota = lax.broadcasted_iota(jnp.int32, dims_all, 1)
    depth_iota = lax.broadcasted_iota(jnp.int32, dims_all, 2)
    masked_x = jnp.where(row_iota == dims_all[0] - 1, 0.0, trans_x)
    masked_y = jnp.where(col_iota == dims_all[1] - 1, 0.0, trans_y)
    masked_z = jnp.where(depth_iota == dims_all[2] - 1, 0.0, trans_z)

    def apply_fine(field_in):
        return fine_apply(field_in, diag_total, masked_x, masked_y, masked_z)

    def smooth_fine(resid_in):
        return OMEGA_FINE * block_smooth(resid_in, block_map, block_inverses)
    iterate_one = smooth_fine(source)
    iterate_two = iterate_one + smooth_fine(source - apply_fine(iterate_one))
    resid_two = source - apply_fine(iterate_two)
    group_x = CX // 2
    group_y = CY // 4
    operators = level_one(diag_total, trans_x, trans_y, trans_z)
    coarse_res = agg_sum(resid_two)
    corrections = []
    for level_step in range(3):
        correction, coarse_res = descend(coarse_res, operators, group_x, group_y)
        corrections.append(correction)
        operators = pair_level(operators)
    solved = group_solve(coarse_res, operators, group_x, group_y)
    for level_step in (2, 1, 0):
        solved = corrections[level_step] + prolong_pair(solved)
    iterate_three = iterate_two + prolong_agg(solved)
    iterate_four = iterate_three + smooth_fine(source - apply_fine(iterate_three))
    pressure = iterate_four + smooth_fine(source - apply_fine(iterate_four))
    residual_out = source - apply_fine(pressure)
    return (pressure, residual_out)
```

```python
import functools

import jax
import jax.numpy as jnp
from jax import lax
from jax.experimental import pallas as pl
from jax.experimental.pallas import tpu as pltpu
from jax.sharding import PartitionSpec as P

OMEGA = 0.8
GROUP = 16
SIZE = 8
DEPTH = 256
KINDS = 16
WELLS = 4
DOUBLINGS = 10
MESH = pl.DeviceIdType.MESH
HIGHEST = lax.Precision.HIGHEST
F32 = jnp.float32
BF16 = jnp.bfloat16
FIELD = (2, SIZE, SIZE, 128)


def iota(shape, dim):
    return lax.broadcasted_iota(jnp.int32, shape, dim)


def roll(values, shift, axis):
    return pltpu.roll(values, shift % values.shape[axis], axis)


def split_three(values):
    high = values.astype(BF16)
    rest = values - high.astype(F32)
    middle = rest.astype(BF16)
    low = (rest - middle.astype(F32)).astype(BF16)
    return high, middle, low


def split_two(values):
    high = values.astype(BF16)
    low = (values - high.astype(F32)).astype(BF16)
    return high, low


def times_ones(values, ones):
    return sum(jnp.dot(part, ones, preferred_element_type=F32) for part in split_three(values))


def flat(field):
    return jnp.concatenate(
        [field[0].reshape(SIZE * SIZE, 128), field[1].reshape(SIZE * SIZE, 128)], axis=1
    )


def unflat(rows):
    shape = (1, SIZE, SIZE, 128)
    return jnp.concatenate(
        [rows[:, :128].reshape(shape), rows[:, 128:].reshape(shape)], axis=0
    )


def lane_roll(field, shift):
    return roll(field.reshape(-1, 8, 128), shift, 2).reshape(field.shape)


def row_roll(field, shift):
    return roll(field.reshape(-1, 8, 128), shift, 1).reshape(field.shape)


def z_neighbours(field):
    low, high = field[0], field[1]
    lower_lanes = iota(low.shape, 2) < 64
    across = lane_roll(jnp.where(lower_lanes, high, low), 64)
    up = [across, jnp.where(lower_lanes, lane_roll(high, 64), lane_roll(low, 63))]
    down = [jnp.where(lower_lanes, lane_roll(high, 65), lane_roll(low, 64)), across]
    return (
        jnp.concatenate([part[None] for part in up], axis=0),
        jnp.concatenate([part[None] for part in down], axis=0),
    )


def turned(field):
    shape = (field.size // 1024, 8, 128)
    same = (iota(shape, 1) >= 4) == (iota(shape, 2) >= 64)
    tiles = field.reshape(shape)
    return jnp.where(same, tiles, roll(roll(tiles, 4, 1), 64, 2)).reshape(field.shape)


def agg_rows(tile):
    tile = tile + roll(tile, 64, 1)
    tile = tile + roll(tile, -1, 0)
    tile = tile + roll(tile, -2, 0)
    return jnp.where(iota((1, 128), 1) < 64, tile[0:1], tile[4:5])


def xor_sum(values, step, axis):
    place = iota(values.shape, axis)
    return values + jnp.where(
        (place & step) == 0, roll(values, -step, axis), roll(values, step, axis)
    )


def xor_upper(values, step, axis):
    place = iota(values.shape, axis)
    return jnp.where((place & step) == 0, roll(values, -step, axis), values)


def kernel(
    count_x,
    count_y,
    rhs_any,
    acc_any,
    tx_any,
    ty_any,
    tz_any,
    cells,
    flags,
    rates,
    well_index,
    map_any,
    inv_any,
    pressure_any,
    resid_any,
    fields_in,
    map_in,
    inv_in,
    blocks,
    source,
    coef,
    face_x,
    face_y,
    halo_x,
    halo_y,
    ends_in,
    ends_send,
    gop_send,
    gop,
    gres_send,
    gres,
    tail,
    tail_send,
    tail_in,
    out_buf,
    load_sem,
    store_sem,
    face_send_sem,
    face_recv_sem,
    gop_send_sem,
    gop_recv_sem,
    gres_send_sem,
    gres_recv_sem,
    tail_send_sem,
    tail_recv_sem,
):
    index_x = lax.axis_index("gx")
    index_y = lax.axis_index("gy")
    rank = lax.rem(index_x, GROUP)
    base = index_x - rank
    next_x = (lax.rem(index_x + 1, count_x), index_y)
    prev_x = (lax.rem(index_x + count_x - 1, count_x), index_y)
    next_y = (index_x, lax.rem(index_y + 1, count_y))
    prev_y = (index_x, lax.rem(index_y + count_y - 1, count_y))
    sides = (next_x, prev_x, next_y, prev_y)
    mates = [(base + lax.rem(rank + step, GROUP), index_y) for step in range(1, GROUP)]

    loads = [
        pltpu.make_async_copy(src, dst, load_sem.at[place])
        for place, (src, dst) in enumerate(
            (
                (inv_any, inv_in),
                (rhs_any, fields_in.at[0]),
                (tx_any, fields_in.at[1]),
                (ty_any, fields_in.at[2]),
                (tz_any, fields_in.at[3]),
                (acc_any, fields_in.at[4]),
                (map_any, map_in),
            )
        )
    ]
    for load in loads:
        load.start()
    barrier = pltpu.get_barrier_semaphore()
    for device in sides + tuple(mates):
        pl.semaphore_signal(barrier, inc=1, device_id=device, device_id_type=MESH)

    row = iota((DEPTH, DEPTH), 0)
    col = iota((DEPTH, DEPTH), 1)
    to_inside = (row == 4 * (col & 63) + (col >> 6)).astype(F32).astype(BF16)
    to_outside = (col == 4 * (row & 63) + (row >> 6)).astype(F32).astype(BF16)
    lane = iota(FIELD, 3)
    second = iota(FIELD, 2)
    first = iota(FIELD, 1)
    half = iota(FIELD, 0)
    cell_id = ((half * SIZE + first) * SIZE + second) * 128 + lane

    def swapped_offsets(place):
        return (place & ~15) | ((place & 3) << 2) | ((place >> 2) & 3)

    take_rows = (col == swapped_offsets(row)).astype(F32).astype(BF16)
    row_k = iota((64, DEPTH), 0)
    col_k = iota((64, DEPTH), 1)
    take_cols = row_k == swapped_offsets(col_k & 63)
    take_high = (take_cols & (col_k < 128)).astype(F32).astype(BF16)
    take_low = (take_cols & (col_k >= 128)).astype(F32).astype(BF16)
    loads[0].wait()
    for part in range(KINDS // 4):
        here = slice(part * DEPTH, (part + 1) * DEPTH)
        high, low = split_two(OMEGA * inv_in[here, :])
        both = jnp.dot(high, take_high, preferred_element_type=F32) + jnp.dot(
            low, take_low, preferred_element_type=F32
        )
        blocks[here, :] = jnp.dot(
            take_rows, both.astype(BF16), preferred_element_type=F32
        ).astype(BF16)

    plane_cells = SIZE * count_y * DEPTH
    well_ids = []
    for well in range(WELLS):
        cell = cells[well]
        pos_x = cell // plane_cells - index_x * SIZE
        left = lax.rem(cell, plane_cells)
        pos_y = left // DEPTH - index_y * SIZE
        pos_z = lax.rem(left, DEPTH)
        place = lax.rem(pos_z, 4) * 64 + pos_z // 4
        well_ids.append(
            ((place // 128 * SIZE + pos_x) * SIZE + pos_y) * 128 + lax.rem(place, 128)
        )
    signed = [
        jnp.where(flags[well] == 1, rates[well], -rates[well]) for well in range(WELLS)
    ]

    loads[1].wait()
    well_source = jnp.zeros(FIELD, F32)
    for well in range(WELLS):
        well_source = well_source + jnp.where(cell_id == well_ids[well], signed[well], 0.0)
    source[...] = (
        unflat(times_ones(fields_in[0].reshape(SIZE * SIZE, DEPTH), to_inside)) + well_source
    )

    loads[6].wait()
    kinds = []
    for part in range(2):
        kind = map_in[part]
        kinds.append(jnp.concatenate([kind[0:1], kind[1:2]], axis=1))
    kind_ids = jnp.broadcast_to(jnp.concatenate(kinds, axis=1), (8, 256))

    def smooth(resid):
        tiles = turned(resid)
        columns = jnp.concatenate(
            [
                jnp.concatenate(
                    [
                        tiles[half_id, 4 * part + offset]
                        for offset in range(4)
                        for half_id in range(2)
                    ],
                    axis=0,
                )
                for part in range(2)
            ],
            axis=1,
        )
        high, low = split_two(columns)
        product = jnp.dot(
            blocks[...],
            jnp.concatenate([high, low, high, low], axis=0),
            preferred_element_type=F32,
        )
        chosen = product[0:64]
        for kind in range(1, KINDS):
            mask = jnp.broadcast_to((kind_ids == kind)[None], (8, 8, 256)).reshape(64, 256)
            chosen = jnp.where(mask, product[64 * kind : 64 * kind + 64], chosen)
        back = [
            [
                chosen[8 * (2 * offset + half_id) : 8 * (2 * offset + half_id) + 8,
                       128 * part : 128 * part + 128][None]
                for part in range(2)
                for offset in range(4)
            ]
            for half_id in range(2)
        ]
        field = jnp.concatenate(
            [jnp.concatenate(tiles, axis=0)[None] for tiles in back], axis=0
        )
        return turned(field)

    def send_faces(step, field):
        face_x[step, 0] = field[:, SIZE - 1]
        face_x[step, 1] = field[:, 0]
        tiles = field.reshape(2 * SIZE, 8, 128)
        face_y[step, 0] = tiles[:, 7:8, :]
        face_y[step, 1] = tiles[:, 0:1, :]
        copies = []
        for side, (out, into) in enumerate(
            ((face_x, halo_x), (face_x, halo_x), (face_y, halo_y), (face_y, halo_y))
        ):
            copies.append(
                pltpu.make_async_remote_copy(
                    src_ref=out.at[step, side % 2],
                    dst_ref=into.at[step, side % 2],
                    send_sem=face_send_sem.at[step, side],
                    recv_sem=face_recv_sem.at[step, side],
                    device_id=sides[side],
                    device_id_type=MESH,
                )
            )
        for copy in copies:
            copy.start()
        return copies

    iterate = smooth(source[...])

    pl.semaphore_wait(barrier, len(sides) + len(mates))
    pending = []
    copies = send_faces(0, iterate)
    pending += copies

    loads[2].wait()
    loads[3].wait()
    ends_send[0, 0] = fields_in[1, SIZE - 1]
    for place in range(SIZE):
        ends_send[0, 1, place : place + 1] = fields_in[2, place, SIZE - 1 : SIZE, :]
    ends = []
    for side in range(2):
        ends.append(
            pltpu.make_async_remote_copy(
                src_ref=ends_send.at[0, side],
                dst_ref=ends_in.at[0, side],
                send_sem=face_send_sem.at[4, side],
                recv_sem=face_recv_sem.at[4, side],
                device_id=sides[2 * side],
                device_id_type=MESH,
            )
        )
        ends[-1].start()
    pending += ends

    loads[4].wait()
    loads[5].wait()
    inside = times_ones(
        fields_in[1:5].reshape(4 * SIZE * SIZE, DEPTH), to_inside
    )
    tx, ty, tz, acc = [unflat(inside[64 * place : 64 * place + 64]) for place in range(4)]
    well_diag = jnp.zeros(FIELD, F32)
    for well in range(WELLS):
        well_diag = well_diag + jnp.where(cell_id == well_ids[well], well_index[well], 0.0)
    diag = acc + well_diag
    tx = jnp.where((first == SIZE - 1) & (index_x == count_x - 1), 0.0, tx)
    ty = jnp.where((second == SIZE - 1) & (index_y == count_y - 1), 0.0, ty)
    tz = jnp.where((half == 1) & (lane == 127), 0.0, tz)

    for part in range(2):
        mine = slice(4 * part, 4 * part + 4)
        gop_send[part : part + 1] = agg_rows(diag[:, mine].sum(axis=(0, 1)))
        gop_send[2 + part : 3 + part] = agg_rows(tx[:, 4 * part + 3].sum(axis=0))
        tile = ty[:, mine].sum(axis=(0, 1))
        tile = tile + roll(tile, 64, 1)
        gop_send[4 + part : 5 + part] = jnp.where(
            iota((1, 128), 1) < 64, tile[3:4], tile[7:8]
        )
        tile = tz[1, mine].sum(axis=0)
        gop_send[6 + part : 7 + part] = agg_rows(
            jnp.where(iota((8, 128), 1) >= 64, tile, 0.0)
        )

    def gather(mine, every, send_sem, recv_sem):
        copies = []
        for step, device in enumerate(mates):
            copies.append(
                pltpu.make_async_remote_copy(
                    src_ref=mine,
                    dst_ref=every.at[rank],
                    send_sem=send_sem.at[step],
                    recv_sem=recv_sem.at[step],
                    device_id=device,
                    device_id_type=MESH,
                )
            )
        for copy in copies:
            copy.start()
        every[rank] = mine[...]
        return copies

    gop_copies = gather(gop_send, gop, gop_send_sem, gop_recv_sem)
    pending += gop_copies

    tz_down = jnp.where((half == 0) & (lane == 0), 0.0, z_neighbours(tz)[1])
    for copy in ends:
        copy.wait_recv()
    end_rows = times_ones(ends_in[0].reshape(2 * SIZE, DEPTH), to_inside)
    end_x = jnp.where(index_x == 0, 0.0, end_rows[0:SIZE])
    end_y = jnp.where(index_y == 0, 0.0, end_rows[SIZE:])
    end_x = jnp.concatenate([end_x[None, None, :, :128], end_x[None, None, :, 128:]], axis=0)
    tx_down = jnp.concatenate([end_x, tx[:, : SIZE - 1]], axis=1)
    end_y = jnp.concatenate(
        [
            jnp.broadcast_to(
                end_y[place : place + 1, 128 * part : 128 * part + 128], (8, 128)
            )[None]
            for part in range(2)
            for place in range(SIZE)
        ],
        axis=0,
    ).reshape(FIELD)
    ty_in = jnp.where(second == SIZE - 1, 0.0, ty)
    ty_down_in = row_roll(ty_in, 1)
    ty_edge = ty - ty_in
    ty_down_edge = jnp.where(second == 0, end_y, 0.0)
    coef[0] = (
        diag + tx + tx_down + ty + ty_down_in + ty_down_edge + tz + tz_down
    )
    coef[1] = tx
    coef[2] = tx_down
    coef[3] = ty_in
    coef[4] = ty_down_in
    coef[5] = tz
    coef[6] = tz_down
    coef[7] = ty_edge
    coef[8] = ty_down_edge

    def resid_base(field):
        nothing = jnp.zeros((2, 1, SIZE, 128), F32)
        up_z, down_z = z_neighbours(field)
        return (
            source[...]
            - coef[0] * field
            + coef[1] * jnp.concatenate([field[:, 1:], nothing], axis=1)
            + coef[2] * jnp.concatenate([nothing, field[:, : SIZE - 1]], axis=1)
            + coef[3] * row_roll(field, -1)
            + coef[4] * row_roll(field, 1)
            + coef[5] * up_z
            + coef[6] * down_z
        )

    def resid_edges(resid, high_x, low_x, high_y, low_y):
        first_row = resid[:, 0:1] + (coef[2, :, 0] * low_x)[:, None]
        last_row = resid[:, SIZE - 1 :] + (coef[1, :, SIZE - 1] * high_x)[:, None]
        resid = jnp.concatenate([first_row, resid[:, 1 : SIZE - 1], last_row], axis=1)
        return resid + coef[7] * high_y + coef[8] * low_y

    def halos(step):
        spread = [
            jnp.broadcast_to(halo_y[step, side], (2 * SIZE, 8, 128)).reshape(FIELD)
            for side in (1, 0)
        ]
        return halo_x[step, 1], halo_x[step, 0], spread[0], spread[1]

    resid = resid_base(iterate)
    for copy in copies:
        copy.wait_recv()
    resid = resid_edges(resid, *halos(0))
    iterate = iterate + smooth(resid)

    copies = send_faces(1, iterate)
    pending += copies
    resid = resid_base(iterate)

    for copy in gop_copies:
        copy.wait_recv()
    shape = (GROUP, 128)
    member = iota(shape, 0)
    lane_c = iota(shape, 1)
    deep = lane_c & 63
    base_a, base_b, tx_a, tx_b, ty_a, ty_b, tz_a, tz_b = [
        gop[:, place, :] for place in range(8)
    ]

    def y_terms(values):
        return jnp.where(lane_c < 64, values, roll(values, 64, 1))

    def z_terms(values, step):
        up = jnp.where(deep < 64 - step, values, 0.0)
        down = jnp.where(deep >= step, roll(values, step, 1), 0.0)
        return up, down

    across_up = jnp.where((member & 1) == 0, tx_b, 0.0)
    across_down = jnp.where((member & 1) == 1, roll(tx_b, 1, 0), 0.0)
    y_a, y_b = y_terms(ty_a), y_terms(ty_b)
    (zu_a, zd_a), (zu_b, zd_b) = z_terms(tz_a, 1), z_terms(tz_b, 1)
    diag_a = base_a + tx_a + across_down + y_a + zu_a + zd_a
    diag_b = base_b + tx_a + across_up + y_b + zu_b + zd_b
    weight_a, weight_b = OMEGA / diag_a, OMEGA / diag_b

    def apply_one(field_a, field_b):
        out_a = (
            diag_a * field_a
            - tx_a * field_b
            - across_down * roll(field_b, 1, 0)
            - y_a * roll(field_a, 64, 1)
            - zu_a * roll(field_a, -1, 1)
            - zd_a * roll(field_a, 1, 1)
        )
        out_b = (
            diag_b * field_b
            - tx_a * field_a
            - across_up * roll(field_a, -1, 0)
            - y_b * roll(field_b, 64, 1)
            - zu_b * roll(field_b, -1, 1)
            - zd_b * roll(field_b, 1, 1)
        )
        return out_a, out_b

    levels = []
    base_k = xor_sum(base_a + base_b, 1, 1)
    tx_k = xor_sum(tx_b, 1, 1)
    ty_k = xor_sum(ty_a + ty_b, 1, 1)
    tz_k = xor_upper(tz_a + tz_b, 1, 1)
    for level in range(2, 5):
        step_x, step_z = 1 << (level - 2), 1 << (level - 1)
        cell_x = member >> (level - 2)
        up_x = jnp.where((cell_x & 3) != 3, tx_k, 0.0)
        down_x = jnp.where((cell_x & 3) != 0, roll(tx_k, step_x, 0), 0.0)
        both_y = y_terms(ty_k)
        up_z, down_z = z_terms(tz_k, step_z)
        diag_k = base_k + up_x + down_x + both_y + up_z + down_z
        levels.append((diag_k, up_x, down_x, both_y, up_z, down_z, step_x, step_z))
        if level < 4:
            base_k = xor_sum(xor_sum(base_k, step_x, 0), step_z, 1)
            ty_k = xor_sum(xor_sum(ty_k, step_x, 0), step_z, 1)
            tx_k = xor_sum(xor_upper(tx_k, step_x, 0), step_z, 1)
            tz_k = xor_upper(xor_sum(tz_k, step_x, 0), step_z, 1)

    def apply_level(field, terms):
        diag_k, up_x, down_x, both_y, up_z, down_z, step_x, step_z = terms
        return (
            diag_k * field
            - up_x * roll(field, -step_x, 0)
            - down_x * roll(field, step_x, 0)
            - both_y * roll(field, 64, 1)
            - up_z * roll(field, -step_z, 1)
            - down_z * roll(field, step_z, 1)
        )

    lane_row = iota((128, 128), 0)
    lane_col = iota((128, 128), 1)
    real = lane_col < 64
    same_place = ((lane_row >> 6) == ((lane_col >> 3) & 1)) & (
        ((lane_row & 63) >> 3) == (lane_col & 7)
    )
    pick_one = (real & same_place & ((lane_row & 7) == 0)).astype(F32).astype(BF16)
    pick_two = (real & same_place & ((lane_row & 3) == 0)).astype(F32).astype(BF16)
    own_x = (member >> 2) == (lane_c >> 4)
    diag_k, up_x, down_x, both_y, up_z, down_z, _, _ = levels[2]
    picked = times_ones(
        jnp.concatenate(
            [1.0 / diag_k, up_x, down_x, both_y, up_z, down_z], axis=0
        ),
        pick_one,
    )
    one_member = own_x & ((member & 3) == 0)
    inverse_diag, up_x, down_x, both_y, up_z, down_z = [
        jnp.sum(
            jnp.where(one_member, picked[GROUP * place : GROUP * place + GROUP], 0.0),
            axis=0,
            keepdims=True,
        )
        for place in range(6)
    ]
    gap = lane_row - lane_col
    upper_y = (lane_col >> 3) & 1
    coupling = jnp.where(gap == 16, up_x, 0.0)
    coupling = jnp.where(gap == -16, down_x, coupling)
    coupling = jnp.where(gap == 8 - 16 * upper_y, both_y, coupling)
    coupling = jnp.where(gap == 1, up_z, coupling)
    coupling = jnp.where(gap == -1, down_z, coupling)
    power = coupling * inverse_diag
    total = power + jnp.where(gap == 0, 1.0, 0.0)
    for _ in range(DOUBLINGS):
        power = jnp.dot(power, power, precision=HIGHEST, preferred_element_type=F32)
        total = total + jnp.dot(
            total, power, precision=HIGHEST, preferred_element_type=F32
        )
    spread = jnp.concatenate(
        [
            ((lane_row >> 4) == part)
            & ((lane_row >> 3 & 1) == (lane_col >> 6))
            & ((lane_row & 7) == ((lane_col & 63) >> 3))
            & (lane_row < 64)
            for part in range(4)
        ],
        axis=1,
    )
    solver = times_ones(total, spread.astype(F32).astype(BF16))

    for copy in copies:
        copy.wait_recv()
    high_x, low_x, high_y, low_y = halos(1)
    resid = resid_edges(resid, high_x, low_x, high_y, low_y)

    for part in range(2):
        gres_send[:, 128 * part : 128 * part + 128] = agg_rows(
            resid[:, 4 * part : 4 * part + 4].sum(axis=(0, 1))
        )
    gres_copies = gather(gres_send, gres, gres_send_sem, gres_recv_sem)
    pending += gres_copies
    for copy in gres_copies:
        copy.wait_recv()
    every = gres[:, 0, :]
    res_a, res_b = every[:, :128], every[:, 128:]

    def descend_one(res_a, res_b):
        cor_a, cor_b = weight_a * res_a, weight_b * res_b
        out_a, out_b = apply_one(cor_a, cor_b)
        cor_a = cor_a + weight_a * (res_a - out_a)
        cor_b = cor_b + weight_b * (res_b - out_b)
        out_a, out_b = apply_one(cor_a, cor_b)
        return cor_a, cor_b, (res_a - out_a) + (res_b - out_b)

    cor_a, cor_b, left = descend_one(res_a, res_b)
    res_k = xor_sum(left, 1, 1)
    cor_k = jnp.zeros(shape, F32)
    for level in (2, 3):
        terms = levels[level - 2]
        weight = OMEGA / terms[0]
        cor = weight * res_k
        cor = cor + weight * (res_k - apply_level(cor, terms))
        left = res_k - apply_level(cor, terms)
        cor_k = cor_k + cor
        if level == 2:
            res_k = xor_sum(xor_sum(left, 1, 0), 2, 1)
    last = times_ones(left, pick_two)
    last = jnp.sum(
        jnp.where(own_x & ((member & 1) == 0), last, 0.0), axis=0, keepdims=True
    )
    last = jnp.broadcast_to(last * inverse_diag, (8, 128))
    solved = jnp.dot(last, solver, precision=HIGHEST, preferred_element_type=F32)
    solved = [jnp.broadcast_to(solved[0:1, 128 * part : 128 * part + 128], (8, 128)) for part in range(4)]
    upper_rows = (iota((8, 128), 0) & 4) != 0
    cor_k = cor_k + jnp.concatenate(
        [
            jnp.where(upper_rows, solved[1], solved[0]),
            jnp.where(upper_rows, solved[3], solved[2]),
        ],
        axis=0,
    )
    tail[0] = cor_a + cor_k
    tail[1] = cor_b + cor_k
    tail_send[0] = tail[0, pl.ds(rank, 1), :]
    tail_send[1] = tail[1, pl.ds(rank, 1), :]
    tails = []
    for side in range(4):
        tails.append(
            pltpu.make_async_remote_copy(
                src_ref=tail_send,
                dst_ref=tail_in.at[side],
                send_sem=tail_send_sem.at[side],
                recv_sem=tail_recv_sem.at[side],
                device_id=sides[side],
                device_id_type=MESH,
            )
        )
        tails[-1].start()
    pending += tails

    def over_aggregates(line):
        return turned(jnp.broadcast_to(line, (8, 128)))

    added = [over_aggregates(tail_send[part]) for part in range(2)]
    added = jnp.concatenate([added[place // 4][None] for place in range(SIZE)], axis=0)
    iterate = iterate + jnp.broadcast_to(added[None], FIELD)
    resid = resid_base(iterate)
    for copy in tails:
        copy.wait_recv()
    high_x = high_x + over_aggregates(tail_in[1, 0])[None]
    low_x = low_x + over_aggregates(tail_in[0, 1])[None]
    lower_lanes = iota((8, 128), 1) < 64

    def over_rows(side, upper):
        lines = []
        for part in range(2):
            line = jnp.broadcast_to(tail_in[side, part], (8, 128))
            moved = roll(line, 64, 1)
            line = jnp.where(lower_lanes, moved, line) if upper else jnp.where(lower_lanes, line, moved)
            lines.append(line)
        tiles = jnp.concatenate([lines[place // 4][None] for place in range(SIZE)], axis=0)
        return jnp.broadcast_to(tiles[None], FIELD)

    high_y = high_y + over_rows(3, False)
    low_y = low_y + over_rows(2, True)
    resid = resid_edges(resid, high_x, low_x, high_y, low_y)
    iterate = iterate + smooth(resid)

    copies = send_faces(2, iterate)
    pending += copies
    resid = resid_base(iterate)
    for copy in copies:
        copy.wait_recv()
    resid = resid_edges(resid, *halos(2))
    iterate = iterate + smooth(resid)

    copies = send_faces(3, iterate)
    pending += copies
    out_buf[0] = times_ones(flat(iterate), to_outside).reshape(SIZE, SIZE, DEPTH)
    stores = [
        pltpu.make_async_copy(out_buf.at[place], dst, store_sem.at[place])
        for place, dst in enumerate((pressure_any, resid_any))
    ]
    stores[0].start()
    resid = resid_base(iterate)
    for copy in copies:
        copy.wait_recv()
    resid = resid_edges(resid, *halos(3))
    out_buf[1] = times_ones(flat(resid), to_outside).reshape(SIZE, SIZE, DEPTH)
    stores[1].start()
    for copy in pending:
        copy.wait_send()
    for store in stores:
        store.wait()


def on_device(
    count_x,
    count_y,
    pressure_rhs,
    accumulation,
    trans_x,
    trans_y,
    trans_z,
    well_cells,
    well_flags,
    well_rates,
    well_index,
    block_map,
    block_inverses,
):
    anywhere = pl.BlockSpec(memory_space=pl.ANY)
    scalars = pl.BlockSpec(memory_space=pltpu.SMEM)
    dma = pltpu.SemaphoreType.DMA
    out = jax.ShapeDtypeStruct(pressure_rhs.shape, F32)
    return pl.pallas_call(
        functools.partial(kernel, count_x, count_y),
        out_shape=(out, out),
        in_specs=[anywhere] * 5 + [scalars] * 4 + [anywhere] * 2,
        out_specs=(anywhere, anywhere),
        scratch_shapes=[
            pltpu.VMEM((5, SIZE, SIZE, DEPTH), F32),
            pltpu.VMEM((2, 2, 64), jnp.int32),
            pltpu.VMEM((KINDS * 64, 64), F32),
            pltpu.VMEM((KINDS * 64, DEPTH), BF16),
            pltpu.VMEM(FIELD, F32),
            pltpu.VMEM((9,) + FIELD, F32),
            pltpu.VMEM((4, 2, 2, SIZE, 128), F32),
            pltpu.VMEM((4, 2, 2 * SIZE, 1, 128), F32),
            pltpu.VMEM((4, 2, 2, SIZE, 128), F32),
            pltpu.VMEM((4, 2, 2 * SIZE, 1, 128), F32),
            pltpu.VMEM((1, 2, SIZE, DEPTH), F32),
            pltpu.VMEM((1, 2, SIZE, DEPTH), F32),
            pltpu.VMEM((8, 128), F32),
            pltpu.VMEM((GROUP, 8, 128), F32),
            pltpu.VMEM((1, 256), F32),
            pltpu.VMEM((GROUP, 1, 256), F32),
            pltpu.VMEM((2, GROUP, 128), F32),
            pltpu.VMEM((2, 1, 128), F32),
            pltpu.VMEM((4, 2, 1, 128), F32),
            pltpu.VMEM((2, SIZE, SIZE, DEPTH), F32),
            dma((7,)),
            dma((2,)),
            dma((5, 4)),
            dma((5, 4)),
            dma((GROUP - 1,)),
            dma((GROUP - 1,)),
            dma((GROUP - 1,)),
            dma((GROUP - 1,)),
            dma((4,)),
            dma((4,)),
        ],
        compiler_params=pltpu.CompilerParams(
            collective_id=0, has_side_effects=True, vmem_limit_bytes=48 * 1024 * 1024
        ),
    )(
        pressure_rhs,
        accumulation,
        trans_x,
        trans_y,
        trans_z,
        well_cells,
        well_flags,
        well_rates,
        well_index,
        block_map,
        block_inverses.reshape(KINDS * 64, 64),
    )


def solution(mesh):
    cells = P("gx", "gy", None)
    wells = P(("gx", "gy"))
    return jax.shard_map(
        functools.partial(on_device, mesh.shape["gx"], mesh.shape["gy"]),
        mesh=mesh,
        in_specs=(cells,) * 5 + (wells,) * 4 + (cells, P()),
        out_specs=(cells, cells),
        check_vma=False,
    )
```

```python
import functools

import jax
import jax.numpy as jnp
from jax import lax
from jax.experimental import pallas as pl
from jax.experimental.pallas import tpu as pltpu
from jax.sharding import PartitionSpec as P

OMEGA = 0.8
GROUP = 16
SIZE = 8
DEPTH = 256
KINDS = 16
WELLS = 4
DOUBLINGS = 10
MESH = pl.DeviceIdType.MESH
HIGHEST = lax.Precision.HIGHEST
F32 = jnp.float32
BF16 = jnp.bfloat16
FIELD = (2, SIZE, SIZE, 128)


def iota(shape, dim):
    return lax.broadcasted_iota(jnp.int32, shape, dim)


def roll(values, shift, axis):
    return pltpu.roll(values, shift % values.shape[axis], axis)


def split_three(values):
    high = values.astype(BF16)
    rest = values - high.astype(F32)
    middle = rest.astype(BF16)
    low = (rest - middle.astype(F32)).astype(BF16)
    return high, middle, low


def split_two(values):
    high = values.astype(BF16)
    low = (values - high.astype(F32)).astype(BF16)
    return high, low


def times_ones(values, ones):
    return sum(jnp.dot(part, ones, preferred_element_type=F32) for part in split_three(values))


def flat(field):
    return jnp.concatenate(
        [field[0].reshape(SIZE * SIZE, 128), field[1].reshape(SIZE * SIZE, 128)], axis=1
    )


def unflat(rows):
    shape = (1, SIZE, SIZE, 128)
    return jnp.concatenate(
        [rows[:, :128].reshape(shape), rows[:, 128:].reshape(shape)], axis=0
    )


def lane_roll(field, shift):
    return roll(field.reshape(-1, 8, 128), shift, 2).reshape(field.shape)


def row_roll(field, shift):
    return roll(field.reshape(-1, 8, 128), shift, 1).reshape(field.shape)


def z_neighbours(field):
    low, high = field[0], field[1]
    lower_lanes = iota(low.shape, 2) < 64
    across = lane_roll(jnp.where(lower_lanes, high, low), 64)
    up = [across, jnp.where(lower_lanes, lane_roll(high, 64), lane_roll(low, 63))]
    down = [jnp.where(lower_lanes, lane_roll(high, 65), lane_roll(low, 64)), across]
    return (
        jnp.concatenate([part[None] for part in up], axis=0),
        jnp.concatenate([part[None] for part in down], axis=0),
    )


def turned(field):
    shape = (field.size // 1024, 8, 128)
    same = (iota(shape, 1) >= 4) == (iota(shape, 2) >= 64)
    tiles = field.reshape(shape)
    return jnp.where(same, tiles, roll(roll(tiles, 4, 1), 64, 2)).reshape(field.shape)


def agg_rows(tile):
    tile = tile + roll(tile, 64, 1)
    tile = tile + roll(tile, -1, 0)
    tile = tile + roll(tile, -2, 0)
    return jnp.where(iota((1, 128), 1) < 64, tile[0:1], tile[4:5])


def xor_sum(values, step, axis):
    place = iota(values.shape, axis)
    return values + jnp.where(
        (place & step) == 0, roll(values, -step, axis), roll(values, step, axis)
    )


def xor_upper(values, step, axis):
    place = iota(values.shape, axis)
    return jnp.where((place & step) == 0, roll(values, -step, axis), values)


def only_if(condition, action):
    if condition is None:
        action()
    else:
        pl.when(condition)(action)


class Remote:
    def __init__(self, src, dst, send_sem, recv_sem, device, send_if=None, recv_if=None):
        self.copy = pltpu.make_async_remote_copy(
            src_ref=src,
            dst_ref=dst,
            send_sem=send_sem,
            recv_sem=recv_sem,
            device_id=device,
            device_id_type=MESH,
        )
        self.send_if = send_if
        self.recv_if = recv_if

    def start(self):
        only_if(self.send_if, self.copy.start)

    def wait_recv(self):
        only_if(self.recv_if, self.copy.wait_recv)

    def wait_send(self):
        only_if(self.send_if, self.copy.wait_send)


def kernel(
    count_x,
    count_y,
    rhs_any,
    acc_any,
    tx_any,
    ty_any,
    tz_any,
    cells,
    flags,
    rates,
    well_index,
    map_any,
    inv_any,
    pressure_any,
    resid_any,
    fields_in,
    map_in,
    inv_in,
    blocks,
    source,
    coef,
    face_x,
    face_y,
    halo_x,
    halo_y,
    ends_in,
    ends_send,
    gop_send,
    gop,
    gres_send,
    gres,
    beside_send,
    beside,
    edge_send,
    edge_in,
    tail,
    tail_send,
    tail_in,
    out_buf,
    load_sem,
    store_sem,
    face_send_sem,
    face_recv_sem,
    gop_send_sem,
    gop_recv_sem,
    gres_send_sem,
    gres_recv_sem,
    beside_send_sem,
    beside_recv_sem,
    edge_send_sem,
    edge_recv_sem,
    tail_send_sem,
    tail_recv_sem,
):
    index_x = lax.axis_index("gx")
    index_y = lax.axis_index("gy")
    rank = lax.rem(index_x, GROUP)
    base = index_x - rank
    next_x = (lax.rem(index_x + 1, count_x), index_y)
    prev_x = (lax.rem(index_x + count_x - 1, count_x), index_y)
    next_y = (index_x, lax.rem(index_y + 1, count_y))
    prev_y = (index_x, lax.rem(index_y + count_y - 1, count_y))
    sides = (next_x, prev_x, next_y, prev_y)
    mates = [(base + lax.rem(rank + step, GROUP), index_y) for step in range(1, GROUP)]
    upper_group = [(base + lax.rem(rank + step, GROUP), next_y[1]) for step in range(GROUP)]
    lower_group = [(base + lax.rem(rank + step, GROUP), prev_y[1]) for step in range(GROUP)]
    has_next = index_x < count_x - 1
    has_prev = index_x > 0
    group_after = base + GROUP < count_x
    group_before = base > 0
    last_member = group_after & (rank == GROUP - 1)
    first_member = group_before & (rank == 0)
    send_if = (has_next, has_prev, None, None)
    recv_if = (has_prev, has_next, None, None)

    loads = [
        pltpu.make_async_copy(src, dst, load_sem.at[place])
        for place, (src, dst) in enumerate(
            (
                (inv_any, inv_in),
                (rhs_any, fields_in.at[0]),
                (tx_any, fields_in.at[1]),
                (ty_any, fields_in.at[2]),
                (tz_any, fields_in.at[3]),
                (acc_any, fields_in.at[4]),
                (map_any, map_in),
            )
        )
    ]
    for load in loads:
        load.start()
    halo_x[...] = jnp.zeros_like(halo_x)
    ends_in[...] = jnp.zeros_like(ends_in)
    edge_in[...] = jnp.zeros_like(edge_in)
    tail_in[...] = jnp.zeros_like(tail_in)

    barrier = pltpu.get_barrier_semaphore()

    def announce(device):
        pl.semaphore_signal(barrier, inc=1, device_id=device, device_id_type=MESH)

    for device in mates + upper_group + lower_group:
        announce(device)
    only_if(group_after, lambda: announce((base + GROUP, index_y)))
    only_if(group_before, lambda: announce((base - 1, index_y)))
    announced = (
        len(mates)
        + 2 * GROUP
        + GROUP * (last_member.astype(jnp.int32) + first_member.astype(jnp.int32))
    )

    row = iota((DEPTH, DEPTH), 0)
    col = iota((DEPTH, DEPTH), 1)
    to_inside = (row == 4 * (col & 63) + (col >> 6)).astype(F32).astype(BF16)
    to_outside = (col == 4 * (row & 63) + (row >> 6)).astype(F32).astype(BF16)
    lane = iota(FIELD, 3)
    second = iota(FIELD, 2)
    first = iota(FIELD, 1)
    half = iota(FIELD, 0)
    cell_id = ((half * SIZE + first) * SIZE + second) * 128 + lane

    def swapped_offsets(place):
        return (place & ~15) | ((place & 3) << 2) | ((place >> 2) & 3)

    take_rows = (col == swapped_offsets(row)).astype(F32).astype(BF16)
    row_k = iota((64, DEPTH), 0)
    col_k = iota((64, DEPTH), 1)
    take_cols = row_k == swapped_offsets(col_k & 63)
    take_high = (take_cols & (col_k < 128)).astype(F32).astype(BF16)
    take_low = (take_cols & (col_k >= 128)).astype(F32).astype(BF16)
    loads[0].wait()
    for part in range(KINDS // 4):
        here = slice(part * DEPTH, (part + 1) * DEPTH)
        high, low = split_two(OMEGA * inv_in[here, :])
        both = jnp.dot(high, take_high, preferred_element_type=F32) + jnp.dot(
            low, take_low, preferred_element_type=F32
        )
        blocks[here, :] = jnp.dot(
            take_rows, both.astype(BF16), preferred_element_type=F32
        ).astype(BF16)

    plane_cells = SIZE * count_y * DEPTH
    well_ids = []
    for well in range(WELLS):
        cell = cells[well]
        pos_x = cell // plane_cells - index_x * SIZE
        left = lax.rem(cell, plane_cells)
        pos_y = left // DEPTH - index_y * SIZE
        pos_z = lax.rem(left, DEPTH)
        place = lax.rem(pos_z, 4) * 64 + pos_z // 4
        well_ids.append(
            ((place // 128 * SIZE + pos_x) * SIZE + pos_y) * 128 + lax.rem(place, 128)
        )
    signed = [
        jnp.where(flags[well] == 1, rates[well], -rates[well]) for well in range(WELLS)
    ]

    loads[1].wait()
    well_source = jnp.zeros(FIELD, F32)
    for well in range(WELLS):
        well_source = well_source + jnp.where(cell_id == well_ids[well], signed[well], 0.0)
    source[...] = (
        unflat(times_ones(fields_in[0].reshape(SIZE * SIZE, DEPTH), to_inside)) + well_source
    )

    loads[6].wait()
    kinds = []
    for part in range(2):
        kind = map_in[part]
        kinds.append(jnp.concatenate([kind[0:1], kind[1:2]], axis=1))
    kind_ids = jnp.broadcast_to(jnp.concatenate(kinds, axis=1), (8, 256))

    def smooth(resid):
        tiles = turned(resid)
        columns = jnp.concatenate(
            [
                jnp.concatenate(
                    [
                        tiles[half_id, 4 * part + offset]
                        for offset in range(4)
                        for half_id in range(2)
                    ],
                    axis=0,
                )
                for part in range(2)
            ],
            axis=1,
        )
        high, low = split_two(columns)
        product = jnp.dot(
            blocks[...],
            jnp.concatenate([high, low, high, low], axis=0),
            preferred_element_type=F32,
        )
        chosen = product[0:64]
        for kind in range(1, KINDS):
            mask = jnp.broadcast_to((kind_ids == kind)[None], (8, 8, 256)).reshape(64, 256)
            chosen = jnp.where(mask, product[64 * kind : 64 * kind + 64], chosen)
        back = [
            [
                chosen[8 * (2 * offset + half_id) : 8 * (2 * offset + half_id) + 8,
                       128 * part : 128 * part + 128][None]
                for part in range(2)
                for offset in range(4)
            ]
            for half_id in range(2)
        ]
        field = jnp.concatenate(
            [jnp.concatenate(tiles, axis=0)[None] for tiles in back], axis=0
        )
        return turned(field)

    def send_faces(step, field):
        face_x[step, 0] = field[:, SIZE - 1]
        face_x[step, 1] = field[:, 0]
        tiles = field.reshape(2 * SIZE, 8, 128)
        face_y[step, 0] = tiles[:, 7:8, :]
        face_y[step, 1] = tiles[:, 0:1, :]
        copies = []
        for side, (out, into) in enumerate(
            ((face_x, halo_x), (face_x, halo_x), (face_y, halo_y), (face_y, halo_y))
        ):
            copies.append(
                Remote(
                    out.at[step, side % 2],
                    into.at[step, side % 2],
                    face_send_sem.at[step, side],
                    face_recv_sem.at[step, side],
                    sides[side],
                    send_if[side],
                    recv_if[side],
                )
            )
        for copy in copies:
            copy.start()
        return copies

    iterate = smooth(source[...])

    pl.semaphore_wait(barrier, announced)
    pending = []
    copies = send_faces(0, iterate)
    pending += copies

    loads[2].wait()
    loads[3].wait()
    ends_send[0, 0] = fields_in[1, SIZE - 1]
    for place in range(SIZE):
        ends_send[0, 1, place : place + 1] = fields_in[2, place, SIZE - 1 : SIZE, :]
    ends = []
    for side in range(2):
        ends.append(
            Remote(
                ends_send.at[0, side],
                ends_in.at[0, side],
                face_send_sem.at[4, side],
                face_recv_sem.at[4, side],
                sides[2 * side],
                send_if[2 * side],
                recv_if[2 * side],
            )
        )
        ends[-1].start()
    pending += ends

    loads[4].wait()
    loads[5].wait()
    inside = times_ones(
        fields_in[1:5].reshape(4 * SIZE * SIZE, DEPTH), to_inside
    )
    tx, ty, tz, acc = [unflat(inside[64 * place : 64 * place + 64]) for place in range(4)]
    well_diag = jnp.zeros(FIELD, F32)
    for well in range(WELLS):
        well_diag = well_diag + jnp.where(cell_id == well_ids[well], well_index[well], 0.0)
    diag = acc + well_diag
    tx = jnp.where((first == SIZE - 1) & (index_x == count_x - 1), 0.0, tx)
    ty = jnp.where((second == SIZE - 1) & (index_y == count_y - 1), 0.0, ty)
    tz = jnp.where((half == 1) & (lane == 127), 0.0, tz)

    for part in range(2):
        mine = slice(4 * part, 4 * part + 4)
        gop_send[part : part + 1] = agg_rows(diag[:, mine].sum(axis=(0, 1)))
        gop_send[2 + part : 3 + part] = agg_rows(tx[:, 4 * part + 3].sum(axis=0))
        tile = ty[:, mine].sum(axis=(0, 1))
        tile = tile + roll(tile, 64, 1)
        gop_send[4 + part : 5 + part] = jnp.where(
            iota((1, 128), 1) < 64, tile[3:4], tile[7:8]
        )
        tile = tz[1, mine].sum(axis=0)
        gop_send[6 + part : 7 + part] = agg_rows(
            jnp.where(iota((8, 128), 1) >= 64, tile, 0.0)
        )

    def to_all(devices, mine, target, send_sem, recv_sem, send_if=None, recv_if=None):
        return [
            Remote(mine, target, send_sem.at[step], recv_sem.at[step], device, send_if, recv_if)
            for step, device in enumerate(devices)
        ]

    gop_copies = to_all(mates, gop_send, gop.at[rank], gop_send_sem, gop_recv_sem)
    for copy in gop_copies:
        copy.start()
    gop[rank] = gop_send[...]
    pending += gop_copies

    tz_down = jnp.where((half == 0) & (lane == 0), 0.0, z_neighbours(tz)[1])
    for copy in ends:
        copy.wait_recv()
    end_rows = times_ones(ends_in[0].reshape(2 * SIZE, DEPTH), to_inside)
    end_x = jnp.where(index_x == 0, 0.0, end_rows[0:SIZE])
    end_y = jnp.where(index_y == 0, 0.0, end_rows[SIZE:])
    end_x = jnp.concatenate([end_x[None, None, :, :128], end_x[None, None, :, 128:]], axis=0)
    tx_down = jnp.concatenate([end_x, tx[:, : SIZE - 1]], axis=1)
    end_y = jnp.concatenate(
        [
            jnp.broadcast_to(
                end_y[place : place + 1, 128 * part : 128 * part + 128], (8, 128)
            )[None]
            for part in range(2)
            for place in range(SIZE)
        ],
        axis=0,
    ).reshape(FIELD)
    ty_in = jnp.where(second == SIZE - 1, 0.0, ty)
    ty_down_in = row_roll(ty_in, 1)
    ty_edge = ty - ty_in
    ty_down_edge = jnp.where(second == 0, end_y, 0.0)
    coef[0] = (
        diag + tx + tx_down + ty + ty_down_in + ty_down_edge + tz + tz_down
    )
    coef[1] = tx
    coef[2] = tx_down
    coef[3] = ty_in
    coef[4] = ty_down_in
    coef[5] = tz
    coef[6] = tz_down
    coef[7] = ty_edge
    coef[8] = ty_down_edge

    def resid_base(field):
        nothing = jnp.zeros((2, 1, SIZE, 128), F32)
        up_z, down_z = z_neighbours(field)
        return (
            source[...]
            - coef[0] * field
            + coef[1] * jnp.concatenate([field[:, 1:], nothing], axis=1)
            + coef[2] * jnp.concatenate([nothing, field[:, : SIZE - 1]], axis=1)
            + coef[3] * row_roll(field, -1)
            + coef[4] * row_roll(field, 1)
            + coef[5] * up_z
            + coef[6] * down_z
        )

    def resid_edges(resid, high_x, low_x, high_y, low_y):
        first_row = resid[:, 0:1] + (coef[2, :, 0] * low_x)[:, None]
        last_row = resid[:, SIZE - 1 :] + (coef[1, :, SIZE - 1] * high_x)[:, None]
        resid = jnp.concatenate([first_row, resid[:, 1 : SIZE - 1], last_row], axis=1)
        return resid + coef[7] * high_y + coef[8] * low_y

    def halos(step):
        spread = [
            jnp.broadcast_to(halo_y[step, side], (2 * SIZE, 8, 128)).reshape(FIELD)
            for side in (1, 0)
        ]
        return halo_x[step, 1], halo_x[step, 0], spread[0], spread[1]

    resid = resid_base(iterate)
    for copy in copies:
        copy.wait_recv()
    resid = resid_edges(resid, *halos(0))
    iterate = iterate + smooth(resid)

    copies = send_faces(1, iterate)
    pending += copies
    resid = resid_base(iterate)

    for part in range(2):
        mine = slice(4 * part, 4 * part + 4)
        gres_send[:, 128 * part : 128 * part + 128] = agg_rows(resid[:, mine].sum(axis=(0, 1)))
    flux_up = agg_rows((coef[1, :, SIZE - 1] * iterate[:, SIZE - 1]).sum(axis=0))
    flux_down = agg_rows((coef[2, :, 0] * iterate[:, 0]).sum(axis=0))
    gres_send[:, 256:384] = flux_up
    gres_send[:, 384:512] = flux_down
    edge_send[0] = flux_up
    edge_send[1] = flux_down
    for side in range(2):
        flux = coef[7 + side] * iterate
        lines = []
        for part in range(2):
            tile = flux[:, 4 * part : 4 * part + 4].sum(axis=(0, 1))
            tile = tile + roll(tile, 64, 1)
            lines.append(tile[7:8] if side == 0 else tile[0:1])
        beside_send[side] = jnp.where(iota((1, 128), 1) < 64, lines[0], lines[1])
    gres_copies = (
        to_all(mates, gres_send, gres.at[rank], gres_send_sem, gres_recv_sem)
        + to_all(
            upper_group,
            beside_send.at[0],
            beside.at[0, rank],
            beside_send_sem.at[0],
            beside_recv_sem.at[0],
        )
        + to_all(
            lower_group,
            beside_send.at[1],
            beside.at[1, rank],
            beside_send_sem.at[1],
            beside_recv_sem.at[1],
        )
    )
    for copy in gres_copies:
        copy.start()

    def edges(side, target):
        return [
            Remote(
                edge_send.at[side],
                edge_in.at[side],
                edge_send_sem.at[side, step],
                edge_recv_sem.at[side],
                (target + step, index_y),
            )
            for step in range(GROUP)
        ]

    edge_copies = (
        (last_member, edges(0, base + GROUP)),
        (first_member, edges(1, base - GROUP)),
    )
    for condition, each in edge_copies:
        only_if(condition, lambda each=each: [copy.start() for copy in each] and None)
    gres[rank] = gres_send[...]
    pending += gres_copies

    for copy in gop_copies:
        copy.wait_recv()
    shape = (GROUP, 128)
    member = iota(shape, 0)
    lane_c = iota(shape, 1)
    deep = lane_c & 63
    base_a, base_b, tx_a, tx_b, ty_a, ty_b, tz_a, tz_b = [
        gop[:, place, :] for place in range(8)
    ]

    def y_terms(values):
        return jnp.where(lane_c < 64, values, roll(values, 64, 1))

    def z_terms(values, step):
        up = jnp.where(deep < 64 - step, values, 0.0)
        down = jnp.where(deep >= step, roll(values, step, 1), 0.0)
        return up, down

    across_up = jnp.where((member & 1) == 0, tx_b, 0.0)
    across_down = jnp.where((member & 1) == 1, roll(tx_b, 1, 0), 0.0)
    y_a, y_b = y_terms(ty_a), y_terms(ty_b)
    (zu_a, zd_a), (zu_b, zd_b) = z_terms(tz_a, 1), z_terms(tz_b, 1)
    diag_a = base_a + tx_a + across_down + y_a + zu_a + zd_a
    diag_b = base_b + tx_a + across_up + y_b + zu_b + zd_b
    weight_a, weight_b = OMEGA / diag_a, OMEGA / diag_b

    def apply_one(field_a, field_b):
        out_a = (
            diag_a * field_a
            - tx_a * field_b
            - across_down * roll(field_b, 1, 0)
            - y_a * roll(field_a, 64, 1)
            - zu_a * roll(field_a, -1, 1)
            - zd_a * roll(field_a, 1, 1)
        )
        out_b = (
            diag_b * field_b
            - tx_a * field_a
            - across_up * roll(field_a, -1, 0)
            - y_b * roll(field_b, 64, 1)
            - zu_b * roll(field_b, -1, 1)
            - zd_b * roll(field_b, 1, 1)
        )
        return out_a, out_b

    levels = []
    base_k = xor_sum(base_a + base_b, 1, 1)
    tx_k = xor_sum(tx_b, 1, 1)
    ty_k = xor_sum(ty_a + ty_b, 1, 1)
    tz_k = xor_upper(tz_a + tz_b, 1, 1)
    for level in range(2, 5):
        step_x, step_z = 1 << (level - 2), 1 << (level - 1)
        cell_x = member >> (level - 2)
        up_x = jnp.where((cell_x & 3) != 3, tx_k, 0.0)
        down_x = jnp.where((cell_x & 3) != 0, roll(tx_k, step_x, 0), 0.0)
        both_y = y_terms(ty_k)
        up_z, down_z = z_terms(tz_k, step_z)
        diag_k = base_k + up_x + down_x + both_y + up_z + down_z
        levels.append((diag_k, up_x, down_x, both_y, up_z, down_z, step_x, step_z))
        if level < 4:
            base_k = xor_sum(xor_sum(base_k, step_x, 0), step_z, 1)
            ty_k = xor_sum(xor_sum(ty_k, step_x, 0), step_z, 1)
            tx_k = xor_sum(xor_upper(tx_k, step_x, 0), step_z, 1)
            tz_k = xor_upper(xor_sum(tz_k, step_x, 0), step_z, 1)

    def apply_level(field, terms):
        diag_k, up_x, down_x, both_y, up_z, down_z, step_x, step_z = terms
        return (
            diag_k * field
            - up_x * roll(field, -step_x, 0)
            - down_x * roll(field, step_x, 0)
            - both_y * roll(field, 64, 1)
            - up_z * roll(field, -step_z, 1)
            - down_z * roll(field, step_z, 1)
        )

    lane_row = iota((128, 128), 0)
    lane_col = iota((128, 128), 1)
    real = lane_col < 64
    same_place = ((lane_row >> 6) == ((lane_col >> 3) & 1)) & (
        ((lane_row & 63) >> 3) == (lane_col & 7)
    )
    pick_one = (real & same_place & ((lane_row & 7) == 0)).astype(F32).astype(BF16)
    pick_two = (real & same_place & ((lane_row & 3) == 0)).astype(F32).astype(BF16)
    own_x = (member >> 2) == (lane_c >> 4)
    diag_k, up_x, down_x, both_y, up_z, down_z, _, _ = levels[2]
    picked = times_ones(
        jnp.concatenate(
            [1.0 / diag_k, up_x, down_x, both_y, up_z, down_z], axis=0
        ),
        pick_one,
    )
    one_member = own_x & ((member & 3) == 0)
    inverse_diag, up_x, down_x, both_y, up_z, down_z = [
        jnp.sum(
            jnp.where(one_member, picked[GROUP * place : GROUP * place + GROUP], 0.0),
            axis=0,
            keepdims=True,
        )
        for place in range(6)
    ]
    gap = lane_row - lane_col
    upper_y = (lane_col >> 3) & 1
    coupling = jnp.where(gap == 16, up_x, 0.0)
    coupling = jnp.where(gap == -16, down_x, coupling)
    coupling = jnp.where(gap == 8 - 16 * upper_y, both_y, coupling)
    coupling = jnp.where(gap == 1, up_z, coupling)
    coupling = jnp.where(gap == -1, down_z, coupling)
    power = coupling * inverse_diag
    total = power + jnp.where(gap == 0, 1.0, 0.0)
    for _ in range(DOUBLINGS):
        power = jnp.dot(power, power, precision=HIGHEST, preferred_element_type=F32)
        total = total + jnp.dot(
            total, power, precision=HIGHEST, preferred_element_type=F32
        )
    spread = jnp.concatenate(
        [
            ((lane_row >> 4) == part)
            & ((lane_row >> 3 & 1) == (lane_col >> 6))
            & ((lane_row & 7) == ((lane_col & 63) >> 3))
            & (lane_row < 64)
            for part in range(4)
        ],
        axis=1,
    )
    solver = times_ones(total, spread.astype(F32).astype(BF16))

    for copy in copies:
        copy.wait_recv()
    high_x, low_x, high_y, low_y = halos(1)

    for copy in gres_copies:
        copy.wait_recv()
    only_if(group_before, edge_copies[0][1][0].wait_recv)
    only_if(group_after, edge_copies[1][1][0].wait_recv)
    every = gres[:, 0, :]
    first_a, first_b, from_low, from_high = [
        every[:, 128 * part : 128 * part + 128] for part in range(4)
    ]
    from_low = jnp.where(member == 0, edge_in[0], roll(from_low, 1, 0))
    from_high = jnp.where(member == GROUP - 1, edge_in[1], roll(from_high, -1, 0))
    below, above = beside[0, :, 0, :], beside[1, :, 0, :]
    res_a = first_a + from_low + jnp.where(lane_c < 64, below, roll(above, 64, 1))
    res_b = first_b + from_high + jnp.where(lane_c < 64, roll(below, 64, 1), above)

    def descend_one(res_a, res_b):
        cor_a, cor_b = weight_a * res_a, weight_b * res_b
        out_a, out_b = apply_one(cor_a, cor_b)
        cor_a = cor_a + weight_a * (res_a - out_a)
        cor_b = cor_b + weight_b * (res_b - out_b)
        out_a, out_b = apply_one(cor_a, cor_b)
        return cor_a, cor_b, (res_a - out_a) + (res_b - out_b)

    cor_a, cor_b, left = descend_one(res_a, res_b)
    res_k = xor_sum(left, 1, 1)
    cor_k = jnp.zeros(shape, F32)
    for level in (2, 3):
        terms = levels[level - 2]
        weight = OMEGA / terms[0]
        cor = weight * res_k
        cor = cor + weight * (res_k - apply_level(cor, terms))
        left = res_k - apply_level(cor, terms)
        cor_k = cor_k + cor
        if level == 2:
            res_k = xor_sum(xor_sum(left, 1, 0), 2, 1)
    last = times_ones(left, pick_two)
    last = jnp.sum(
        jnp.where(own_x & ((member & 1) == 0), last, 0.0), axis=0, keepdims=True
    )
    last = jnp.broadcast_to(last * inverse_diag, (8, 128))
    solved = jnp.dot(last, solver, precision=HIGHEST, preferred_element_type=F32)
    solved = [jnp.broadcast_to(solved[0:1, 128 * part : 128 * part + 128], (8, 128)) for part in range(4)]
    upper_rows = (iota((8, 128), 0) & 4) != 0
    cor_k = cor_k + jnp.concatenate(
        [
            jnp.where(upper_rows, solved[1], solved[0]),
            jnp.where(upper_rows, solved[3], solved[2]),
        ],
        axis=0,
    )
    tail[0] = cor_a + cor_k
    tail[1] = cor_b + cor_k
    tail_send[0] = tail[0, pl.ds(rank, 1), :]
    tail_send[1] = tail[1, pl.ds(rank, 1), :]
    tails = []
    for side in range(4):
        tails.append(
            Remote(
                tail_send,
                tail_in.at[side],
                tail_send_sem.at[side],
                tail_recv_sem.at[side],
                sides[side],
                send_if[side],
                recv_if[side],
            )
        )
        tails[-1].start()
    pending += tails

    def over_aggregates(line):
        return turned(jnp.broadcast_to(line, (8, 128)))

    added = [over_aggregates(tail_send[part]) for part in range(2)]
    added = jnp.concatenate([added[place // 4][None] for place in range(SIZE)], axis=0)
    iterate = iterate + jnp.broadcast_to(added[None], FIELD)
    resid = resid_base(iterate)
    for copy in tails:
        copy.wait_recv()
    high_x = high_x + over_aggregates(tail_in[1, 0])[None]
    low_x = low_x + over_aggregates(tail_in[0, 1])[None]
    lower_lanes = iota((8, 128), 1) < 64

    def over_rows(side, upper):
        lines = []
        for part in range(2):
            line = jnp.broadcast_to(tail_in[side, part], (8, 128))
            moved = roll(line, 64, 1)
            line = jnp.where(lower_lanes, moved, line) if upper else jnp.where(lower_lanes, line, moved)
            lines.append(line)
        tiles = jnp.concatenate([lines[place // 4][None] for place in range(SIZE)], axis=0)
        return jnp.broadcast_to(tiles[None], FIELD)

    high_y = high_y + over_rows(3, False)
    low_y = low_y + over_rows(2, True)
    resid = resid_edges(resid, high_x, low_x, high_y, low_y)
    iterate = iterate + smooth(resid)

    copies = send_faces(2, iterate)
    pending += copies
    resid = resid_base(iterate)
    for copy in copies:
        copy.wait_recv()
    resid = resid_edges(resid, *halos(2))
    iterate = iterate + smooth(resid)

    copies = send_faces(3, iterate)
    pending += copies
    out_buf[0] = times_ones(flat(iterate), to_outside).reshape(SIZE, SIZE, DEPTH)
    stores = [
        pltpu.make_async_copy(out_buf.at[place], dst, store_sem.at[place])
        for place, dst in enumerate((pressure_any, resid_any))
    ]
    stores[0].start()
    resid = resid_base(iterate)
    for copy in copies:
        copy.wait_recv()
    resid = resid_edges(resid, *halos(3))
    out_buf[1] = times_ones(flat(resid), to_outside).reshape(SIZE, SIZE, DEPTH)
    stores[1].start()
    for copy in pending:
        copy.wait_send()
    for condition, each in edge_copies:
        only_if(condition, lambda each=each: [copy.wait_send() for copy in each] and None)
    for store in stores:
        store.wait()


def on_device(
    count_x,
    count_y,
    pressure_rhs,
    accumulation,
    trans_x,
    trans_y,
    trans_z,
    well_cells,
    well_flags,
    well_rates,
    well_index,
    block_map,
    block_inverses,
):
    anywhere = pl.BlockSpec(memory_space=pl.ANY)
    scalars = pl.BlockSpec(memory_space=pltpu.SMEM)
    dma = pltpu.SemaphoreType.DMA
    out = jax.ShapeDtypeStruct(pressure_rhs.shape, F32)
    return pl.pallas_call(
        functools.partial(kernel, count_x, count_y),
        out_shape=(out, out),
        in_specs=[anywhere] * 5 + [scalars] * 4 + [anywhere] * 2,
        out_specs=(anywhere, anywhere),
        scratch_shapes=[
            pltpu.VMEM((5, SIZE, SIZE, DEPTH), F32),
            pltpu.VMEM((2, 2, 64), jnp.int32),
            pltpu.VMEM((KINDS * 64, 64), F32),
            pltpu.VMEM((KINDS * 64, DEPTH), BF16),
            pltpu.VMEM(FIELD, F32),
            pltpu.VMEM((9,) + FIELD, F32),
            pltpu.VMEM((4, 2, 2, SIZE, 128), F32),
            pltpu.VMEM((4, 2, 2 * SIZE, 1, 128), F32),
            pltpu.VMEM((4, 2, 2, SIZE, 128), F32),
            pltpu.VMEM((4, 2, 2 * SIZE, 1, 128), F32),
            pltpu.VMEM((1, 2, SIZE, DEPTH), F32),
            pltpu.VMEM((1, 2, SIZE, DEPTH), F32),
            pltpu.VMEM((8, 128), F32),
            pltpu.VMEM((GROUP, 8, 128), F32),
            pltpu.VMEM((1, 512), F32),
            pltpu.VMEM((GROUP, 1, 512), F32),
            pltpu.VMEM((2, 1, 128), F32),
            pltpu.VMEM((2, GROUP, 1, 128), F32),
            pltpu.VMEM((2, 1, 128), F32),
            pltpu.VMEM((2, 1, 128), F32),
            pltpu.VMEM((2, GROUP, 128), F32),
            pltpu.VMEM((2, 1, 128), F32),
            pltpu.VMEM((4, 2, 1, 128), F32),
            pltpu.VMEM((2, SIZE, SIZE, DEPTH), F32),
            dma((7,)),
            dma((2,)),
            dma((5, 4)),
            dma((5, 4)),
            dma((GROUP - 1,)),
            dma((GROUP - 1,)),
            dma((GROUP - 1,)),
            dma((GROUP - 1,)),
            dma((2, GROUP)),
            dma((2, GROUP)),
            dma((2, GROUP)),
            dma((2,)),
            dma((4,)),
            dma((4,)),
        ],
        compiler_params=pltpu.CompilerParams(
            collective_id=0, has_side_effects=True, vmem_limit_bytes=60 * 1024 * 1024
        ),
    )(
        pressure_rhs,
        accumulation,
        trans_x,
        trans_y,
        trans_z,
        well_cells,
        well_flags,
        well_rates,
        well_index,
        block_map,
        block_inverses.reshape(KINDS * 64, 64),
    )


def solution(mesh):
    cells = P("gx", "gy", None)
    wells = P(("gx", "gy"))
    return jax.shard_map(
        functools.partial(on_device, mesh.shape["gx"], mesh.shape["gy"]),
        mesh=mesh,
        in_specs=(cells,) * 5 + (wells,) * 4 + (cells, P()),
        out_specs=(cells, cells),
        check_vma=False,
    )
```

```python
import functools

import jax
import jax.numpy as jnp
from jax import lax
from jax.experimental import pallas as pl
from jax.experimental.pallas import tpu as pltpu
from jax.sharding import PartitionSpec as P

OMEGA = 0.8
GROUP = 16
SIZE = 8
DEPTH = 256
KINDS = 16
WELLS = 4
DOUBLINGS = 10
MESH = pl.DeviceIdType.MESH
HIGHEST = lax.Precision.HIGHEST
F32 = jnp.float32
BF16 = jnp.bfloat16
FIELD = (2, SIZE, SIZE, 128)


def iota(shape, dim):
    return lax.broadcasted_iota(jnp.int32, shape, dim)


def roll(values, shift, axis):
    return pltpu.roll(values, shift % values.shape[axis], axis)


def split_three(values):
    high = values.astype(BF16)
    rest = values - high.astype(F32)
    middle = rest.astype(BF16)
    low = (rest - middle.astype(F32)).astype(BF16)
    return high, middle, low


def split_two(values):
    high = values.astype(BF16)
    low = (values - high.astype(F32)).astype(BF16)
    return high, low


def times_ones(values, ones):
    return sum(jnp.dot(part, ones, preferred_element_type=F32) for part in split_three(values))


def flat(field):
    return jnp.concatenate(
        [field[0].reshape(SIZE * SIZE, 128), field[1].reshape(SIZE * SIZE, 128)], axis=1
    )


def unflat(rows):
    shape = (1, SIZE, SIZE, 128)
    return jnp.concatenate(
        [rows[:, :128].reshape(shape), rows[:, 128:].reshape(shape)], axis=0
    )


def lane_roll(field, shift):
    return roll(field.reshape(-1, 8, 128), shift, 2).reshape(field.shape)


def row_roll(field, shift):
    return roll(field.reshape(-1, 8, 128), shift, 1).reshape(field.shape)


def z_neighbours(field):
    low, high = field[0], field[1]
    lower_lanes = iota(low.shape, 2) < 64
    across = lane_roll(jnp.where(lower_lanes, high, low), 64)
    up = [across, jnp.where(lower_lanes, lane_roll(high, 64), lane_roll(low, 63))]
    down = [jnp.where(lower_lanes, lane_roll(high, 65), lane_roll(low, 64)), across]
    return (
        jnp.concatenate([part[None] for part in up], axis=0),
        jnp.concatenate([part[None] for part in down], axis=0),
    )


def turned(field):
    shape = (field.size // 1024, 8, 128)
    same = (iota(shape, 1) >= 4) == (iota(shape, 2) >= 64)
    tiles = field.reshape(shape)
    return jnp.where(same, tiles, roll(roll(tiles, 4, 1), 64, 2)).reshape(field.shape)


def agg_rows(tile):
    tile = tile + roll(tile, 64, 1)
    tile = tile + roll(tile, -1, 0)
    tile = tile + roll(tile, -2, 0)
    return jnp.where(iota((1, 128), 1) < 64, tile[0:1], tile[4:5])


def xor_sum(values, step, axis):
    place = iota(values.shape, axis)
    return values + jnp.where(
        (place & step) == 0, roll(values, -step, axis), roll(values, step, axis)
    )


def xor_upper(values, step, axis):
    place = iota(values.shape, axis)
    return jnp.where((place & step) == 0, roll(values, -step, axis), values)


def only_if(condition, action):
    if condition is None:
        action()
    else:
        pl.when(condition)(action)


def send(src, dst, send_sem, recv_sem, device):
    pltpu.make_async_remote_copy(
        src_ref=src,
        dst_ref=dst,
        send_sem=send_sem,
        recv_sem=recv_sem,
        device_id=device,
        device_id_type=MESH,
    ).start()


def wait_bytes(like, sem):
    pltpu.make_async_copy(like, like, sem).wait()


def kernel(
    count_x,
    count_y,
    rhs_any,
    acc_any,
    tx_any,
    ty_any,
    tz_any,
    cells_any,
    flags_any,
    rates_any,
    index_any,
    map_any,
    inv_any,
    both_any,
    fields_in,
    map_in,
    cells,
    flags,
    rates,
    well_index,
    inv_in,
    blocks,
    source,
    coef,
    face_x,
    face_y,
    halo_x,
    halo_y,
    ends_in,
    ends_send,
    gop_send,
    gop,
    gres_send,
    gres,
    beside_send,
    beside,
    edge_send,
    edge_in,
    tail,
    tail_send,
    tail_in,
    out_buf,
    load_sem,
    store_sem,
    face_send_sem,
    face_recv_sem,
    ends_sem,
    gop_sem,
    gres_sem,
    beside_sem,
    edge_sem,
    tail_sem,
):
    index_x = lax.axis_index("gx")
    index_y = lax.axis_index("gy")
    rank = lax.rem(index_x, GROUP)
    base = index_x - rank
    next_x = (lax.rem(index_x + 1, count_x), index_y)
    prev_x = (lax.rem(index_x + count_x - 1, count_x), index_y)
    next_y = (index_x, lax.rem(index_y + 1, count_y))
    prev_y = (index_x, lax.rem(index_y + count_y - 1, count_y))
    sides = (next_x, prev_x, next_y, prev_y)
    mates = [(base + lax.rem(rank + step, GROUP), index_y) for step in range(1, GROUP)]
    upper_group = [(base + lax.rem(rank + step, GROUP), next_y[1]) for step in range(GROUP)]
    lower_group = [(base + lax.rem(rank + step, GROUP), prev_y[1]) for step in range(GROUP)]
    has_next = index_x < count_x - 1
    has_prev = index_x > 0
    group_after = base + GROUP < count_x
    group_before = base > 0
    last_member = group_after & (rank == GROUP - 1)
    first_member = group_before & (rank == 0)
    send_if = (has_next, has_prev, None, None)

    loads = [
        pltpu.make_async_copy(src, dst, load_sem.at[place])
        for place, (src, dst) in enumerate(
            (
                (inv_any, inv_in),
                (rhs_any, fields_in.at[0]),
                (tx_any, fields_in.at[1]),
                (ty_any, fields_in.at[2]),
                (tz_any, fields_in.at[3]),
                (acc_any, fields_in.at[4]),
                (map_any, map_in),
                (cells_any, cells),
                (flags_any, flags),
                (rates_any, rates),
                (index_any, well_index),
            )
        )
    ]
    for load in loads:
        load.start()
    halo_x[...] = jnp.zeros_like(halo_x)
    ends_in[...] = jnp.zeros_like(ends_in)
    edge_in[...] = jnp.zeros_like(edge_in)
    tail_in[...] = jnp.zeros_like(tail_in)

    barrier = pltpu.get_barrier_semaphore()

    def announce(device):
        pl.semaphore_signal(barrier, inc=1, device_id=device, device_id_type=MESH)

    for device in mates + upper_group + lower_group:
        announce(device)
    only_if(group_after, lambda: announce((base + GROUP, index_y)))
    only_if(group_before, lambda: announce((base - 1, index_y)))
    announced = (
        len(mates)
        + 2 * GROUP
        + GROUP * (last_member.astype(jnp.int32) + first_member.astype(jnp.int32))
    )

    row = iota((DEPTH, DEPTH), 0)
    col = iota((DEPTH, DEPTH), 1)
    to_inside = (row == 4 * (col & 63) + (col >> 6)).astype(F32).astype(BF16)
    lane = iota(FIELD, 3)
    second = iota(FIELD, 2)
    first = iota(FIELD, 1)
    half = iota(FIELD, 0)
    cell_id = ((half * SIZE + first) * SIZE + second) * 128 + lane

    def swapped_offsets(place):
        return (place & ~15) | ((place & 3) << 2) | ((place >> 2) & 3)

    row_k = iota((128, DEPTH), 0)
    col_k = iota((128, DEPTH), 1)
    take_cols = ((row_k & 63) == swapped_offsets(col_k & 63)) & ((row_k < 64) == (col_k < 128))
    take_cols = take_cols.astype(F32).astype(BF16)
    loads[0].wait()
    tiles = [
        (OMEGA * inv_in[pl.ds(third, KINDS * 16, stride=4), :]).reshape(KINDS * 2, 8, 64)
        for third in range(4)
    ]
    upper_half = iota((KINDS * 2, 8, 64), 1) >= 4
    rows = jnp.concatenate(
        [
            tile[:, None]
            for tile in (
                jnp.where(upper_half, roll(tiles[1], 4, 1), tiles[0]),
                jnp.where(upper_half, roll(tiles[3], 4, 1), tiles[2]),
                jnp.where(upper_half, tiles[1], roll(tiles[0], 4, 1)),
                jnp.where(upper_half, tiles[3], roll(tiles[2], 4, 1)),
            )
        ],
        axis=1,
    ).reshape(KINDS * 64, 64)
    high, low = split_two(rows)
    blocks[...] = jnp.dot(
        jnp.concatenate([high, low], axis=1), take_cols, preferred_element_type=F32
    ).astype(BF16)

    for place in range(7, 11):
        loads[place].wait()
    plane_cells = SIZE * count_y * DEPTH
    well_ids = []
    for well in range(WELLS):
        cell = cells[well]
        pos_x = cell // plane_cells - index_x * SIZE
        left = lax.rem(cell, plane_cells)
        pos_y = left // DEPTH - index_y * SIZE
        pos_z = lax.rem(left, DEPTH)
        place = lax.rem(pos_z, 4) * 64 + pos_z // 4
        well_ids.append(
            ((place // 128 * SIZE + pos_x) * SIZE + pos_y) * 128 + lax.rem(place, 128)
        )
    signed = [
        jnp.where(flags[well] == 1, rates[well], -rates[well]) for well in range(WELLS)
    ]

    loads[1].wait()
    well_source = jnp.zeros(FIELD, F32)
    for well in range(WELLS):
        well_source = well_source + jnp.where(cell_id == well_ids[well], signed[well], 0.0)
    source[...] = (
        unflat(times_ones(fields_in[0].reshape(SIZE * SIZE, DEPTH), to_inside)) + well_source
    )

    loads[6].wait()
    kinds = []
    for part in range(2):
        kind = map_in[part]
        kinds.append(jnp.concatenate([kind[0:1], kind[1:2]], axis=1))
    kind_ids = jnp.broadcast_to(jnp.concatenate(kinds, axis=1), (8, 256))

    def smooth(resid):
        tiles = turned(resid)
        columns = jnp.concatenate(
            [
                jnp.concatenate(
                    [
                        tiles[half_id, 4 * part + offset]
                        for offset in range(4)
                        for half_id in range(2)
                    ],
                    axis=0,
                )
                for part in range(2)
            ],
            axis=1,
        )
        high, low = split_two(columns)
        product = jnp.dot(
            blocks[...],
            jnp.concatenate([high, low, high, low], axis=0),
            preferred_element_type=F32,
        )
        chosen = product[0:64]
        for kind in range(1, KINDS):
            mask = jnp.broadcast_to((kind_ids == kind)[None], (8, 8, 256)).reshape(64, 256)
            chosen = jnp.where(mask, product[64 * kind : 64 * kind + 64], chosen)
        back = [
            [
                chosen[8 * (2 * offset + half_id) : 8 * (2 * offset + half_id) + 8,
                       128 * part : 128 * part + 128][None]
                for part in range(2)
                for offset in range(4)
            ]
            for half_id in range(2)
        ]
        field = jnp.concatenate(
            [jnp.concatenate(tiles, axis=0)[None] for tiles in back], axis=0
        )
        return turned(field)

    def send_faces(step, field):
        face_x[step, 0] = field[:, SIZE - 1]
        face_x[step, 1] = field[:, 0]
        tiles = field.reshape(2 * SIZE, 8, 128)
        face_y[step, 0] = tiles[:, 7:8, :]
        face_y[step, 1] = tiles[:, 0:1, :]
        for side, (out, into) in enumerate(
            ((face_x, halo_x), (face_x, halo_x), (face_y, halo_y), (face_y, halo_y))
        ):
            to_side(
                side,
                out.at[step, side % 2],
                into.at[step, side % 2],
                face_send_sem,
                face_recv_sem.at[step],
            )

    def to_side(side, src, dst, send_sems, recv_sems):
        kind = min(side, 2)
        only_if(
            send_if[side],
            lambda: send(src, dst, send_sems.at[kind], recv_sems.at[kind], sides[side]),
        )

    def wait_sides(buffer_x, buffer_y, sems):
        only_if(has_prev, lambda: wait_bytes(buffer_x[0], sems.at[0]))
        only_if(has_next, lambda: wait_bytes(buffer_x[1], sems.at[1]))
        wait_bytes(buffer_y, sems.at[2])

    def wait_faces(step):
        wait_sides(
            (halo_x.at[step, 0], halo_x.at[step, 1]), halo_y.at[step], face_recv_sem.at[step]
        )

    iterate = smooth(source[...])

    pl.semaphore_wait(barrier, announced)
    send_faces(0, iterate)

    loads[2].wait()
    loads[3].wait()
    ends_send[0, 0] = fields_in[1, SIZE - 1]
    for place in range(SIZE):
        ends_send[0, 1, place : place + 1] = fields_in[2, place, SIZE - 1 : SIZE, :]
    for side in range(2):
        to_side(2 * side, ends_send.at[0, side], ends_in.at[0, side], ends_sem.at[0], ends_sem.at[1])

    loads[4].wait()
    loads[5].wait()
    inside = times_ones(
        fields_in[1:5].reshape(4 * SIZE * SIZE, DEPTH), to_inside
    )
    tx, ty, tz, acc = [unflat(inside[64 * place : 64 * place + 64]) for place in range(4)]
    well_diag = jnp.zeros(FIELD, F32)
    for well in range(WELLS):
        well_diag = well_diag + jnp.where(cell_id == well_ids[well], well_index[well], 0.0)
    diag = acc + well_diag
    tx = jnp.where((first == SIZE - 1) & (index_x == count_x - 1), 0.0, tx)
    ty = jnp.where((second == SIZE - 1) & (index_y == count_y - 1), 0.0, ty)
    tz = jnp.where((half == 1) & (lane == 127), 0.0, tz)

    for part in range(2):
        mine = slice(4 * part, 4 * part + 4)
        gop_send[part : part + 1] = agg_rows(diag[:, mine].sum(axis=(0, 1)))
        gop_send[2 + part : 3 + part] = agg_rows(tx[:, 4 * part + 3].sum(axis=0))
        tile = ty[:, mine].sum(axis=(0, 1))
        tile = tile + roll(tile, 64, 1)
        gop_send[4 + part : 5 + part] = jnp.where(
            iota((1, 128), 1) < 64, tile[3:4], tile[7:8]
        )
        tile = tz[1, mine].sum(axis=0)
        gop_send[6 + part : 7 + part] = agg_rows(
            jnp.where(iota((8, 128), 1) >= 64, tile, 0.0)
        )

    def to_all(devices, mine, target, sems):
        for device in devices:
            send(mine, target, sems.at[0], sems.at[1], device)

    to_all(mates, gop_send, gop.at[rank], gop_sem)
    gop[rank] = gop_send[...]

    tz_down = jnp.where((half == 0) & (lane == 0), 0.0, z_neighbours(tz)[1])
    only_if(has_prev, lambda: wait_bytes(ends_in.at[0, 0], ends_sem.at[1, 0]))
    wait_bytes(ends_in.at[0, 1], ends_sem.at[1, 2])
    end_rows = times_ones(ends_in[0].reshape(2 * SIZE, DEPTH), to_inside)
    end_x = jnp.where(index_x == 0, 0.0, end_rows[0:SIZE])
    end_y = jnp.where(index_y == 0, 0.0, end_rows[SIZE:])
    end_x = jnp.concatenate([end_x[None, None, :, :128], end_x[None, None, :, 128:]], axis=0)
    tx_down = jnp.concatenate([end_x, tx[:, : SIZE - 1]], axis=1)
    end_y = jnp.concatenate(
        [
            jnp.broadcast_to(
                end_y[place : place + 1, 128 * part : 128 * part + 128], (8, 128)
            )[None]
            for part in range(2)
            for place in range(SIZE)
        ],
        axis=0,
    ).reshape(FIELD)
    ty_in = jnp.where(second == SIZE - 1, 0.0, ty)
    ty_down_in = row_roll(ty_in, 1)
    ty_edge = ty - ty_in
    ty_down_edge = jnp.where(second == 0, end_y, 0.0)
    coef[0] = (
        diag + tx + tx_down + ty + ty_down_in + ty_down_edge + tz + tz_down
    )
    coef[1] = tx
    coef[2] = tx_down
    coef[3] = ty_in
    coef[4] = ty_down_in
    coef[5] = tz
    coef[6] = tz_down
    coef[7] = ty_edge
    coef[8] = ty_down_edge

    def resid_base(field):
        nothing = jnp.zeros((2, 1, SIZE, 128), F32)
        up_z, down_z = z_neighbours(field)
        return (
            source[...]
            - coef[0] * field
            + coef[1] * jnp.concatenate([field[:, 1:], nothing], axis=1)
            + coef[2] * jnp.concatenate([nothing, field[:, : SIZE - 1]], axis=1)
            + coef[3] * row_roll(field, -1)
            + coef[4] * row_roll(field, 1)
            + coef[5] * up_z
            + coef[6] * down_z
        )

    def resid_edges(resid, high_x, low_x, high_y, low_y):
        first_row = resid[:, 0:1] + (coef[2, :, 0] * low_x)[:, None]
        last_row = resid[:, SIZE - 1 :] + (coef[1, :, SIZE - 1] * high_x)[:, None]
        resid = jnp.concatenate([first_row, resid[:, 1 : SIZE - 1], last_row], axis=1)
        return resid + coef[7] * high_y + coef[8] * low_y

    def halos(step):
        spread = [
            jnp.broadcast_to(halo_y[step, side], (2 * SIZE, 8, 128)).reshape(FIELD)
            for side in (1, 0)
        ]
        return halo_x[step, 1], halo_x[step, 0], spread[0], spread[1]

    resid = resid_base(iterate)
    wait_faces(0)
    resid = resid_edges(resid, *halos(0))
    iterate = iterate + smooth(resid)

    send_faces(1, iterate)
    resid = resid_base(iterate)

    for part in range(2):
        mine = slice(4 * part, 4 * part + 4)
        gres_send[:, 128 * part : 128 * part + 128] = agg_rows(resid[:, mine].sum(axis=(0, 1)))
    flux_up = agg_rows((coef[1, :, SIZE - 1] * iterate[:, SIZE - 1]).sum(axis=0))
    flux_down = agg_rows((coef[2, :, 0] * iterate[:, 0]).sum(axis=0))
    gres_send[:, 256:384] = flux_up
    gres_send[:, 384:512] = flux_down
    edge_send[0] = flux_up
    edge_send[1] = flux_down
    for side in range(2):
        flux = coef[7 + side] * iterate
        lines = []
        for part in range(2):
            tile = flux[:, 4 * part : 4 * part + 4].sum(axis=(0, 1))
            tile = tile + roll(tile, 64, 1)
            lines.append(tile[7:8] if side == 0 else tile[0:1])
        beside_send[side] = jnp.where(iota((1, 128), 1) < 64, lines[0], lines[1])
    to_all(mates, gres_send, gres.at[rank], gres_sem)
    to_all(upper_group, beside_send.at[0], beside.at[0, rank], beside_sem)
    to_all(lower_group, beside_send.at[1], beside.at[1, rank], beside_sem)

    def to_edge(side, target):
        for step in range(GROUP):
            send(
                edge_send.at[side],
                edge_in.at[side, 0],
                edge_sem.at[0, side],
                edge_sem.at[1, side],
                (target + step, index_y),
            )

    only_if(last_member, lambda: to_edge(0, base + GROUP))
    only_if(first_member, lambda: to_edge(1, base - GROUP))
    gres[rank] = gres_send[...]

    wait_bytes(gop.at[1:], gop_sem.at[1])
    shape = (GROUP, 128)
    member = iota(shape, 0)
    lane_c = iota(shape, 1)
    deep = lane_c & 63
    base_a, base_b, tx_a, tx_b, ty_a, ty_b, tz_a, tz_b = [
        gop[:, place, :] for place in range(8)
    ]

    def y_terms(values):
        return jnp.where(lane_c < 64, values, roll(values, 64, 1))

    def z_terms(values, step):
        up = jnp.where(deep < 64 - step, values, 0.0)
        down = jnp.where(deep >= step, roll(values, step, 1), 0.0)
        return up, down

    across_up = jnp.where((member & 1) == 0, tx_b, 0.0)
    across_down = jnp.where((member & 1) == 1, roll(tx_b, 1, 0), 0.0)
    y_a, y_b = y_terms(ty_a), y_terms(ty_b)
    (zu_a, zd_a), (zu_b, zd_b) = z_terms(tz_a, 1), z_terms(tz_b, 1)
    diag_a = base_a + tx_a + across_down + y_a + zu_a + zd_a
    diag_b = base_b + tx_a + across_up + y_b + zu_b + zd_b
    weight_a, weight_b = OMEGA / diag_a, OMEGA / diag_b

    def apply_one(field_a, field_b):
        out_a = (
            diag_a * field_a
            - tx_a * field_b
            - across_down * roll(field_b, 1, 0)
            - y_a * roll(field_a, 64, 1)
            - zu_a * roll(field_a, -1, 1)
            - zd_a * roll(field_a, 1, 1)
        )
        out_b = (
            diag_b * field_b
            - tx_a * field_a
            - across_up * roll(field_a, -1, 0)
            - y_b * roll(field_b, 64, 1)
            - zu_b * roll(field_b, -1, 1)
            - zd_b * roll(field_b, 1, 1)
        )
        return out_a, out_b

    levels = []
    base_k = xor_sum(base_a + base_b, 1, 1)
    tx_k = xor_sum(tx_b, 1, 1)
    ty_k = xor_sum(ty_a + ty_b, 1, 1)
    tz_k = xor_upper(tz_a + tz_b, 1, 1)
    for level in range(2, 5):
        step_x, step_z = 1 << (level - 2), 1 << (level - 1)
        cell_x = member >> (level - 2)
        up_x = jnp.where((cell_x & 3) != 3, tx_k, 0.0)
        down_x = jnp.where((cell_x & 3) != 0, roll(tx_k, step_x, 0), 0.0)
        both_y = y_terms(ty_k)
        up_z, down_z = z_terms(tz_k, step_z)
        diag_k = base_k + up_x + down_x + both_y + up_z + down_z
        levels.append((diag_k, up_x, down_x, both_y, up_z, down_z, step_x, step_z))
        if level < 4:
            base_k = xor_sum(xor_sum(base_k, step_x, 0), step_z, 1)
            ty_k = xor_sum(xor_sum(ty_k, step_x, 0), step_z, 1)
            tx_k = xor_sum(xor_upper(tx_k, step_x, 0), step_z, 1)
            tz_k = xor_upper(xor_sum(tz_k, step_x, 0), step_z, 1)

    def apply_level(field, terms):
        diag_k, up_x, down_x, both_y, up_z, down_z, step_x, step_z = terms
        return (
            diag_k * field
            - up_x * roll(field, -step_x, 0)
            - down_x * roll(field, step_x, 0)
            - both_y * roll(field, 64, 1)
            - up_z * roll(field, -step_z, 1)
            - down_z * roll(field, step_z, 1)
        )

    lane_row = iota((128, 128), 0)
    lane_col = iota((128, 128), 1)
    real = lane_col < 64
    same_place = ((lane_row >> 6) == ((lane_col >> 3) & 1)) & (
        ((lane_row & 63) >> 3) == (lane_col & 7)
    )
    pick_one = (real & same_place & ((lane_row & 7) == 0)).astype(F32).astype(BF16)
    pick_two = (real & same_place & ((lane_row & 3) == 0)).astype(F32).astype(BF16)
    own_x = (member >> 2) == (lane_c >> 4)
    diag_k, up_x, down_x, both_y, up_z, down_z, _, _ = levels[2]
    picked = times_ones(
        jnp.concatenate(
            [1.0 / diag_k, up_x, down_x, both_y, up_z, down_z], axis=0
        ),
        pick_one,
    )
    one_member = own_x & ((member & 3) == 0)
    inverse_diag, up_x, down_x, both_y, up_z, down_z = [
        jnp.sum(
            jnp.where(one_member, picked[GROUP * place : GROUP * place + GROUP], 0.0),
            axis=0,
            keepdims=True,
        )
        for place in range(6)
    ]
    gap = lane_row - lane_col
    upper_y = (lane_col >> 3) & 1
    coupling = jnp.where(gap == 16, up_x, 0.0)
    coupling = jnp.where(gap == -16, down_x, coupling)
    coupling = jnp.where(gap == 8 - 16 * upper_y, both_y, coupling)
    coupling = jnp.where(gap == 1, up_z, coupling)
    coupling = jnp.where(gap == -1, down_z, coupling)
    power = coupling * inverse_diag
    total = power + jnp.where(gap == 0, 1.0, 0.0)
    for _ in range(DOUBLINGS):
        power = jnp.dot(power, power, precision=HIGHEST, preferred_element_type=F32)
        total = total + jnp.dot(
            total, power, precision=HIGHEST, preferred_element_type=F32
        )
    spread = jnp.concatenate(
        [
            ((lane_row >> 4) == part)
            & ((lane_row >> 3 & 1) == (lane_col >> 6))
            & ((lane_row & 7) == ((lane_col & 63) >> 3))
            & (lane_row < 64)
            for part in range(4)
        ],
        axis=1,
    )
    solver = times_ones(total, spread.astype(F32).astype(BF16))

    wait_faces(1)
    high_x, low_x, high_y, low_y = halos(1)

    wait_bytes(gres.at[1:], gres_sem.at[1])
    wait_bytes(beside, beside_sem.at[1])
    only_if(group_before, lambda: wait_bytes(edge_in.at[0, 0], edge_sem.at[1, 0]))
    only_if(group_after, lambda: wait_bytes(edge_in.at[1, 0], edge_sem.at[1, 1]))
    every = gres[:, 0, :]
    first_a, first_b, from_low, from_high = [
        every[:, 128 * part : 128 * part + 128] for part in range(4)
    ]
    from_low = jnp.where(member == 0, edge_in[0, 0], roll(from_low, 1, 0))
    from_high = jnp.where(member == GROUP - 1, edge_in[1, 0], roll(from_high, -1, 0))
    below, above = beside[0, :, 0, :], beside[1, :, 0, :]
    res_a = first_a + from_low + jnp.where(lane_c < 64, below, roll(above, 64, 1))
    res_b = first_b + from_high + jnp.where(lane_c < 64, roll(below, 64, 1), above)

    def descend_one(res_a, res_b):
        cor_a, cor_b = weight_a * res_a, weight_b * res_b
        out_a, out_b = apply_one(cor_a, cor_b)
        cor_a = cor_a + weight_a * (res_a - out_a)
        cor_b = cor_b + weight_b * (res_b - out_b)
        out_a, out_b = apply_one(cor_a, cor_b)
        return cor_a, cor_b, (res_a - out_a) + (res_b - out_b)

    cor_a, cor_b, left = descend_one(res_a, res_b)
    res_k = xor_sum(left, 1, 1)
    cor_k = jnp.zeros(shape, F32)
    for level in (2, 3):
        terms = levels[level - 2]
        weight = OMEGA / terms[0]
        cor = weight * res_k
        cor = cor + weight * (res_k - apply_level(cor, terms))
        left = res_k - apply_level(cor, terms)
        cor_k = cor_k + cor
        if level == 2:
            res_k = xor_sum(xor_sum(left, 1, 0), 2, 1)
    last = times_ones(left, pick_two)
    last = jnp.sum(
        jnp.where(own_x & ((member & 1) == 0), last, 0.0), axis=0, keepdims=True
    )
    last = jnp.broadcast_to(last * inverse_diag, (8, 128))
    solved = jnp.dot(last, solver, precision=HIGHEST, preferred_element_type=F32)
    solved = [jnp.broadcast_to(solved[0:1, 128 * part : 128 * part + 128], (8, 128)) for part in range(4)]
    upper_rows = (iota((8, 128), 0) & 4) != 0
    cor_k = cor_k + jnp.concatenate(
        [
            jnp.where(upper_rows, solved[1], solved[0]),
            jnp.where(upper_rows, solved[3], solved[2]),
        ],
        axis=0,
    )
    tail[0] = cor_a + cor_k
    tail[1] = cor_b + cor_k
    tail_send[0] = tail[0, pl.ds(rank, 1), :]
    tail_send[1] = tail[1, pl.ds(rank, 1), :]
    for side in range(4):
        to_side(side, tail_send, tail_in.at[side], tail_sem.at[0], tail_sem.at[1])

    def over_aggregates(line):
        return turned(jnp.broadcast_to(line, (8, 128)))

    added = [over_aggregates(tail_send[part]) for part in range(2)]
    added = jnp.concatenate([added[place // 4][None] for place in range(SIZE)], axis=0)
    iterate = iterate + jnp.broadcast_to(added[None], FIELD)
    resid = resid_base(iterate)
    wait_sides((tail_in.at[0], tail_in.at[1]), tail_in.at[2:4], tail_sem.at[1])
    high_x = high_x + over_aggregates(tail_in[1, 0])[None]
    low_x = low_x + over_aggregates(tail_in[0, 1])[None]
    lower_lanes = iota((8, 128), 1) < 64

    def over_rows(side, upper):
        lines = []
        for part in range(2):
            line = jnp.broadcast_to(tail_in[side, part], (8, 128))
            moved = roll(line, 64, 1)
            line = jnp.where(lower_lanes, moved, line) if upper else jnp.where(lower_lanes, line, moved)
            lines.append(line)
        tiles = jnp.concatenate([lines[place // 4][None] for place in range(SIZE)], axis=0)
        return jnp.broadcast_to(tiles[None], FIELD)

    high_y = high_y + over_rows(3, False)
    low_y = low_y + over_rows(2, True)
    resid = resid_edges(resid, high_x, low_x, high_y, low_y)
    iterate = iterate + smooth(resid)

    send_faces(2, iterate)
    resid = resid_base(iterate)
    wait_faces(2)
    resid = resid_edges(resid, *halos(2))
    iterate = iterate + smooth(resid)

    send_faces(3, iterate)
    out_buf[0] = iterate
    stores = [
        pltpu.make_async_copy(out_buf.at[place], both_any.at[place], store_sem.at[place])
        for place in range(2)
    ]
    stores[0].start()
    resid = resid_base(iterate)
    wait_faces(3)
    out_buf[1] = resid_edges(resid, *halos(3))
    stores[1].start()
    only_if(has_next, lambda: wait_bytes(face_x.at[:, 0], face_send_sem.at[0]))
    only_if(has_prev, lambda: wait_bytes(face_x.at[:, 1], face_send_sem.at[1]))
    wait_bytes(face_y, face_send_sem.at[2])
    only_if(has_next, lambda: wait_bytes(ends_send.at[0, 0], ends_sem.at[0, 0]))
    wait_bytes(ends_send.at[0, 1], ends_sem.at[0, 2])
    wait_bytes(gop.at[1:], gop_sem.at[0])
    wait_bytes(gres.at[1:], gres_sem.at[0])
    wait_bytes(beside, beside_sem.at[0])
    only_if(last_member, lambda: wait_bytes(edge_in.at[0], edge_sem.at[0, 0]))
    only_if(first_member, lambda: wait_bytes(edge_in.at[1], edge_sem.at[0, 1]))
    only_if(has_next, lambda: wait_bytes(tail_in.at[0], tail_sem.at[0, 0]))
    only_if(has_prev, lambda: wait_bytes(tail_in.at[1], tail_sem.at[0, 1]))
    wait_bytes(tail_in.at[2:4], tail_sem.at[0, 2])
    for store in stores:
        store.wait()


def to_outer_order(both, pressure, resid):
    row = iota((DEPTH, DEPTH), 0)
    col = iota((DEPTH, DEPTH), 1)
    to_outside = (col == 4 * (row & 63) + (row >> 6)).astype(F32).astype(BF16)
    for place, out in enumerate((pressure, resid)):
        out[...] = times_ones(flat(both[place]), to_outside).reshape(SIZE, SIZE, DEPTH)


def on_device(
    count_x,
    count_y,
    pressure_rhs,
    accumulation,
    trans_x,
    trans_y,
    trans_z,
    well_cells,
    well_flags,
    well_rates,
    well_index,
    block_map,
    block_inverses,
):
    anywhere = pl.BlockSpec(memory_space=pl.ANY)
    dma = pltpu.SemaphoreType.DMA
    out = jax.ShapeDtypeStruct(pressure_rhs.shape, F32)
    both = pl.pallas_call(
        functools.partial(kernel, count_x, count_y),
        out_shape=jax.ShapeDtypeStruct((2,) + FIELD, F32),
        in_specs=[anywhere] * 11,
        out_specs=anywhere,
        scratch_shapes=[
            pltpu.VMEM((5, SIZE, SIZE, DEPTH), F32),
            pltpu.VMEM((2, 2, 64), jnp.int32),
            pltpu.SMEM((WELLS,), jnp.int32),
            pltpu.SMEM((WELLS,), jnp.int32),
            pltpu.SMEM((WELLS,), F32),
            pltpu.SMEM((WELLS,), F32),
            pltpu.VMEM((KINDS * 64, 64), F32),
            pltpu.VMEM((KINDS * 64, DEPTH), BF16),
            pltpu.VMEM(FIELD, F32),
            pltpu.VMEM((9,) + FIELD, F32),
            pltpu.VMEM((4, 2, 2, SIZE, 128), F32),
            pltpu.VMEM((4, 2, 2 * SIZE, 1, 128), F32),
            pltpu.VMEM((4, 2, 2, SIZE, 128), F32),
            pltpu.VMEM((4, 2, 2 * SIZE, 1, 128), F32),
            pltpu.VMEM((1, 2, SIZE, DEPTH), F32),
            pltpu.VMEM((1, 2, SIZE, DEPTH), F32),
            pltpu.VMEM((8, 128), F32),
            pltpu.VMEM((GROUP, 8, 128), F32),
            pltpu.VMEM((1, 512), F32),
            pltpu.VMEM((GROUP, 1, 512), F32),
            pltpu.VMEM((2, 1, 128), F32),
            pltpu.VMEM((2, GROUP, 1, 128), F32),
            pltpu.VMEM((2, 1, 128), F32),
            pltpu.VMEM((2, GROUP, 1, 128), F32),
            pltpu.VMEM((2, GROUP, 128), F32),
            pltpu.VMEM((2, 1, 128), F32),
            pltpu.VMEM((4, 2, 1, 128), F32),
            pltpu.VMEM((2,) + FIELD, F32),
            dma((11,)),
            dma((2,)),
            dma((3,)),
            dma((4, 3)),
            dma((2, 3)),
            dma((2,)),
            dma((2,)),
            dma((2,)),
            dma((2, 2)),
            dma((2, 3)),
        ],
        compiler_params=pltpu.CompilerParams(
            collective_id=0, has_side_effects=True, vmem_limit_bytes=60 * 1024 * 1024
        ),
    )(
        pressure_rhs,
        accumulation,
        trans_x,
        trans_y,
        trans_z,
        well_cells,
        well_flags,
        well_rates,
        well_index,
        block_map,
        block_inverses.reshape(KINDS * 64, 64),
    )
    return pl.pallas_call(to_outer_order, out_shape=(out, out))(both)


def solution(mesh):
    cells = P("gx", "gy", None)
    wells = P(("gx", "gy"))
    return jax.shard_map(
        functools.partial(on_device, mesh.shape["gx"], mesh.shape["gy"]),
        mesh=mesh,
        in_specs=(cells,) * 5 + (wells,) * 4 + (cells, P()),
        out_specs=(cells, cells),
        check_vma=False,
    )
```

```python
import functools

import jax
import jax.numpy as jnp
from jax import lax
from jax.experimental import pallas as pl
from jax.experimental.pallas import tpu as pltpu
from jax.sharding import PartitionSpec as P

OMEGA = 0.8
GROUP = 16
SIZE = 8
DEPTH = 256
KINDS = 16
WELLS = 4
DOUBLINGS = 10
MESH = pl.DeviceIdType.MESH
HIGHEST = lax.Precision.HIGHEST
F32 = jnp.float32
BF16 = jnp.bfloat16
FIELD = (2, SIZE, SIZE, 128)


def iota(shape, dim):
    return lax.broadcasted_iota(jnp.int32, shape, dim)


def roll(values, shift, axis):
    return pltpu.roll(values, shift % values.shape[axis], axis)


def split_three(values):
    high = values.astype(BF16)
    rest = values - high.astype(F32)
    middle = rest.astype(BF16)
    low = (rest - middle.astype(F32)).astype(BF16)
    return high, middle, low


def split_two(values):
    high = values.astype(BF16)
    low = (values - high.astype(F32)).astype(BF16)
    return high, low


def times_ones(values, ones):
    return sum(jnp.dot(part, ones, preferred_element_type=F32) for part in split_three(values))


def flat(field):
    return jnp.concatenate(
        [field[0].reshape(SIZE * SIZE, 128), field[1].reshape(SIZE * SIZE, 128)], axis=1
    )


def unflat(rows):
    shape = (1, SIZE, SIZE, 128)
    return jnp.concatenate(
        [rows[:, :128].reshape(shape), rows[:, 128:].reshape(shape)], axis=0
    )


def lane_roll(field, shift):
    return roll(field.reshape(-1, 8, 128), shift, 2).reshape(field.shape)


def row_roll(field, shift):
    return roll(field.reshape(-1, 8, 128), shift, 1).reshape(field.shape)


def z_neighbours(field):
    low, high = field[0], field[1]
    lower_lanes = iota(low.shape, 2) < 64
    across = lane_roll(jnp.where(lower_lanes, high, low), 64)
    up = [across, jnp.where(lower_lanes, lane_roll(high, 64), lane_roll(low, 63))]
    down = [jnp.where(lower_lanes, lane_roll(high, 65), lane_roll(low, 64)), across]
    return (
        jnp.concatenate([part[None] for part in up], axis=0),
        jnp.concatenate([part[None] for part in down], axis=0),
    )


def turned(field):
    shape = (field.size // 1024, 8, 128)
    same = (iota(shape, 1) >= 4) == (iota(shape, 2) >= 64)
    tiles = field.reshape(shape)
    return jnp.where(same, tiles, roll(roll(tiles, 4, 1), 64, 2)).reshape(field.shape)


def agg_rows(tile):
    tile = tile + roll(tile, 64, 1)
    tile = tile + roll(tile, -1, 0)
    tile = tile + roll(tile, -2, 0)
    return jnp.where(iota((1, 128), 1) < 64, tile[0:1], tile[4:5])


def xor_sum(values, step, axis):
    place = iota(values.shape, axis)
    return values + jnp.where(
        (place & step) == 0, roll(values, -step, axis), roll(values, step, axis)
    )


def xor_upper(values, step, axis):
    place = iota(values.shape, axis)
    return jnp.where((place & step) == 0, roll(values, -step, axis), values)


def only_if(condition, action):
    if condition is None:
        action()
    else:
        pl.when(condition)(action)


def send(src, dst, send_sem, recv_sem, device):
    pltpu.make_async_remote_copy(
        src_ref=src,
        dst_ref=dst,
        send_sem=send_sem,
        recv_sem=recv_sem,
        device_id=device,
        device_id_type=MESH,
    ).start()


def wait_bytes(like, sem):
    pltpu.make_async_copy(like, like, sem).wait()


def kernel(
    count_x,
    count_y,
    rhs_any,
    acc_any,
    tx_any,
    ty_any,
    tz_any,
    cells_any,
    flags_any,
    rates_any,
    index_any,
    map_any,
    inv_any,
    both_any,
    fields_in,
    map_in,
    cells,
    flags,
    rates,
    well_index,
    inv_in,
    blocks,
    source,
    coef,
    face_x,
    face_y,
    halo_x,
    halo_y,
    ends_in,
    ends_send,
    gop_send,
    gop,
    gres_send,
    gres,
    beside_send,
    beside,
    edge_send,
    edge_in,
    tail,
    tail_send,
    tail_in,
    out_buf,
    agg,
    resid_two,
    side_x,
    side_y,
    late_send_x,
    late_send_y,
    late_x,
    late_y,
    blocks_x,
    blocks_y,
    sizes,
    load_sem,
    store_sem,
    face_send_sem,
    face_recv_sem,
    ends_sem,
    gop_sem,
    gres_sem,
    beside_sem,
    edge_sem,
    tail_sem,
    agg_sem,
    more_sem,
):
    index_x = lax.axis_index("gx")
    index_y = lax.axis_index("gy")
    rank = lax.rem(index_x, GROUP)
    base = index_x - rank
    next_x = (lax.rem(index_x + 1, count_x), index_y)
    prev_x = (lax.rem(index_x + count_x - 1, count_x), index_y)
    next_y = (index_x, lax.rem(index_y + 1, count_y))
    prev_y = (index_x, lax.rem(index_y + count_y - 1, count_y))
    sides = (next_x, prev_x, next_y, prev_y)
    steps = sorted(range(GROUP), key=lambda step: -min(step % 8, -step % 8))
    members = [base + lax.rem(rank + step, GROUP) for step in steps]
    mates = [(member, index_y) for step, member in zip(steps, members) if step > 0]
    upper_group = [(member, next_y[1]) for member in members]
    lower_group = [(member, prev_y[1]) for member in members]
    has_next = index_x < count_x - 1
    has_prev = index_x > 0
    group_after = base + GROUP < count_x
    group_before = base > 0
    last_member = group_after & (rank == GROUP - 1)
    first_member = group_before & (rank == 0)
    send_if = (has_next, has_prev, None, None)

    loads = [
        pltpu.make_async_copy(src, dst, load_sem.at[place])
        for place, (src, dst) in enumerate(
            (
                (inv_any, inv_in),
                (rhs_any, fields_in.at[0]),
                (tx_any, fields_in.at[1]),
                (ty_any, fields_in.at[2]),
                (tz_any, fields_in.at[3]),
                (acc_any, fields_in.at[4]),
                (map_any, map_in),
                (cells_any, cells),
                (flags_any, flags),
                (rates_any, rates),
                (index_any, well_index),
            )
        )
    ]
    for load in loads:
        load.start()
    halo_x[...] = jnp.zeros_like(halo_x)
    ends_in[...] = jnp.zeros_like(ends_in)
    edge_in[...] = jnp.zeros_like(edge_in)
    tail_in[...] = jnp.zeros_like(tail_in)
    side_x[...] = jnp.zeros_like(side_x)
    late_x[...] = jnp.zeros_like(late_x)

    barrier = pltpu.get_barrier_semaphore()

    def announce(device):
        pl.semaphore_signal(barrier, inc=1, device_id=device, device_id_type=MESH)

    for several in zip(upper_group, lower_group, mates + [None]):
        for device in several:
            if device is not None:
                announce(device)
    only_if(group_after, lambda: announce((base + GROUP, index_y)))
    only_if(group_before, lambda: announce((base - 1, index_y)))
    for other_y in (next_y[1], prev_y[1]):
        only_if(last_member, lambda other_y=other_y: announce((index_x + 1, other_y)))
        only_if(first_member, lambda other_y=other_y: announce((index_x - 1, other_y)))
    announced = (
        len(mates)
        + 2 * GROUP
        + (GROUP + 2) * (last_member.astype(jnp.int32) + first_member.astype(jnp.int32))
    )

    row = iota((DEPTH, DEPTH), 0)
    col = iota((DEPTH, DEPTH), 1)
    to_inside = (row == 4 * (col & 63) + (col >> 6)).astype(F32).astype(BF16)
    lane = iota(FIELD, 3)
    second = iota(FIELD, 2)
    first = iota(FIELD, 1)
    half = iota(FIELD, 0)
    cell_id = ((half * SIZE + first) * SIZE + second) * 128 + lane

    def swapped_offsets(place):
        return (place & ~15) | ((place & 3) << 2) | ((place >> 2) & 3)

    row_k = iota((128, DEPTH), 0)
    col_k = iota((128, DEPTH), 1)
    take_cols = ((row_k & 63) == swapped_offsets(col_k & 63)) & ((row_k < 64) == (col_k < 128))
    take_cols = take_cols.astype(F32).astype(BF16)
    loads[0].wait()
    tiles = [
        (OMEGA * inv_in[pl.ds(third, KINDS * 16, stride=4), :]).reshape(KINDS * 2, 8, 64)
        for third in range(4)
    ]
    upper_half = iota((KINDS * 2, 8, 64), 1) >= 4
    rows = jnp.concatenate(
        [
            tile[:, None]
            for tile in (
                jnp.where(upper_half, roll(tiles[1], 4, 1), tiles[0]),
                jnp.where(upper_half, roll(tiles[3], 4, 1), tiles[2]),
                jnp.where(upper_half, tiles[1], roll(tiles[0], 4, 1)),
                jnp.where(upper_half, tiles[3], roll(tiles[2], 4, 1)),
            )
        ],
        axis=1,
    ).reshape(KINDS * 64, 64)
    high, low = split_two(rows)
    blocks[...] = jnp.dot(
        jnp.concatenate([high, low], axis=1), take_cols, preferred_element_type=F32
    ).astype(BF16)

    for place in range(7, 11):
        loads[place].wait()
    plane_cells = SIZE * count_y * DEPTH
    well_ids = []
    for well in range(WELLS):
        cell = cells[well]
        pos_x = cell // plane_cells - index_x * SIZE
        left = lax.rem(cell, plane_cells)
        pos_y = left // DEPTH - index_y * SIZE
        pos_z = lax.rem(left, DEPTH)
        place = lax.rem(pos_z, 4) * 64 + pos_z // 4
        well_ids.append(
            ((place // 128 * SIZE + pos_x) * SIZE + pos_y) * 128 + lax.rem(place, 128)
        )
    signed = [
        jnp.where(flags[well] == 1, rates[well], -rates[well]) for well in range(WELLS)
    ]

    loads[1].wait()
    well_source = jnp.zeros(FIELD, F32)
    for well in range(WELLS):
        well_source = well_source + jnp.where(cell_id == well_ids[well], signed[well], 0.0)
    source[...] = (
        unflat(times_ones(fields_in[0].reshape(SIZE * SIZE, DEPTH), to_inside)) + well_source
    )

    loads[6].wait()
    kinds = []
    for part in range(2):
        kind = map_in[part]
        kinds.append(jnp.concatenate([kind[0:1], kind[1:2]], axis=1))
    kind_ids = jnp.broadcast_to(jnp.concatenate(kinds, axis=1), (8, 256))

    def products(field, operators, rows, kind_row):
        tiles = turned(field)
        columns = jnp.concatenate(
            [
                jnp.concatenate(
                    [
                        tiles[half_id, 4 * part + offset]
                        for offset in range(4)
                        for half_id in range(2)
                    ],
                    axis=0,
                )
                for part in range(2)
            ],
            axis=1,
        )
        high, low = split_two(columns)
        product = jnp.dot(
            operators[...],
            jnp.concatenate([high, low, high, low], axis=0),
            preferred_element_type=F32,
        )
        chosen = product[0:rows]
        for kind in range(1, KINDS):
            mask = jnp.broadcast_to((kind_row == kind)[None], (rows // 8, 8, 256))
            chosen = jnp.where(
                mask.reshape(rows, 256), product[rows * kind : rows * kind + rows], chosen
            )
        return chosen

    def smooth(resid, operators=blocks, kind_row=kind_ids):
        chosen = products(resid, operators, 64, kind_row)
        back = [
            [
                chosen[8 * (2 * offset + half_id) : 8 * (2 * offset + half_id) + 8,
                       128 * part : 128 * part + 128][None]
                for part in range(2)
                for offset in range(4)
            ]
            for half_id in range(2)
        ]
        field = jnp.concatenate(
            [jnp.concatenate(tiles, axis=0)[None] for tiles in back], axis=0
        )
        return turned(field)

    def send_faces(step, field):
        face_x[step, 0] = field[:, SIZE - 1]
        face_x[step, 1] = field[:, 0]
        tiles = field.reshape(2 * SIZE, 8, 128)
        face_y[step, 0] = tiles[:, 7:8, :]
        face_y[step, 1] = tiles[:, 0:1, :]
        for side, (out, into) in enumerate(
            ((face_x, halo_x), (face_x, halo_x), (face_y, halo_y), (face_y, halo_y))
        ):
            to_side(
                side,
                out.at[step, side % 2],
                into.at[step, side % 2],
                face_send_sem,
                face_recv_sem.at[step],
            )

    def to_side(side, src, dst, send_sems, recv_sems):
        kind = min(side, 2)
        only_if(
            send_if[side],
            lambda: send(src, dst, send_sems.at[kind], recv_sems.at[kind], sides[side]),
        )

    def wait_sides(buffer_x, buffer_y, sems):
        only_if(has_prev, lambda: wait_bytes(buffer_x[0], sems.at[0]))
        only_if(has_next, lambda: wait_bytes(buffer_x[1], sems.at[1]))
        wait_bytes(buffer_y, sems.at[2])

    def wait_faces(step):
        wait_sides(
            (halo_x.at[step, 0], halo_x.at[step, 1]), halo_y.at[step], face_recv_sem.at[step]
        )

    iterate = smooth(source[...])

    loads[2].wait()
    loads[3].wait()
    ends_send[0, 0] = fields_in[1, SIZE - 1]
    for place in range(SIZE):
        ends_send[0, 1, place : place + 1] = fields_in[2, place, SIZE - 1 : SIZE, :]
    loads[4].wait()
    loads[5].wait()
    inside = times_ones(
        fields_in[1:5].reshape(4 * SIZE * SIZE, DEPTH), to_inside
    )
    tx, ty, tz, acc = [unflat(inside[64 * place : 64 * place + 64]) for place in range(4)]
    well_diag = jnp.zeros(FIELD, F32)
    for well in range(WELLS):
        well_diag = well_diag + jnp.where(cell_id == well_ids[well], well_index[well], 0.0)
    diag = acc + well_diag
    tx = jnp.where((first == SIZE - 1) & (index_x == count_x - 1), 0.0, tx)
    ty = jnp.where((second == SIZE - 1) & (index_y == count_y - 1), 0.0, ty)
    tz = jnp.where((half == 1) & (lane == 127), 0.0, tz)

    for part in range(2):
        mine = slice(4 * part, 4 * part + 4)
        gop_send[part : part + 1] = agg_rows(diag[:, mine].sum(axis=(0, 1)))
        gop_send[2 + part : 3 + part] = agg_rows(tx[:, 4 * part + 3].sum(axis=0))
        tile = ty[:, mine].sum(axis=(0, 1))
        tile = tile + roll(tile, 64, 1)
        gop_send[4 + part : 5 + part] = jnp.where(
            iota((1, 128), 1) < 64, tile[3:4], tile[7:8]
        )
        tile = tz[1, mine].sum(axis=0)
        gop_send[6 + part : 7 + part] = agg_rows(
            jnp.where(iota((8, 128), 1) >= 64, tile, 0.0)
        )

    tz_down = jnp.where((half == 0) & (lane == 0), 0.0, z_neighbours(tz)[1])
    agg[0] = diag
    agg[1] = jnp.zeros(FIELD, F32)
    for place, layer in ((3, 3), (4, 3), (7, 7)):
        agg[1, :, place] = tx[:, layer]
    for part in range(2):
        agg[1, 0, 4 * part + 1] = kind_ids[:, 128 * part : 128 * part + 128].astype(F32)
    agg[2] = jnp.where(
        (second & 3) == 3, ty, jnp.where(second == 4, row_roll(ty, 1), 0.0)
    )
    agg[3] = jnp.where(
        (half == 0) & (lane < 64), tz_down, jnp.where((half == 1) & (lane >= 64), tz, 0.0)
    )

    pl.semaphore_wait(barrier, announced)
    send_faces(0, iterate)

    for side in range(2):
        to_side(2 * side, ends_send.at[0, side], ends_in.at[0, side], ends_sem.at[0], ends_sem.at[1])

    def to_all(devices, mine, target, sems):
        for device in devices:
            send(mine, target, sems.at[0], sems.at[1], device)

    to_all(mates, gop_send, gop.at[rank], gop_sem)
    gop[rank] = gop_send[...]

    for side, part in enumerate((slice(4, 8), slice(0, 4))):
        to_side(side, agg.at[:, :, part], side_x.at[side, 0:4], agg_sem.at[0], agg_sem.at[1])
        to_side(2 + side, agg, side_y.at[side, 0:4], agg_sem.at[0], agg_sem.at[1])

    for kind in range(KINDS):
        blocks_x[32 * kind : 32 * kind + 16, :] = blocks[64 * kind : 64 * kind + 16, :]
        blocks_x[32 * kind + 16 : 32 * kind + 32, :] = blocks[64 * kind + 48 : 64 * kind + 64, :]
    mirror = (col == (row ^ 3)).astype(F32).astype(BF16)
    for part in range(KINDS // 4):
        here = slice(part * DEPTH, (part + 1) * DEPTH)
        blocks_y[here, :] = jnp.dot(
            mirror, blocks[here, :], preferred_element_type=F32
        ).astype(BF16)

    only_if(has_prev, lambda: wait_bytes(ends_in.at[0, 0], ends_sem.at[1, 0]))
    wait_bytes(ends_in.at[0, 1], ends_sem.at[1, 2])
    end_rows = times_ones(ends_in[0].reshape(2 * SIZE, DEPTH), to_inside)
    end_x = jnp.where(index_x == 0, 0.0, end_rows[0:SIZE])
    end_y = jnp.where(index_y == 0, 0.0, end_rows[SIZE:])
    end_x = jnp.concatenate([end_x[None, None, :, :128], end_x[None, None, :, 128:]], axis=0)
    tx_down = jnp.concatenate([end_x, tx[:, : SIZE - 1]], axis=1)
    for part in range(2):
        for place in range(SIZE):
            late_send_x[SIZE * part + place] = end_y[
                place : place + 1, 128 * part : 128 * part + 128
            ]
    late_send_y[...] = end_x[:, 0]
    end_y = jnp.broadcast_to(late_send_x[...], (2 * SIZE, 8, 128)).reshape(FIELD)
    ty_in = jnp.where(second == SIZE - 1, 0.0, ty)
    ty_down_in = row_roll(ty_in, 1)
    ty_edge = ty - ty_in
    ty_down_edge = jnp.where(second == 0, end_y, 0.0)
    coef[0] = (
        diag + tx + tx_down + ty + ty_down_in + ty_down_edge + tz + tz_down
    )
    coef[1] = tx
    coef[2] = tx_down
    coef[3] = ty_in
    coef[4] = ty_down_in
    coef[5] = tz
    coef[6] = tz_down
    coef[7] = ty_edge
    coef[8] = ty_down_edge
    tx_at = [tx[:, 3], tx[:, 7]]

    def resid_base(field):
        nothing = jnp.zeros((2, 1, SIZE, 128), F32)
        up_z, down_z = z_neighbours(field)
        return (
            source[...]
            - coef[0] * field
            + coef[1] * jnp.concatenate([field[:, 1:], nothing], axis=1)
            + coef[2] * jnp.concatenate([nothing, field[:, : SIZE - 1]], axis=1)
            + coef[3] * row_roll(field, -1)
            + coef[4] * row_roll(field, 1)
            + coef[5] * up_z
            + coef[6] * down_z
        )

    def resid_edges(resid, high_x, low_x, high_y, low_y):
        first_row = resid[:, 0:1] + (coef[2, :, 0] * low_x)[:, None]
        last_row = resid[:, SIZE - 1 :] + (coef[1, :, SIZE - 1] * high_x)[:, None]
        resid = jnp.concatenate([first_row, resid[:, 1 : SIZE - 1], last_row], axis=1)
        return resid + coef[7] * high_y + coef[8] * low_y

    def halos(step):
        spread = [
            jnp.broadcast_to(halo_y[step, side], (2 * SIZE, 8, 128)).reshape(FIELD)
            for side in (1, 0)
        ]
        return halo_x[step, 1], halo_x[step, 0], spread[0], spread[1]

    resid = resid_base(iterate)
    wait_faces(0)
    resid = resid_edges(resid, *halos(0))
    iterate = iterate + smooth(resid)

    send_faces(1, iterate)
    resid = resid_base(iterate)

    for part in range(2):
        mine = slice(4 * part, 4 * part + 4)
        gres_send[:, 128 * part : 128 * part + 128] = agg_rows(resid[:, mine].sum(axis=(0, 1)))
    flux_up = agg_rows((coef[1, :, SIZE - 1] * iterate[:, SIZE - 1]).sum(axis=0))
    flux_down = agg_rows((coef[2, :, 0] * iterate[:, 0]).sum(axis=0))
    gres_send[:, 256:384] = flux_up
    gres_send[:, 384:512] = flux_down
    edge_send[0] = flux_up
    edge_send[1] = flux_down
    for side in range(2):
        flux = coef[7 + side] * iterate
        lines = []
        for part in range(2):
            tile = flux[:, 4 * part : 4 * part + 4].sum(axis=(0, 1))
            tile = tile + roll(tile, 64, 1)
            lines.append(tile[7:8] if side == 0 else tile[0:1])
        beside_send[side] = jnp.where(iota((1, 128), 1) < 64, lines[0], lines[1])
    to_all(mates, gres_send, gres.at[rank], gres_sem)
    to_all(upper_group, beside_send.at[0], beside.at[0, rank], beside_sem)
    to_all(lower_group, beside_send.at[1], beside.at[1, rank], beside_sem)

    def to_edge(side, target):
        for step in range(GROUP):
            send(
                edge_send.at[side],
                edge_in.at[side, 0],
                edge_sem.at[0, side],
                edge_sem.at[1, side],
                (target + step, index_y),
            )

    only_if(last_member, lambda: to_edge(0, base + GROUP))
    only_if(first_member, lambda: to_edge(1, base - GROUP))
    gres[rank] = gres_send[...]

    wait_bytes(gop.at[1:], gop_sem.at[1])
    shape = (GROUP, 128)
    member = iota(shape, 0)
    lane_c = iota(shape, 1)
    deep = lane_c & 63
    base_a, base_b, tx_a, tx_b, ty_a, ty_b, tz_a, tz_b = [
        gop[:, place, :] for place in range(8)
    ]

    def y_terms(values):
        return jnp.where(lane_c < 64, values, roll(values, 64, 1))

    def z_terms(values, step):
        up = jnp.where(deep < 64 - step, values, 0.0)
        down = jnp.where(deep >= step, roll(values, step, 1), 0.0)
        return up, down

    across_up = jnp.where((member & 1) == 0, tx_b, 0.0)
    across_down = jnp.where((member & 1) == 1, roll(tx_b, 1, 0), 0.0)
    y_a, y_b = y_terms(ty_a), y_terms(ty_b)
    (zu_a, zd_a), (zu_b, zd_b) = z_terms(tz_a, 1), z_terms(tz_b, 1)
    diag_a = base_a + tx_a + across_down + y_a + zu_a + zd_a
    diag_b = base_b + tx_a + across_up + y_b + zu_b + zd_b
    weight_a, weight_b = OMEGA / diag_a, OMEGA / diag_b

    def apply_one(field_a, field_b):
        out_a = (
            diag_a * field_a
            - tx_a * field_b
            - across_down * roll(field_b, 1, 0)
            - y_a * roll(field_a, 64, 1)
            - zu_a * roll(field_a, -1, 1)
            - zd_a * roll(field_a, 1, 1)
        )
        out_b = (
            diag_b * field_b
            - tx_a * field_a
            - across_up * roll(field_a, -1, 0)
            - y_b * roll(field_b, 64, 1)
            - zu_b * roll(field_b, -1, 1)
            - zd_b * roll(field_b, 1, 1)
        )
        return out_a, out_b

    levels = []
    base_k = xor_sum(base_a + base_b, 1, 1)
    tx_k = xor_sum(tx_b, 1, 1)
    ty_k = xor_sum(ty_a + ty_b, 1, 1)
    tz_k = xor_upper(tz_a + tz_b, 1, 1)
    for level in range(2, 5):
        step_x, step_z = 1 << (level - 2), 1 << (level - 1)
        cell_x = member >> (level - 2)
        up_x = jnp.where((cell_x & 3) != 3, tx_k, 0.0)
        down_x = jnp.where((cell_x & 3) != 0, roll(tx_k, step_x, 0), 0.0)
        both_y = y_terms(ty_k)
        up_z, down_z = z_terms(tz_k, step_z)
        diag_k = base_k + up_x + down_x + both_y + up_z + down_z
        levels.append((diag_k, up_x, down_x, both_y, up_z, down_z, step_x, step_z))
        if level < 4:
            base_k = xor_sum(xor_sum(base_k, step_x, 0), step_z, 1)
            ty_k = xor_sum(xor_sum(ty_k, step_x, 0), step_z, 1)
            tx_k = xor_sum(xor_upper(tx_k, step_x, 0), step_z, 1)
            tz_k = xor_upper(xor_sum(tz_k, step_x, 0), step_z, 1)

    def apply_level(field, terms):
        diag_k, up_x, down_x, both_y, up_z, down_z, step_x, step_z = terms
        return (
            diag_k * field
            - up_x * roll(field, -step_x, 0)
            - down_x * roll(field, step_x, 0)
            - both_y * roll(field, 64, 1)
            - up_z * roll(field, -step_z, 1)
            - down_z * roll(field, step_z, 1)
        )

    lane_row = iota((128, 128), 0)
    lane_col = iota((128, 128), 1)
    real = lane_col < 64
    same_place = ((lane_row >> 6) == ((lane_col >> 3) & 1)) & (
        ((lane_row & 63) >> 3) == (lane_col & 7)
    )
    pick_one = (real & same_place & ((lane_row & 7) == 0)).astype(F32).astype(BF16)
    pick_two = (real & same_place & ((lane_row & 3) == 0)).astype(F32).astype(BF16)
    own_x = (member >> 2) == (lane_c >> 4)
    diag_k, up_x, down_x, both_y, up_z, down_z, _, _ = levels[2]
    picked = times_ones(
        jnp.concatenate(
            [1.0 / diag_k, up_x, down_x, both_y, up_z, down_z], axis=0
        ),
        pick_one,
    )
    one_member = own_x & ((member & 3) == 0)
    inverse_diag, up_x, down_x, both_y, up_z, down_z = [
        jnp.sum(
            jnp.where(one_member, picked[GROUP * place : GROUP * place + GROUP], 0.0),
            axis=0,
            keepdims=True,
        )
        for place in range(6)
    ]
    gap = lane_row - lane_col
    upper_y = (lane_col >> 3) & 1
    coupling = jnp.where(gap == 16, up_x, 0.0)
    coupling = jnp.where(gap == -16, down_x, coupling)
    coupling = jnp.where(gap == 8 - 16 * upper_y, both_y, coupling)
    coupling = jnp.where(gap == 1, up_z, coupling)
    coupling = jnp.where(gap == -1, down_z, coupling)
    power = coupling * inverse_diag
    total = power + jnp.where(gap == 0, 1.0, 0.0)
    for _ in range(DOUBLINGS):
        power = jnp.dot(power, power, precision=HIGHEST, preferred_element_type=F32)
        total = total + jnp.dot(
            total, power, precision=HIGHEST, preferred_element_type=F32
        )
    spread = jnp.concatenate(
        [
            ((lane_row >> 4) == part)
            & ((lane_row >> 3 & 1) == (lane_col >> 6))
            & ((lane_row & 7) == ((lane_col & 63) >> 3))
            & (lane_row < 64)
            for part in range(4)
        ],
        axis=1,
    )
    solver = times_ones(total, spread.astype(F32).astype(BF16))

    wait_faces(1)
    high_x, low_x, high_y, low_y = halos(1)
    resid = resid_edges(resid, high_x, low_x, high_y, low_y)
    resid_two[...] = resid
    for side, part in enumerate((slice(4, 8), slice(0, 4))):
        to_side(side, resid_two.at[:, part], side_x.at[side, 4], more_sem.at[0], more_sem.at[1])
        to_side(side, late_send_x, late_x.at[side], more_sem.at[0], more_sem.at[1])
        to_side(2 + side, resid_two, side_y.at[side, 4], more_sem.at[0], more_sem.at[1])
        to_side(2 + side, late_send_y, late_y.at[side], more_sem.at[0], more_sem.at[1])

    wait_bytes(gres.at[1:], gres_sem.at[1])
    wait_bytes(beside, beside_sem.at[1])
    only_if(group_before, lambda: wait_bytes(edge_in.at[0, 0], edge_sem.at[1, 0]))
    only_if(group_after, lambda: wait_bytes(edge_in.at[1, 0], edge_sem.at[1, 1]))
    every = gres[:, 0, :]
    first_a, first_b, from_low, from_high = [
        every[:, 128 * part : 128 * part + 128] for part in range(4)
    ]
    from_low = jnp.where(member == 0, edge_in[0, 0], roll(from_low, 1, 0))
    from_high = jnp.where(member == GROUP - 1, edge_in[1, 0], roll(from_high, -1, 0))
    below, above = beside[0, :, 0, :], beside[1, :, 0, :]
    res_a = first_a + from_low + jnp.where(lane_c < 64, below, roll(above, 64, 1))
    res_b = first_b + from_high + jnp.where(lane_c < 64, roll(below, 64, 1), above)

    def descend_one(res_a, res_b):
        cor_a, cor_b = weight_a * res_a, weight_b * res_b
        out_a, out_b = apply_one(cor_a, cor_b)
        cor_a = cor_a + weight_a * (res_a - out_a)
        cor_b = cor_b + weight_b * (res_b - out_b)
        out_a, out_b = apply_one(cor_a, cor_b)
        return cor_a, cor_b, (res_a - out_a) + (res_b - out_b)

    cor_a, cor_b, left = descend_one(res_a, res_b)
    res_k = xor_sum(left, 1, 1)
    cor_k = jnp.zeros(shape, F32)
    for level in (2, 3):
        terms = levels[level - 2]
        weight = OMEGA / terms[0]
        cor = weight * res_k
        cor = cor + weight * (res_k - apply_level(cor, terms))
        left = res_k - apply_level(cor, terms)
        cor_k = cor_k + cor
        if level == 2:
            res_k = xor_sum(xor_sum(left, 1, 0), 2, 1)
    last = times_ones(left, pick_two)
    last = jnp.sum(
        jnp.where(own_x & ((member & 1) == 0), last, 0.0), axis=0, keepdims=True
    )
    last = jnp.broadcast_to(last * inverse_diag, (8, 128))
    solved = jnp.dot(last, solver, precision=HIGHEST, preferred_element_type=F32)
    solved = [jnp.broadcast_to(solved[0:1, 128 * part : 128 * part + 128], (8, 128)) for part in range(4)]
    upper_rows = (iota((8, 128), 0) & 4) != 0
    cor_k = cor_k + jnp.concatenate(
        [
            jnp.where(upper_rows, solved[1], solved[0]),
            jnp.where(upper_rows, solved[3], solved[2]),
        ],
        axis=0,
    )
    tail[0] = cor_a + cor_k
    tail[1] = cor_b + cor_k
    tail_send[0] = tail[0, pl.ds(rank, 1), :]
    tail_send[1] = tail[1, pl.ds(rank, 1), :]
    def tails_to(slot, kind, other_x):
        for step, other_y in enumerate((index_y, next_y[1], prev_y[1])):
            send(
                tail_send,
                tail_in.at[slot + step],
                tail_sem.at[0, kind],
                tail_sem.at[1, kind],
                (other_x, other_y),
            )

    only_if(has_next, lambda: tails_to(0, 0, next_x[0]))
    only_if(has_prev, lambda: tails_to(3, 1, prev_x[0]))
    for side in range(2):
        send(tail_send, tail_in.at[6 + side], tail_sem.at[0, 2], tail_sem.at[1, 2], sides[2 + side])

    def wait_bulk(sem, tiles_x, tiles_y):
        wait_sides(
            (sizes.at[0:tiles_x], sizes.at[0:tiles_x]), sizes.at[0 : 2 * tiles_y], sem
        )

    wait_bulk(agg_sem.at[1], 32, 64)
    wait_bulk(more_sem.at[1], 10, 18)

    def both_x(place):
        return jnp.concatenate([side_x[0, place], side_x[1, place]], axis=1)

    def both_y(low, high):
        shape = low.shape
        low, high = low.reshape(-1, 8, 128), high.reshape(-1, 8, 128)
        return roll(jnp.where(iota(low.shape, 1) < 4, high, low), 4, 1).reshape(shape)

    diag_x, y_x, z_x, resid_x = [both_x(place) for place in (0, 2, 3, 4)]
    diag_y, x_y, y_y, z_y, resid_y = [
        both_y(side_y[0, place], side_y[1, place]) for place in range(5)
    ]
    rows_x = [
        jnp.broadcast_to(late_x[side], (2 * SIZE, 8, 128)).reshape(FIELD) for side in range(2)
    ]
    rows_x = jnp.concatenate([rows_x[0][:, 4:], rows_x[1][:, :4]], axis=1)
    y_x = y_x + jnp.where(second == 0, rows_x, 0.0)
    y_y = y_y + row_roll(coef[7], -3)
    first_x = both_y(late_y[0], late_y[1])
    kinds_x = jnp.concatenate([side_x[0, 1, 0, 1], side_x[1, 1, 0, 1]], axis=1)
    lower = iota((1, 128), 1) < 64

    def swap_halves(line):
        return roll(line, 64, 1)

    kinds_y = jnp.concatenate(
        [
            swap_halves(
                jnp.where(
                    iota((8, 128), 1) < 64,
                    side_y[1, 1, 0, 4 * part + 1],
                    side_y[0, 1, 0, 4 * part + 1],
                )
            )
            for part in range(2)
        ],
        axis=1,
    )

    own = [tail_send[part] for part in range(2)]
    wait_sides((tail_in.at[0:3], tail_in.at[3:6]), tail_in.at[6:8], tail_sem.at[1])
    low_mid, low_from_low, low_from_high = [tail_in[place, 1] for place in (0, 1, 2)]
    low_far = tail_in[0, 0]
    high_mid, high_from_low, high_from_high = [tail_in[place, 0] for place in (3, 4, 5)]
    high_far = tail_in[3, 1]
    below = [tail_in[6, part] for part in range(2)]
    above = [tail_in[7, part] for part in range(2)]

    def y_lines(mid, from_low, from_high):
        return (
            swap_halves(jnp.where(lower, from_high, mid)),
            swap_halves(jnp.where(lower, mid, from_low)),
        )

    def spread_lines(lines):
        return turned(
            jnp.concatenate(
                [jnp.broadcast_to(line, (8, 128))[None] for line in lines], axis=0
            )
        )

    def minus_coarse(resid, diag_f, x_low, x_high, y_f, z_f, mid, x_lines, y_pair):
        up, down = y_pair
        tiles = spread_lines(
            [mid, x_lines[0], x_lines[1], up, down, roll(mid, 1, 1), roll(mid, -1, 1)]
        )
        value = tiles[0]
        across_y = value - jnp.where((iota((8, 128), 0) & 3) == 3, tiles[3], tiles[4])
        across_z = jnp.concatenate(
            [(value - tiles[5])[None, None], (value - tiles[6])[None, None]], axis=0
        )
        resid = resid - diag_f * value - y_f * across_y - z_f * across_z
        first_layer = resid[:, 0:1] - (x_low * (value - tiles[1]))[:, None]
        last_layer = resid[:, 3:4] - (x_high * (value - tiles[2]))[:, None]
        return jnp.concatenate([first_layer, resid[:, 1:3], last_layer], axis=1), value

    def two_rows(resid, fields, x_faces, mids, x_lines, y_pairs):
        parts = [
            minus_coarse(
                resid[:, 4 * part : 4 * part + 4],
                fields[0][:, 4 * part : 4 * part + 4],
                x_faces[part][0],
                x_faces[part][1],
                fields[1][:, 4 * part : 4 * part + 4],
                fields[2][:, 4 * part : 4 * part + 4],
                mids[part],
                x_lines[part],
                y_pairs[part],
            )
            for part in range(2)
        ]
        return jnp.concatenate([parts[0][0], parts[1][0]], axis=1), [part[1] for part in parts]

    resid, own_tiles = two_rows(
        resid,
        (agg[0], agg[2] + coef[8], agg[3]),
        ((coef[2, :, 0], tx_at[0]), (tx_at[0], tx_at[1])),
        own,
        ((low_mid, own[1]), (own[0], high_mid)),
        [y_lines(own[part], below[part], above[part]) for part in range(2)],
    )
    resid_x, tiles_x = two_rows(
        resid_x,
        (diag_x, y_x, z_x),
        ((side_x[0, 1, :, 0], side_x[0, 1, :, 3]), (tx_at[1], side_x[1, 1, :, 3])),
        (low_mid, high_mid),
        ((low_far, own[0]), (own[1], high_far)),
        (
            y_lines(low_mid, low_from_low, low_from_high),
            y_lines(high_mid, high_from_low, high_from_high),
        ),
    )

    def beside_y(low, high):
        return swap_halves(jnp.where(lower, high, low))

    mids_y = [beside_y(below[part], above[part]) for part in range(2)]
    resid_y, tiles_y = two_rows(
        resid_y,
        (diag_y, y_y, z_y),
        ((first_x, x_y[:, 3]), (x_y[:, 4], x_y[:, 7])),
        mids_y,
        (
            (beside_y(low_from_low, low_from_high), mids_y[1]),
            (mids_y[0], beside_y(high_from_low, high_from_high)),
        ),
        [
            (
                jnp.where(lower, own[part], above[part]),
                jnp.where(lower, below[part], own[part]),
            )
            for part in range(2)
        ],
    )

    def over_layers(tiles):
        tiles = jnp.concatenate([tiles[place // 4][None] for place in range(SIZE)], axis=0)
        return jnp.broadcast_to(tiles[None], FIELD)

    iterate = iterate + over_layers(own_tiles) + smooth(resid)
    outer_x = products(resid_x, blocks_x, 32, kinds_x)
    low_x = low_x + tiles_x[0][None] + turned(outer_x[16:32, :128].reshape(2, 8, 128))
    high_x = high_x + tiles_x[1][None] + turned(outer_x[0:16, 128:].reshape(2, 8, 128))
    outer_y = jnp.where(second < 4, low_y, high_y) + over_layers(tiles_y)
    outer_y = outer_y + smooth(resid_y, blocks_y, kinds_y)
    resid = resid_edges(resid_base(iterate), high_x, low_x, outer_y, outer_y)
    iterate = iterate + smooth(resid)

    send_faces(2, iterate)
    out_buf[0] = iterate
    stores = [
        pltpu.make_async_copy(out_buf.at[place], both_any.at[place], store_sem.at[place])
        for place in range(2)
    ]
    stores[0].start()
    resid = resid_base(iterate)
    wait_faces(2)
    out_buf[1] = resid_edges(resid, *halos(2))
    stores[1].start()
    only_if(has_next, lambda: wait_bytes(face_x.at[:, 0], face_send_sem.at[0]))
    only_if(has_prev, lambda: wait_bytes(face_x.at[:, 1], face_send_sem.at[1]))
    wait_bytes(face_y, face_send_sem.at[2])
    only_if(has_next, lambda: wait_bytes(ends_send.at[0, 0], ends_sem.at[0, 0]))
    wait_bytes(ends_send.at[0, 1], ends_sem.at[0, 2])
    wait_bytes(gop.at[1:], gop_sem.at[0])
    wait_bytes(gres.at[1:], gres_sem.at[0])
    wait_bytes(beside, beside_sem.at[0])
    only_if(last_member, lambda: wait_bytes(edge_in.at[0], edge_sem.at[0, 0]))
    only_if(first_member, lambda: wait_bytes(edge_in.at[1], edge_sem.at[0, 1]))
    only_if(has_next, lambda: wait_bytes(tail_in.at[0:3], tail_sem.at[0, 0]))
    only_if(has_prev, lambda: wait_bytes(tail_in.at[3:6], tail_sem.at[0, 1]))
    wait_bytes(tail_in.at[6:8], tail_sem.at[0, 2])
    for sem, tiles_x, tiles_y in ((agg_sem.at[0], 32, 64), (more_sem.at[0], 10, 18)):
        only_if(has_next, lambda: wait_bytes(sizes.at[0:tiles_x], sem.at[0]))
        only_if(has_prev, lambda: wait_bytes(sizes.at[0:tiles_x], sem.at[1]))
        wait_bytes(sizes.at[0 : 2 * tiles_y], sem.at[2])
    for store in stores:
        store.wait()


def to_outer_order(both, pressure, resid):
    row = iota((DEPTH, DEPTH), 0)
    col = iota((DEPTH, DEPTH), 1)
    to_outside = (col == 4 * (row & 63) + (row >> 6)).astype(F32).astype(BF16)
    for place, out in enumerate((pressure, resid)):
        out[...] = times_ones(flat(both[place]), to_outside).reshape(SIZE, SIZE, DEPTH)


def on_device(
    count_x,
    count_y,
    pressure_rhs,
    accumulation,
    trans_x,
    trans_y,
    trans_z,
    well_cells,
    well_flags,
    well_rates,
    well_index,
    block_map,
    block_inverses,
):
    anywhere = pl.BlockSpec(memory_space=pl.ANY)
    dma = pltpu.SemaphoreType.DMA
    out = jax.ShapeDtypeStruct(pressure_rhs.shape, F32)
    both = pl.pallas_call(
        functools.partial(kernel, count_x, count_y),
        out_shape=jax.ShapeDtypeStruct((2,) + FIELD, F32),
        in_specs=[anywhere] * 11,
        out_specs=anywhere,
        scratch_shapes=[
            pltpu.VMEM((5, SIZE, SIZE, DEPTH), F32),
            pltpu.VMEM((2, 2, 64), jnp.int32),
            pltpu.SMEM((WELLS,), jnp.int32),
            pltpu.SMEM((WELLS,), jnp.int32),
            pltpu.SMEM((WELLS,), F32),
            pltpu.SMEM((WELLS,), F32),
            pltpu.VMEM((KINDS * 64, 64), F32),
            pltpu.VMEM((KINDS * 64, DEPTH), BF16),
            pltpu.VMEM(FIELD, F32),
            pltpu.VMEM((9,) + FIELD, F32),
            pltpu.VMEM((3, 2, 2, SIZE, 128), F32),
            pltpu.VMEM((3, 2, 2 * SIZE, 1, 128), F32),
            pltpu.VMEM((3, 2, 2, SIZE, 128), F32),
            pltpu.VMEM((3, 2, 2 * SIZE, 1, 128), F32),
            pltpu.VMEM((1, 2, SIZE, DEPTH), F32),
            pltpu.VMEM((1, 2, SIZE, DEPTH), F32),
            pltpu.VMEM((8, 128), F32),
            pltpu.VMEM((GROUP, 8, 128), F32),
            pltpu.VMEM((1, 512), F32),
            pltpu.VMEM((GROUP, 1, 512), F32),
            pltpu.VMEM((2, 1, 128), F32),
            pltpu.VMEM((2, GROUP, 1, 128), F32),
            pltpu.VMEM((2, 1, 128), F32),
            pltpu.VMEM((2, GROUP, 1, 128), F32),
            pltpu.VMEM((2, GROUP, 128), F32),
            pltpu.VMEM((2, 1, 128), F32),
            pltpu.VMEM((8, 2, 1, 128), F32),
            pltpu.VMEM((2,) + FIELD, F32),
            pltpu.VMEM((4,) + FIELD, F32),
            pltpu.VMEM(FIELD, F32),
            pltpu.VMEM((2, 5, 2, 4, 8, 128), F32),
            pltpu.VMEM((2, 5) + FIELD, F32),
            pltpu.VMEM((2 * SIZE, 1, 128), F32),
            pltpu.VMEM((2, SIZE, 128), F32),
            pltpu.VMEM((2, 2 * SIZE, 1, 128), F32),
            pltpu.VMEM((2, 2, SIZE, 128), F32),
            pltpu.VMEM((KINDS * 32, DEPTH), BF16),
            pltpu.VMEM((KINDS * 64, DEPTH), BF16),
            pltpu.VMEM((128, 8, 128), F32),
            dma((11,)),
            dma((2,)),
            dma((3,)),
            dma((3, 3)),
            dma((2, 3)),
            dma((2,)),
            dma((2,)),
            dma((2,)),
            dma((2, 2)),
            dma((2, 3)),
            dma((2, 3)),
            dma((2, 3)),
        ],
        compiler_params=pltpu.CompilerParams(
            collective_id=0, has_side_effects=True, vmem_limit_bytes=60 * 1024 * 1024
        ),
    )(
        pressure_rhs,
        accumulation,
        trans_x,
        trans_y,
        trans_z,
        well_cells,
        well_flags,
        well_rates,
        well_index,
        block_map,
        block_inverses.reshape(KINDS * 64, 64),
    )
    return pl.pallas_call(to_outer_order, out_shape=(out, out))(both)


def solution(mesh):
    cells = P("gx", "gy", None)
    wells = P(("gx", "gy"))
    return jax.shard_map(
        functools.partial(on_device, mesh.shape["gx"], mesh.shape["gy"]),
        mesh=mesh,
        in_specs=(cells,) * 5 + (wells,) * 4 + (cells, P()),
        out_specs=(cells, cells),
        check_vma=False,
    )
```

```python
import functools

import jax
import jax.numpy as jnp
from jax import lax
from jax.experimental import pallas as pl
from jax.experimental.pallas import tpu as pltpu
from jax.sharding import PartitionSpec as P

OMEGA = 0.8
GROUP = 16
SIZE = 8
DEPTH = 256
KINDS = 16
WELLS = 4
DOUBLINGS = 10
LATE_DOUBLINGS = 5
MESH = pl.DeviceIdType.MESH
HIGHEST = lax.Precision.HIGHEST
F32 = jnp.float32
BF16 = jnp.bfloat16
FIELD = (2, SIZE, SIZE, 128)


def iota(shape, dim):
    return lax.broadcasted_iota(jnp.int32, shape, dim)


def roll(values, shift, axis):
    return pltpu.roll(values, shift % values.shape[axis], axis)


def split_three(values):
    high = values.astype(BF16)
    rest = values - high.astype(F32)
    middle = rest.astype(BF16)
    low = (rest - middle.astype(F32)).astype(BF16)
    return high, middle, low


def split_two(values):
    high = values.astype(BF16)
    low = (values - high.astype(F32)).astype(BF16)
    return high, low


def times_ones(values, ones):
    return sum(jnp.dot(part, ones, preferred_element_type=F32) for part in split_three(values))


def flat(field):
    return jnp.concatenate(
        [field[0].reshape(SIZE * SIZE, 128), field[1].reshape(SIZE * SIZE, 128)], axis=1
    )


def unflat(rows):
    shape = (1, SIZE, SIZE, 128)
    return jnp.concatenate(
        [rows[:, :128].reshape(shape), rows[:, 128:].reshape(shape)], axis=0
    )


def lane_roll(field, shift):
    return roll(field.reshape(-1, 8, 128), shift, 2).reshape(field.shape)


def row_roll(field, shift):
    return roll(field.reshape(-1, 8, 128), shift, 1).reshape(field.shape)


def z_neighbours(field):
    low, high = field[0], field[1]
    lower_lanes = iota(low.shape, 2) < 64
    across = lane_roll(jnp.where(lower_lanes, high, low), 64)
    up = [across, jnp.where(lower_lanes, lane_roll(high, 64), lane_roll(low, 63))]
    down = [jnp.where(lower_lanes, lane_roll(high, 65), lane_roll(low, 64)), across]
    return (
        jnp.concatenate([part[None] for part in up], axis=0),
        jnp.concatenate([part[None] for part in down], axis=0),
    )


def turned(field):
    shape = (field.size // 1024, 8, 128)
    same = (iota(shape, 1) >= 4) == (iota(shape, 2) >= 64)
    tiles = field.reshape(shape)
    return jnp.where(same, tiles, roll(roll(tiles, 4, 1), 64, 2)).reshape(field.shape)


def agg_rows(tile):
    tile = tile + roll(tile, 64, 1)
    tile = tile + roll(tile, -1, 0)
    tile = tile + roll(tile, -2, 0)
    return jnp.where(iota((1, 128), 1) < 64, tile[0:1], tile[4:5])


def xor_sum(values, step, axis):
    place = iota(values.shape, axis)
    return values + jnp.where(
        (place & step) == 0, roll(values, -step, axis), roll(values, step, axis)
    )


def xor_upper(values, step, axis):
    place = iota(values.shape, axis)
    return jnp.where((place & step) == 0, roll(values, -step, axis), values)


def only_if(condition, action):
    if condition is None:
        action()
    else:
        pl.when(condition)(action)


def send(src, dst, send_sem, recv_sem, device):
    pltpu.make_async_remote_copy(
        src_ref=src,
        dst_ref=dst,
        send_sem=send_sem,
        recv_sem=recv_sem,
        device_id=device,
        device_id_type=MESH,
    ).start()


def wait_bytes(like, sem):
    pltpu.make_async_copy(like, like, sem).wait()


def kernel(
    count_x,
    count_y,
    rhs_any,
    acc_any,
    tx_any,
    ty_any,
    tz_any,
    cells_any,
    flags_any,
    rates_any,
    index_any,
    map_any,
    inv_any,
    both_any,
    fields_in,
    map_in,
    cells,
    flags,
    rates,
    well_index,
    inv_in,
    blocks,
    source,
    coef,
    face_x,
    face_y,
    halo_x,
    halo_y,
    ends_in,
    ends_send,
    gop_send,
    gop,
    gres_send,
    gres,
    beside_send,
    beside,
    edge_send,
    edge_in,
    tail,
    tail_send,
    tail_in,
    out_buf,
    agg,
    resid_two,
    side_x,
    side_y,
    late_send_x,
    late_send_y,
    late_x,
    late_y,
    blocks_x,
    blocks_y,
    sizes,
    load_sem,
    store_sem,
    face_send_sem,
    face_recv_sem,
    ends_sem,
    gop_sem,
    gres_sem,
    beside_sem,
    edge_sem,
    tail_sem,
    agg_sem,
    more_sem,
    near_sem,
    end_sem,
):
    index_x = lax.axis_index("gx")
    index_y = lax.axis_index("gy")
    rank = lax.rem(index_x, GROUP)
    base = index_x - rank
    next_x = (lax.rem(index_x + 1, count_x), index_y)
    prev_x = (lax.rem(index_x + count_x - 1, count_x), index_y)
    next_y = (index_x, lax.rem(index_y + 1, count_y))
    prev_y = (index_x, lax.rem(index_y + count_y - 1, count_y))
    sides = (next_x, prev_x, next_y, prev_y)
    steps = sorted(range(GROUP), key=lambda step: -min(step % 8, -step % 8))
    members = [base + lax.rem(rank + step, GROUP) for step in steps]
    mates = [(member, index_y) for step, member in zip(steps, members) if step > 0]
    upper_group = [(member, next_y[1]) for member in members]
    lower_group = [(member, prev_y[1]) for member in members]
    has_next = index_x < count_x - 1
    has_prev = index_x > 0
    group_after = base + GROUP < count_x
    group_before = base > 0
    last_member = group_after & (rank == GROUP - 1)
    first_member = group_before & (rank == 0)
    send_if = (has_next, has_prev, None, None)

    loads = [
        pltpu.make_async_copy(src, dst, load_sem.at[place])
        for place, (src, dst) in enumerate(
            (
                (inv_any, inv_in),
                (rhs_any, fields_in.at[0]),
                (tx_any, fields_in.at[1]),
                (ty_any, fields_in.at[2]),
                (tz_any, fields_in.at[3]),
                (acc_any, fields_in.at[4]),
                (map_any, map_in),
                (cells_any, cells),
                (flags_any, flags),
                (rates_any, rates),
                (index_any, well_index),
            )
        )
    ]
    for load in loads:
        load.start()
    halo_x[...] = jnp.zeros_like(halo_x)
    ends_in[...] = jnp.zeros_like(ends_in)
    edge_in[...] = jnp.zeros_like(edge_in)
    tail_in[...] = jnp.zeros_like(tail_in)
    side_x[...] = jnp.zeros_like(side_x)
    late_x[...] = jnp.zeros_like(late_x)

    barrier = pltpu.get_barrier_semaphore()

    def member(step_z, step_y):
        place = lax.rem(rank // 8 + step_y, 2) * 8 + lax.rem(lax.rem(rank, 8) + step_z + 8, 8)
        return base + place

    near = []
    for step_z in (2, -2, 1, -1, 0):
        near.append((member(step_z, 1), index_y))
        near.append((member(step_z, 0), next_y[1]))
        near.append((member(step_z, 0), prev_y[1]))
        if step_z != 0:
            near.append((member(step_z, 0), index_y))

    def announce(semaphore):
        for device in near:
            pl.semaphore_signal(semaphore, inc=1, device_id=device, device_id_type=MESH)
        announce_end(semaphore)

    def announce_end(semaphore):
        for condition, device in ((last_member, next_x), (first_member, prev_x)):
            only_if(
                condition,
                lambda device=device: pl.semaphore_signal(
                    semaphore, inc=1, device_id=device, device_id_type=MESH
                ),
            )

    group_end = last_member.astype(jnp.int32) + first_member.astype(jnp.int32)
    announced = len(near) + group_end
    announce(barrier)

    row = iota((DEPTH, DEPTH), 0)
    col = iota((DEPTH, DEPTH), 1)
    to_inside = (row == 4 * (col & 63) + (col >> 6)).astype(F32).astype(BF16)
    lane = iota(FIELD, 3)
    second = iota(FIELD, 2)
    first = iota(FIELD, 1)
    half = iota(FIELD, 0)
    cell_id = ((half * SIZE + first) * SIZE + second) * 128 + lane

    def swapped_offsets(place):
        return (place & ~15) | ((place & 3) << 2) | ((place >> 2) & 3)

    row_k = iota((128, DEPTH), 0)
    col_k = iota((128, DEPTH), 1)
    take_cols = ((row_k & 63) == swapped_offsets(col_k & 63)) & ((row_k < 64) == (col_k < 128))
    take_cols = take_cols.astype(F32).astype(BF16)
    loads[0].wait()
    tiles = [
        (OMEGA * inv_in[pl.ds(third, KINDS * 16, stride=4), :]).reshape(KINDS * 2, 8, 64)
        for third in range(4)
    ]
    upper_half = iota((KINDS * 2, 8, 64), 1) >= 4
    rows = jnp.concatenate(
        [
            tile[:, None]
            for tile in (
                jnp.where(upper_half, roll(tiles[1], 4, 1), tiles[0]),
                jnp.where(upper_half, roll(tiles[3], 4, 1), tiles[2]),
                jnp.where(upper_half, tiles[1], roll(tiles[0], 4, 1)),
                jnp.where(upper_half, tiles[3], roll(tiles[2], 4, 1)),
            )
        ],
        axis=1,
    ).reshape(KINDS * 64, 64)
    high, low = split_two(rows)
    blocks[...] = jnp.dot(
        jnp.concatenate([high, low], axis=1), take_cols, preferred_element_type=F32
    ).astype(BF16)

    for place in range(7, 11):
        loads[place].wait()
    plane_cells = SIZE * count_y * DEPTH
    well_ids = []
    for well in range(WELLS):
        cell = cells[well]
        pos_x = cell // plane_cells - index_x * SIZE
        left = lax.rem(cell, plane_cells)
        pos_y = left // DEPTH - index_y * SIZE
        pos_z = lax.rem(left, DEPTH)
        place = lax.rem(pos_z, 4) * 64 + pos_z // 4
        well_ids.append(
            ((place // 128 * SIZE + pos_x) * SIZE + pos_y) * 128 + lax.rem(place, 128)
        )
    signed = [
        jnp.where(flags[well] == 1, rates[well], -rates[well]) for well in range(WELLS)
    ]

    loads[1].wait()
    well_source = jnp.zeros(FIELD, F32)
    for well in range(WELLS):
        well_source = well_source + jnp.where(cell_id == well_ids[well], signed[well], 0.0)
    source[...] = (
        unflat(times_ones(fields_in[0].reshape(SIZE * SIZE, DEPTH), to_inside)) + well_source
    )

    loads[6].wait()
    kinds = []
    for part in range(2):
        kind = map_in[part]
        kinds.append(jnp.concatenate([kind[0:1], kind[1:2]], axis=1))
    kind_ids = jnp.broadcast_to(jnp.concatenate(kinds, axis=1), (8, 256))

    def products(field, operators, rows, kind_row):
        tiles = turned(field)
        columns = jnp.concatenate(
            [
                jnp.concatenate(
                    [
                        tiles[half_id, 4 * part + offset]
                        for offset in range(4)
                        for half_id in range(2)
                    ],
                    axis=0,
                )
                for part in range(2)
            ],
            axis=1,
        )
        high, low = split_two(columns)
        product = jnp.dot(
            operators[...],
            jnp.concatenate([high, low, high, low], axis=0),
            preferred_element_type=F32,
        )
        chosen = product[0:rows]
        for kind in range(1, KINDS):
            mask = jnp.broadcast_to((kind_row == kind)[None], (rows // 8, 8, 256))
            chosen = jnp.where(
                mask.reshape(rows, 256), product[rows * kind : rows * kind + rows], chosen
            )
        return chosen

    def smooth(resid, operators=blocks, kind_row=kind_ids):
        chosen = products(resid, operators, 64, kind_row)
        back = [
            [
                chosen[8 * (2 * offset + half_id) : 8 * (2 * offset + half_id) + 8,
                       128 * part : 128 * part + 128][None]
                for part in range(2)
                for offset in range(4)
            ]
            for half_id in range(2)
        ]
        field = jnp.concatenate(
            [jnp.concatenate(tiles, axis=0)[None] for tiles in back], axis=0
        )
        return turned(field)

    def send_faces(step, field):
        face_x[step, 0] = field[:, SIZE - 1]
        face_x[step, 1] = field[:, 0]
        tiles = field.reshape(2 * SIZE, 8, 128)
        face_y[step, 0] = tiles[:, 7:8, :]
        face_y[step, 1] = tiles[:, 0:1, :]
        for side, (out, into) in enumerate(
            ((face_x, halo_x), (face_x, halo_x), (face_y, halo_y), (face_y, halo_y))
        ):
            to_side(
                side,
                out.at[step, side % 2],
                into.at[step, side % 2],
                face_send_sem,
                face_recv_sem.at[step],
            )

    def to_side(side, src, dst, send_sems, recv_sems):
        kind = min(side, 2)
        only_if(
            send_if[side],
            lambda: send(src, dst, send_sems.at[kind], recv_sems.at[kind], sides[side]),
        )

    def wait_sides(buffer_x, buffer_y, sems):
        only_if(has_prev, lambda: wait_bytes(buffer_x[0], sems.at[0]))
        only_if(has_next, lambda: wait_bytes(buffer_x[1], sems.at[1]))
        wait_bytes(buffer_y, sems.at[2])

    def wait_faces(step):
        wait_sides(
            (halo_x.at[step, 0], halo_x.at[step, 1]), halo_y.at[step], face_recv_sem.at[step]
        )

    iterate = smooth(source[...])

    loads[2].wait()
    loads[3].wait()
    ends_send[0, 0] = fields_in[1, SIZE - 1]
    for place in range(SIZE):
        ends_send[0, 1, place : place + 1] = fields_in[2, place, SIZE - 1 : SIZE, :]
    loads[4].wait()
    loads[5].wait()
    inside = times_ones(
        fields_in[1:5].reshape(4 * SIZE * SIZE, DEPTH), to_inside
    )
    tx, ty, tz, acc = [unflat(inside[64 * place : 64 * place + 64]) for place in range(4)]
    well_diag = jnp.zeros(FIELD, F32)
    for well in range(WELLS):
        well_diag = well_diag + jnp.where(cell_id == well_ids[well], well_index[well], 0.0)
    diag = acc + well_diag
    tx = jnp.where((first == SIZE - 1) & (index_x == count_x - 1), 0.0, tx)
    ty = jnp.where((second == SIZE - 1) & (index_y == count_y - 1), 0.0, ty)
    tz = jnp.where((half == 1) & (lane == 127), 0.0, tz)

    for part in range(2):
        mine = slice(4 * part, 4 * part + 4)
        gop_send[part : part + 1] = agg_rows(diag[:, mine].sum(axis=(0, 1)))
        gop_send[2 + part : 3 + part] = agg_rows(tx[:, 4 * part + 3].sum(axis=0))
        tile = ty[:, mine].sum(axis=(0, 1))
        tile = tile + roll(tile, 64, 1)
        gop_send[4 + part : 5 + part] = jnp.where(
            iota((1, 128), 1) < 64, tile[3:4], tile[7:8]
        )
        tile = tz[1, mine].sum(axis=0)
        gop_send[6 + part : 7 + part] = agg_rows(
            jnp.where(iota((8, 128), 1) >= 64, tile, 0.0)
        )

    tz_down = jnp.where((half == 0) & (lane == 0), 0.0, z_neighbours(tz)[1])
    agg[0] = diag
    agg[1] = jnp.zeros(FIELD, F32)
    for place, layer in ((3, 3), (4, 3), (7, 7)):
        agg[1, :, place] = tx[:, layer]
    for part in range(2):
        agg[1, 0, 4 * part + 1] = kind_ids[:, 128 * part : 128 * part + 128].astype(F32)
    agg[2] = jnp.where(
        (second & 3) == 3, ty, jnp.where(second == 4, row_roll(ty, 1), 0.0)
    )
    agg[3] = jnp.where(
        (half == 0) & (lane < 64), tz_down, jnp.where((half == 1) & (lane >= 64), tz, 0.0)
    )

    pl.semaphore_wait(barrier, announced)
    announce(near_sem)
    send_faces(0, iterate)

    for side in range(2):
        to_side(2 * side, ends_send.at[0, side], ends_in.at[0, side], ends_sem.at[0], ends_sem.at[1])

    def to_all(devices, mine, target, sems):
        for device in devices:
            send(mine, target, sems.at[0], sems.at[1], device)

    for side, part in enumerate((slice(4, 8), slice(0, 4))):
        to_side(side, agg.at[:, :, part], side_x.at[side, 0:4], agg_sem.at[0], agg_sem.at[1])
        to_side(2 + side, agg, side_y.at[side, 0:4], agg_sem.at[0], agg_sem.at[1])

    for kind in range(KINDS):
        blocks_x[32 * kind : 32 * kind + 16, :] = blocks[64 * kind : 64 * kind + 16, :]
        blocks_x[32 * kind + 16 : 32 * kind + 32, :] = blocks[64 * kind + 48 : 64 * kind + 64, :]
    mirror = (col == (row ^ 3)).astype(F32).astype(BF16)
    for part in range(KINDS // 4):
        here = slice(part * DEPTH, (part + 1) * DEPTH)
        blocks_y[here, :] = jnp.dot(
            mirror, blocks[here, :], preferred_element_type=F32
        ).astype(BF16)

    pl.semaphore_wait(near_sem, announced)
    announce_end(end_sem)
    to_all(mates, gop_send, gop.at[rank], gop_sem)
    gop[rank] = gop_send[...]

    only_if(has_prev, lambda: wait_bytes(ends_in.at[0, 0], ends_sem.at[1, 0]))
    wait_bytes(ends_in.at[0, 1], ends_sem.at[1, 2])
    end_rows = times_ones(ends_in[0].reshape(2 * SIZE, DEPTH), to_inside)
    end_x = jnp.where(index_x == 0, 0.0, end_rows[0:SIZE])
    end_y = jnp.where(index_y == 0, 0.0, end_rows[SIZE:])
    end_x = jnp.concatenate([end_x[None, None, :, :128], end_x[None, None, :, 128:]], axis=0)
    tx_down = jnp.concatenate([end_x, tx[:, : SIZE - 1]], axis=1)
    for part in range(2):
        for place in range(SIZE):
            late_send_x[SIZE * part + place] = end_y[
                place : place + 1, 128 * part : 128 * part + 128
            ]
    late_send_y[...] = end_x[:, 0]
    end_y = jnp.broadcast_to(late_send_x[...], (2 * SIZE, 8, 128)).reshape(FIELD)
    ty_in = jnp.where(second == SIZE - 1, 0.0, ty)
    ty_down_in = row_roll(ty_in, 1)
    ty_edge = ty - ty_in
    ty_down_edge = jnp.where(second == 0, end_y, 0.0)
    coef[0] = (
        diag + tx + tx_down + ty + ty_down_in + ty_down_edge + tz + tz_down
    )
    coef[1] = tx
    coef[2] = tx_down
    coef[3] = ty_in
    coef[4] = ty_down_in
    coef[5] = tz
    coef[6] = tz_down
    coef[7] = ty_edge
    coef[8] = ty_down_edge
    tx_at = [tx[:, 3], tx[:, 7]]

    def resid_base(field):
        nothing = jnp.zeros((2, 1, SIZE, 128), F32)
        up_z, down_z = z_neighbours(field)
        return (
            source[...]
            - coef[0] * field
            + coef[1] * jnp.concatenate([field[:, 1:], nothing], axis=1)
            + coef[2] * jnp.concatenate([nothing, field[:, : SIZE - 1]], axis=1)
            + coef[3] * row_roll(field, -1)
            + coef[4] * row_roll(field, 1)
            + coef[5] * up_z
            + coef[6] * down_z
        )

    def resid_edges(resid, high_x, low_x, high_y, low_y):
        first_row = resid[:, 0:1] + (coef[2, :, 0] * low_x)[:, None]
        last_row = resid[:, SIZE - 1 :] + (coef[1, :, SIZE - 1] * high_x)[:, None]
        resid = jnp.concatenate([first_row, resid[:, 1 : SIZE - 1], last_row], axis=1)
        return resid + coef[7] * high_y + coef[8] * low_y

    def halos(step):
        spread = [
            jnp.broadcast_to(halo_y[step, side], (2 * SIZE, 8, 128)).reshape(FIELD)
            for side in (1, 0)
        ]
        return halo_x[step, 1], halo_x[step, 0], spread[0], spread[1]

    resid = resid_base(iterate)
    wait_faces(0)
    resid = resid_edges(resid, *halos(0))
    iterate = iterate + smooth(resid)

    send_faces(1, iterate)
    resid = resid_base(iterate)

    for part in range(2):
        mine = slice(4 * part, 4 * part + 4)
        gres_send[:, 128 * part : 128 * part + 128] = agg_rows(resid[:, mine].sum(axis=(0, 1)))
    flux_up = agg_rows((coef[1, :, SIZE - 1] * iterate[:, SIZE - 1]).sum(axis=0))
    flux_down = agg_rows((coef[2, :, 0] * iterate[:, 0]).sum(axis=0))
    gres_send[:, 256:384] = flux_up
    gres_send[:, 384:512] = flux_down
    edge_send[0] = flux_up
    edge_send[1] = flux_down
    for side in range(2):
        flux = coef[7 + side] * iterate
        lines = []
        for part in range(2):
            tile = flux[:, 4 * part : 4 * part + 4].sum(axis=(0, 1))
            tile = tile + roll(tile, 64, 1)
            lines.append(tile[7:8] if side == 0 else tile[0:1])
        beside_send[side] = jnp.where(iota((1, 128), 1) < 64, lines[0], lines[1])
    to_all(mates, gres_send, gres.at[rank], gres_sem)
    to_all(upper_group, beside_send.at[0], beside.at[0, rank], beside_sem)
    to_all(lower_group, beside_send.at[1], beside.at[1, rank], beside_sem)

    def to_edge(side, target):
        for step in range(GROUP):
            send(
                edge_send.at[side],
                edge_in.at[side, 0],
                edge_sem.at[0, side],
                edge_sem.at[1, side],
                (target + step, index_y),
            )

    only_if(last_member | first_member, lambda: pl.semaphore_wait(end_sem, 1))
    only_if(last_member, lambda: to_edge(0, base + GROUP))
    only_if(first_member, lambda: to_edge(1, base - GROUP))
    gres[rank] = gres_send[...]

    wait_bytes(gop.at[1:], gop_sem.at[1])
    shape = (GROUP, 128)
    member = iota(shape, 0)
    lane_c = iota(shape, 1)
    deep = lane_c & 63
    base_a, base_b, tx_a, tx_b, ty_a, ty_b, tz_a, tz_b = [
        gop[:, place, :] for place in range(8)
    ]

    def y_terms(values):
        return jnp.where(lane_c < 64, values, roll(values, 64, 1))

    def z_terms(values, step):
        up = jnp.where(deep < 64 - step, values, 0.0)
        down = jnp.where(deep >= step, roll(values, step, 1), 0.0)
        return up, down

    across_up = jnp.where((member & 1) == 0, tx_b, 0.0)
    across_down = jnp.where((member & 1) == 1, roll(tx_b, 1, 0), 0.0)
    y_a, y_b = y_terms(ty_a), y_terms(ty_b)
    (zu_a, zd_a), (zu_b, zd_b) = z_terms(tz_a, 1), z_terms(tz_b, 1)
    diag_a = base_a + tx_a + across_down + y_a + zu_a + zd_a
    diag_b = base_b + tx_a + across_up + y_b + zu_b + zd_b
    weight_a, weight_b = OMEGA / diag_a, OMEGA / diag_b

    def apply_one(field_a, field_b):
        out_a = (
            diag_a * field_a
            - tx_a * field_b
            - across_down * roll(field_b, 1, 0)
            - y_a * roll(field_a, 64, 1)
            - zu_a * roll(field_a, -1, 1)
            - zd_a * roll(field_a, 1, 1)
        )
        out_b = (
            diag_b * field_b
            - tx_a * field_a
            - across_up * roll(field_a, -1, 0)
            - y_b * roll(field_b, 64, 1)
            - zu_b * roll(field_b, -1, 1)
            - zd_b * roll(field_b, 1, 1)
        )
        return out_a, out_b

    levels = []
    base_k = xor_sum(base_a + base_b, 1, 1)
    tx_k = xor_sum(tx_b, 1, 1)
    ty_k = xor_sum(ty_a + ty_b, 1, 1)
    tz_k = xor_upper(tz_a + tz_b, 1, 1)
    for level in range(2, 5):
        step_x, step_z = 1 << (level - 2), 1 << (level - 1)
        cell_x = member >> (level - 2)
        up_x = jnp.where((cell_x & 3) != 3, tx_k, 0.0)
        down_x = jnp.where((cell_x & 3) != 0, roll(tx_k, step_x, 0), 0.0)
        both_y = y_terms(ty_k)
        up_z, down_z = z_terms(tz_k, step_z)
        diag_k = base_k + up_x + down_x + both_y + up_z + down_z
        levels.append((diag_k, up_x, down_x, both_y, up_z, down_z, step_x, step_z))
        if level < 4:
            base_k = xor_sum(xor_sum(base_k, step_x, 0), step_z, 1)
            ty_k = xor_sum(xor_sum(ty_k, step_x, 0), step_z, 1)
            tx_k = xor_sum(xor_upper(tx_k, step_x, 0), step_z, 1)
            tz_k = xor_upper(xor_sum(tz_k, step_x, 0), step_z, 1)

    def apply_level(field, terms):
        diag_k, up_x, down_x, both_y, up_z, down_z, step_x, step_z = terms
        return (
            diag_k * field
            - up_x * roll(field, -step_x, 0)
            - down_x * roll(field, step_x, 0)
            - both_y * roll(field, 64, 1)
            - up_z * roll(field, -step_z, 1)
            - down_z * roll(field, step_z, 1)
        )

    lane_row = iota((128, 128), 0)
    lane_col = iota((128, 128), 1)
    real = lane_col < 64
    same_place = ((lane_row >> 6) == ((lane_col >> 3) & 1)) & (
        ((lane_row & 63) >> 3) == (lane_col & 7)
    )
    pick_one = (real & same_place & ((lane_row & 7) == 0)).astype(F32).astype(BF16)
    pick_two = (real & same_place & ((lane_row & 3) == 0)).astype(F32).astype(BF16)
    own_x = (member >> 2) == (lane_c >> 4)
    diag_k, up_x, down_x, both_y, up_z, down_z, _, _ = levels[2]
    picked = times_ones(
        jnp.concatenate(
            [1.0 / diag_k, up_x, down_x, both_y, up_z, down_z], axis=0
        ),
        pick_one,
    )
    one_member = own_x & ((member & 3) == 0)
    inverse_diag, up_x, down_x, both_y, up_z, down_z = [
        jnp.sum(
            jnp.where(one_member, picked[GROUP * place : GROUP * place + GROUP], 0.0),
            axis=0,
            keepdims=True,
        )
        for place in range(6)
    ]
    gap = lane_row - lane_col
    upper_y = (lane_col >> 3) & 1
    coupling = jnp.where(gap == 16, up_x, 0.0)
    coupling = jnp.where(gap == -16, down_x, coupling)
    coupling = jnp.where(gap == 8 - 16 * upper_y, both_y, coupling)
    coupling = jnp.where(gap == 1, up_z, coupling)
    coupling = jnp.where(gap == -1, down_z, coupling)
    power = coupling * inverse_diag
    total = jnp.where(gap == 0, 1.0, 0.0)

    def doubled(total, power):
        both = jnp.dot(
            jnp.concatenate([total, power], axis=0),
            power,
            precision=HIGHEST,
            preferred_element_type=F32,
        )
        return total + both[:128], both[128:]

    for _ in range(DOUBLINGS - LATE_DOUBLINGS):
        total, power = doubled(total, power)
    spread = jnp.concatenate(
        [
            ((lane_row >> 4) == part)
            & ((lane_row >> 3 & 1) == (lane_col >> 6))
            & ((lane_row & 7) == ((lane_col & 63) >> 3))
            & (lane_row < 64)
            for part in range(4)
        ],
        axis=1,
    )

    wait_faces(1)
    high_x, low_x, high_y, low_y = halos(1)
    resid = resid_edges(resid, high_x, low_x, high_y, low_y)
    resid_two[...] = resid
    for side, part in enumerate((slice(4, 8), slice(0, 4))):
        to_side(side, resid_two.at[:, part], side_x.at[side, 4], more_sem.at[0], more_sem.at[1])
        to_side(side, late_send_x, late_x.at[side], more_sem.at[0], more_sem.at[1])
        to_side(2 + side, resid_two, side_y.at[side, 4], more_sem.at[0], more_sem.at[1])
        to_side(2 + side, late_send_y, late_y.at[side], more_sem.at[0], more_sem.at[1])

    wait_bytes(gres.at[1:], gres_sem.at[1])
    wait_bytes(beside, beside_sem.at[1])
    only_if(group_before, lambda: wait_bytes(edge_in.at[0, 0], edge_sem.at[1, 0]))
    only_if(group_after, lambda: wait_bytes(edge_in.at[1, 0], edge_sem.at[1, 1]))
    every = gres[:, 0, :]
    first_a, first_b, from_low, from_high = [
        every[:, 128 * part : 128 * part + 128] for part in range(4)
    ]
    from_low = jnp.where(member == 0, edge_in[0, 0], roll(from_low, 1, 0))
    from_high = jnp.where(member == GROUP - 1, edge_in[1, 0], roll(from_high, -1, 0))
    below, above = beside[0, :, 0, :], beside[1, :, 0, :]
    res_a = first_a + from_low + jnp.where(lane_c < 64, below, roll(above, 64, 1))
    res_b = first_b + from_high + jnp.where(lane_c < 64, roll(below, 64, 1), above)

    for _ in range(LATE_DOUBLINGS):
        total, power = doubled(total, power)
    solver = times_ones(total, spread.astype(F32).astype(BF16))

    def descend_one(res_a, res_b):
        cor_a, cor_b = weight_a * res_a, weight_b * res_b
        out_a, out_b = apply_one(cor_a, cor_b)
        cor_a = cor_a + weight_a * (res_a - out_a)
        cor_b = cor_b + weight_b * (res_b - out_b)
        out_a, out_b = apply_one(cor_a, cor_b)
        return cor_a, cor_b, (res_a - out_a) + (res_b - out_b)

    cor_a, cor_b, left = descend_one(res_a, res_b)
    res_k = xor_sum(left, 1, 1)
    cor_k = jnp.zeros(shape, F32)
    for level in (2, 3):
        terms = levels[level - 2]
        weight = OMEGA / terms[0]
        cor = weight * res_k
        cor = cor + weight * (res_k - apply_level(cor, terms))
        left = res_k - apply_level(cor, terms)
        cor_k = cor_k + cor
        if level == 2:
            res_k = xor_sum(xor_sum(left, 1, 0), 2, 1)
    last = times_ones(left, pick_two)
    last = jnp.sum(
        jnp.where(own_x & ((member & 1) == 0), last, 0.0), axis=0, keepdims=True
    )
    last = jnp.broadcast_to(last * inverse_diag, (8, 128))
    solved = jnp.dot(last, solver, precision=HIGHEST, preferred_element_type=F32)
    solved = [jnp.broadcast_to(solved[0:1, 128 * part : 128 * part + 128], (8, 128)) for part in range(4)]
    upper_rows = (iota((8, 128), 0) & 4) != 0
    cor_k = cor_k + jnp.concatenate(
        [
            jnp.where(upper_rows, solved[1], solved[0]),
            jnp.where(upper_rows, solved[3], solved[2]),
        ],
        axis=0,
    )
    tail[0] = cor_a + cor_k
    tail[1] = cor_b + cor_k
    tail_send[0] = tail[0, pl.ds(rank, 1), :]
    tail_send[1] = tail[1, pl.ds(rank, 1), :]
    def tails_to(slot, kind, other_x):
        for step, other_y in enumerate((index_y, next_y[1], prev_y[1])):
            send(
                tail_send,
                tail_in.at[slot + step],
                tail_sem.at[0, kind],
                tail_sem.at[1, kind],
                (other_x, other_y),
            )

    only_if(has_next, lambda: tails_to(0, 0, next_x[0]))
    only_if(has_prev, lambda: tails_to(3, 1, prev_x[0]))
    for side in range(2):
        send(tail_send, tail_in.at[6 + side], tail_sem.at[0, 2], tail_sem.at[1, 2], sides[2 + side])

    def wait_bulk(sem, tiles_x, tiles_y):
        wait_sides(
            (sizes.at[0:tiles_x], sizes.at[0:tiles_x]), sizes.at[0 : 2 * tiles_y], sem
        )

    wait_bulk(agg_sem.at[1], 32, 64)
    wait_bulk(more_sem.at[1], 10, 18)

    def both_x(place):
        return jnp.concatenate([side_x[0, place], side_x[1, place]], axis=1)

    def both_y(low, high):
        shape = low.shape
        low, high = low.reshape(-1, 8, 128), high.reshape(-1, 8, 128)
        return roll(jnp.where(iota(low.shape, 1) < 4, high, low), 4, 1).reshape(shape)

    diag_x, y_x, z_x, resid_x = [both_x(place) for place in (0, 2, 3, 4)]
    diag_y, x_y, y_y, z_y, resid_y = [
        both_y(side_y[0, place], side_y[1, place]) for place in range(5)
    ]
    rows_x = [
        jnp.broadcast_to(late_x[side], (2 * SIZE, 8, 128)).reshape(FIELD) for side in range(2)
    ]
    rows_x = jnp.concatenate([rows_x[0][:, 4:], rows_x[1][:, :4]], axis=1)
    y_x = y_x + jnp.where(second == 0, rows_x, 0.0)
    y_y = y_y + row_roll(coef[7], -3)
    first_x = both_y(late_y[0], late_y[1])
    kinds_x = jnp.concatenate([side_x[0, 1, 0, 1], side_x[1, 1, 0, 1]], axis=1)
    lower = iota((1, 128), 1) < 64

    def swap_halves(line):
        return roll(line, 64, 1)

    kinds_y = jnp.concatenate(
        [
            swap_halves(
                jnp.where(
                    iota((8, 128), 1) < 64,
                    side_y[1, 1, 0, 4 * part + 1],
                    side_y[0, 1, 0, 4 * part + 1],
                )
            )
            for part in range(2)
        ],
        axis=1,
    )

    own = [tail_send[part] for part in range(2)]
    wait_sides((tail_in.at[0:3], tail_in.at[3:6]), tail_in.at[6:8], tail_sem.at[1])
    low_mid, low_from_low, low_from_high = [tail_in[place, 1] for place in (0, 1, 2)]
    low_far = tail_in[0, 0]
    high_mid, high_from_low, high_from_high = [tail_in[place, 0] for place in (3, 4, 5)]
    high_far = tail_in[3, 1]
    below = [tail_in[6, part] for part in range(2)]
    above = [tail_in[7, part] for part in range(2)]

    def y_lines(mid, from_low, from_high):
        return (
            swap_halves(jnp.where(lower, from_high, mid)),
            swap_halves(jnp.where(lower, mid, from_low)),
        )

    def spread_lines(lines):
        return turned(
            jnp.concatenate(
                [jnp.broadcast_to(line, (8, 128))[None] for line in lines], axis=0
            )
        )

    def minus_coarse(resid, diag_f, x_low, x_high, y_f, z_f, mid, x_lines, y_pair):
        up, down = y_pair
        tiles = spread_lines(
            [mid, x_lines[0], x_lines[1], up, down, roll(mid, 1, 1), roll(mid, -1, 1)]
        )
        value = tiles[0]
        across_y = value - jnp.where((iota((8, 128), 0) & 3) == 3, tiles[3], tiles[4])
        across_z = jnp.concatenate(
            [(value - tiles[5])[None, None], (value - tiles[6])[None, None]], axis=0
        )
        resid = resid - diag_f * value - y_f * across_y - z_f * across_z
        first_layer = resid[:, 0:1] - (x_low * (value - tiles[1]))[:, None]
        last_layer = resid[:, 3:4] - (x_high * (value - tiles[2]))[:, None]
        return jnp.concatenate([first_layer, resid[:, 1:3], last_layer], axis=1), value

    def two_rows(resid, fields, x_faces, mids, x_lines, y_pairs):
        parts = [
            minus_coarse(
                resid[:, 4 * part : 4 * part + 4],
                fields[0][:, 4 * part : 4 * part + 4],
                x_faces[part][0],
                x_faces[part][1],
                fields[1][:, 4 * part : 4 * part + 4],
                fields[2][:, 4 * part : 4 * part + 4],
                mids[part],
                x_lines[part],
                y_pairs[part],
            )
            for part in range(2)
        ]
        return jnp.concatenate([parts[0][0], parts[1][0]], axis=1), [part[1] for part in parts]

    resid, own_tiles = two_rows(
        resid,
        (agg[0], agg[2] + coef[8], agg[3]),
        ((coef[2, :, 0], tx_at[0]), (tx_at[0], tx_at[1])),
        own,
        ((low_mid, own[1]), (own[0], high_mid)),
        [y_lines(own[part], below[part], above[part]) for part in range(2)],
    )
    resid_x, tiles_x = two_rows(
        resid_x,
        (diag_x, y_x, z_x),
        ((side_x[0, 1, :, 0], side_x[0, 1, :, 3]), (tx_at[1], side_x[1, 1, :, 3])),
        (low_mid, high_mid),
        ((low_far, own[0]), (own[1], high_far)),
        (
            y_lines(low_mid, low_from_low, low_from_high),
            y_lines(high_mid, high_from_low, high_from_high),
        ),
    )

    def beside_y(low, high):
        return swap_halves(jnp.where(lower, high, low))

    mids_y = [beside_y(below[part], above[part]) for part in range(2)]
    resid_y, tiles_y = two_rows(
        resid_y,
        (diag_y, y_y, z_y),
        ((first_x, x_y[:, 3]), (x_y[:, 4], x_y[:, 7])),
        mids_y,
        (
            (beside_y(low_from_low, low_from_high), mids_y[1]),
            (mids_y[0], beside_y(high_from_low, high_from_high)),
        ),
        [
            (
                jnp.where(lower, own[part], above[part]),
                jnp.where(lower, below[part], own[part]),
            )
            for part in range(2)
        ],
    )

    def over_layers(tiles):
        tiles = jnp.concatenate([tiles[place // 4][None] for place in range(SIZE)], axis=0)
        return jnp.broadcast_to(tiles[None], FIELD)

    iterate = iterate + over_layers(own_tiles) + smooth(resid)
    outer_x = products(resid_x, blocks_x, 32, kinds_x)
    low_x = low_x + tiles_x[0][None] + turned(outer_x[16:32, :128].reshape(2, 8, 128))
    high_x = high_x + tiles_x[1][None] + turned(outer_x[0:16, 128:].reshape(2, 8, 128))
    outer_y = jnp.where(second < 4, low_y, high_y) + over_layers(tiles_y)
    outer_y = outer_y + smooth(resid_y, blocks_y, kinds_y)
    resid = resid_edges(resid_base(iterate), high_x, low_x, outer_y, outer_y)
    iterate = iterate + smooth(resid)

    send_faces(2, iterate)
    out_buf[0] = iterate
    stores = [
        pltpu.make_async_copy(out_buf.at[place], both_any.at[place], store_sem.at[place])
        for place in range(2)
    ]
    stores[0].start()
    resid = resid_base(iterate)
    wait_faces(2)
    out_buf[1] = resid_edges(resid, *halos(2))
    stores[1].start()
    only_if(has_next, lambda: wait_bytes(face_x.at[:, 0], face_send_sem.at[0]))
    only_if(has_prev, lambda: wait_bytes(face_x.at[:, 1], face_send_sem.at[1]))
    wait_bytes(face_y, face_send_sem.at[2])
    only_if(has_next, lambda: wait_bytes(ends_send.at[0, 0], ends_sem.at[0, 0]))
    wait_bytes(ends_send.at[0, 1], ends_sem.at[0, 2])
    wait_bytes(gop.at[1:], gop_sem.at[0])
    wait_bytes(gres.at[1:], gres_sem.at[0])
    wait_bytes(beside, beside_sem.at[0])
    only_if(last_member, lambda: wait_bytes(edge_in.at[0], edge_sem.at[0, 0]))
    only_if(first_member, lambda: wait_bytes(edge_in.at[1], edge_sem.at[0, 1]))
    only_if(has_next, lambda: wait_bytes(tail_in.at[0:3], tail_sem.at[0, 0]))
    only_if(has_prev, lambda: wait_bytes(tail_in.at[3:6], tail_sem.at[0, 1]))
    wait_bytes(tail_in.at[6:8], tail_sem.at[0, 2])
    for sem, tiles_x, tiles_y in ((agg_sem.at[0], 32, 64), (more_sem.at[0], 10, 18)):
        only_if(has_next, lambda: wait_bytes(sizes.at[0:tiles_x], sem.at[0]))
        only_if(has_prev, lambda: wait_bytes(sizes.at[0:tiles_x], sem.at[1]))
        wait_bytes(sizes.at[0 : 2 * tiles_y], sem.at[2])
    for store in stores:
        store.wait()


def to_outer_order(both, pressure, resid):
    row = iota((DEPTH, DEPTH), 0)
    col = iota((DEPTH, DEPTH), 1)
    to_outside = (col == 4 * (row & 63) + (row >> 6)).astype(F32).astype(BF16)
    for place, out in enumerate((pressure, resid)):
        out[...] = times_ones(flat(both[place]), to_outside).reshape(SIZE, SIZE, DEPTH)


def on_device(
    count_x,
    count_y,
    pressure_rhs,
    accumulation,
    trans_x,
    trans_y,
    trans_z,
    well_cells,
    well_flags,
    well_rates,
    well_index,
    block_map,
    block_inverses,
):
    anywhere = pl.BlockSpec(memory_space=pl.ANY)
    dma = pltpu.SemaphoreType.DMA
    out = jax.ShapeDtypeStruct(pressure_rhs.shape, F32)
    both = pl.pallas_call(
        functools.partial(kernel, count_x, count_y),
        out_shape=jax.ShapeDtypeStruct((2,) + FIELD, F32),
        in_specs=[anywhere] * 11,
        out_specs=anywhere,
        scratch_shapes=[
            pltpu.VMEM((5, SIZE, SIZE, DEPTH), F32),
            pltpu.VMEM((2, 2, 64), jnp.int32),
            pltpu.SMEM((WELLS,), jnp.int32),
            pltpu.SMEM((WELLS,), jnp.int32),
            pltpu.SMEM((WELLS,), F32),
            pltpu.SMEM((WELLS,), F32),
            pltpu.VMEM((KINDS * 64, 64), F32),
            pltpu.VMEM((KINDS * 64, DEPTH), BF16),
            pltpu.VMEM(FIELD, F32),
            pltpu.VMEM((9,) + FIELD, F32),
            pltpu.VMEM((3, 2, 2, SIZE, 128), F32),
            pltpu.VMEM((3, 2, 2 * SIZE, 1, 128), F32),
            pltpu.VMEM((3, 2, 2, SIZE, 128), F32),
            pltpu.VMEM((3, 2, 2 * SIZE, 1, 128), F32),
            pltpu.VMEM((1, 2, SIZE, DEPTH), F32),
            pltpu.VMEM((1, 2, SIZE, DEPTH), F32),
            pltpu.VMEM((8, 128), F32),
            pltpu.VMEM((GROUP, 8, 128), F32),
            pltpu.VMEM((1, 512), F32),
            pltpu.VMEM((GROUP, 1, 512), F32),
            pltpu.VMEM((2, 1, 128), F32),
            pltpu.VMEM((2, GROUP, 1, 128), F32),
            pltpu.VMEM((2, 1, 128), F32),
            pltpu.VMEM((2, GROUP, 1, 128), F32),
            pltpu.VMEM((2, GROUP, 128), F32),
            pltpu.VMEM((2, 1, 128), F32),
            pltpu.VMEM((8, 2, 1, 128), F32),
            pltpu.VMEM((2,) + FIELD, F32),
            pltpu.VMEM((4,) + FIELD, F32),
            pltpu.VMEM(FIELD, F32),
            pltpu.VMEM((2, 5, 2, 4, 8, 128), F32),
            pltpu.VMEM((2, 5) + FIELD, F32),
            pltpu.VMEM((2 * SIZE, 1, 128), F32),
            pltpu.VMEM((2, SIZE, 128), F32),
            pltpu.VMEM((2, 2 * SIZE, 1, 128), F32),
            pltpu.VMEM((2, 2, SIZE, 128), F32),
            pltpu.VMEM((KINDS * 32, DEPTH), BF16),
            pltpu.VMEM((KINDS * 64, DEPTH), BF16),
            pltpu.VMEM((128, 8, 128), F32),
            dma((11,)),
            dma((2,)),
            dma((3,)),
            dma((3, 3)),
            dma((2, 3)),
            dma((2,)),
            dma((2,)),
            dma((2,)),
            dma((2, 2)),
            dma((2, 3)),
            dma((2, 3)),
            dma((2, 3)),
            pltpu.SemaphoreType.REGULAR,
            pltpu.SemaphoreType.REGULAR,
        ],
        compiler_params=pltpu.CompilerParams(
            collective_id=0, has_side_effects=True, vmem_limit_bytes=60 * 1024 * 1024
        ),
    )(
        pressure_rhs,
        accumulation,
        trans_x,
        trans_y,
        trans_z,
        well_cells,
        well_flags,
        well_rates,
        well_index,
        block_map,
        block_inverses.reshape(KINDS * 64, 64),
    )
    return pl.pallas_call(to_outer_order, out_shape=(out, out))(both)


def solution(mesh):
    cells = P("gx", "gy", None)
    wells = P(("gx", "gy"))
    return jax.shard_map(
        functools.partial(on_device, mesh.shape["gx"], mesh.shape["gy"]),
        mesh=mesh,
        in_specs=(cells,) * 5 + (wells,) * 4 + (cells, P()),
        out_specs=(cells, cells),
        check_vma=False,
    )
```

```python
import functools

import jax
import jax.numpy as jnp
from jax import lax
from jax.experimental import pallas as pl
from jax.experimental.pallas import tpu as pltpu
from jax.sharding import PartitionSpec as P

OMEGA = 0.8
GROUP = 16
SIZE = 8
DEPTH = 256
KINDS = 16
WELLS = 4
DOUBLINGS = 9
LATE_DOUBLINGS = 4
MESH = pl.DeviceIdType.MESH
HIGHEST = lax.Precision.HIGHEST
F32 = jnp.float32
BF16 = jnp.bfloat16
FIELD = (2, SIZE, SIZE, 128)


def iota(shape, dim):
    return lax.broadcasted_iota(jnp.int32, shape, dim)


def roll(values, shift, axis):
    return pltpu.roll(values, shift % values.shape[axis], axis)


def split_three(values):
    high = values.astype(BF16)
    rest = values - high.astype(F32)
    middle = rest.astype(BF16)
    low = (rest - middle.astype(F32)).astype(BF16)
    return high, middle, low


def split_two(values):
    high = values.astype(BF16)
    low = (values - high.astype(F32)).astype(BF16)
    return high, low


def times_ones(values, ones):
    return sum(jnp.dot(part, ones, preferred_element_type=F32) for part in split_three(values))


def flat(field):
    return jnp.concatenate(
        [field[0].reshape(SIZE * SIZE, 128), field[1].reshape(SIZE * SIZE, 128)], axis=1
    )


def unflat(rows):
    shape = (1, SIZE, SIZE, 128)
    return jnp.concatenate(
        [rows[:, :128].reshape(shape), rows[:, 128:].reshape(shape)], axis=0
    )


def lane_roll(field, shift):
    return roll(field.reshape(-1, 8, 128), shift, 2).reshape(field.shape)


def row_roll(field, shift):
    return roll(field.reshape(-1, 8, 128), shift, 1).reshape(field.shape)


def z_neighbours(field):
    low, high = field[0], field[1]
    lower_lanes = iota(low.shape, 2) < 64
    across = lane_roll(jnp.where(lower_lanes, high, low), 64)
    up = [across, jnp.where(lower_lanes, lane_roll(high, 64), lane_roll(low, 63))]
    down = [jnp.where(lower_lanes, lane_roll(high, 65), lane_roll(low, 64)), across]
    return (
        jnp.concatenate([part[None] for part in up], axis=0),
        jnp.concatenate([part[None] for part in down], axis=0),
    )


def turned(field):
    shape = (field.size // 1024, 8, 128)
    same = (iota(shape, 1) >= 4) == (iota(shape, 2) >= 64)
    tiles = field.reshape(shape)
    return jnp.where(same, tiles, roll(roll(tiles, 4, 1), 64, 2)).reshape(field.shape)


def agg_rows(tile):
    tile = tile + roll(tile, 64, 1)
    tile = tile + roll(tile, -1, 0)
    tile = tile + roll(tile, -2, 0)
    return jnp.where(iota((1, 128), 1) < 64, tile[0:1], tile[4:5])


def xor_sum(values, step, axis):
    place = iota(values.shape, axis)
    return values + jnp.where(
        (place & step) == 0, roll(values, -step, axis), roll(values, step, axis)
    )


def xor_upper(values, step, axis):
    place = iota(values.shape, axis)
    return jnp.where((place & step) == 0, roll(values, -step, axis), values)


def only_if(condition, action):
    if condition is None:
        action()
    else:
        pl.when(condition)(action)


def send(src, dst, send_sem, recv_sem, device):
    pltpu.make_async_remote_copy(
        src_ref=src,
        dst_ref=dst,
        send_sem=send_sem,
        recv_sem=recv_sem,
        device_id=device,
        device_id_type=MESH,
    ).start()


def wait_bytes(like, sem):
    pltpu.make_async_copy(like, like, sem).wait()


def kernel(
    count_x,
    count_y,
    rhs_any,
    acc_any,
    tx_any,
    ty_any,
    tz_any,
    cells_any,
    flags_any,
    rates_any,
    index_any,
    map_any,
    inv_any,
    both_any,
    fields_in,
    map_in,
    cells,
    flags,
    rates,
    well_index,
    inv_in,
    blocks,
    source,
    coef,
    face_x,
    face_y,
    halo_x,
    halo_y,
    ends_in,
    ends_send,
    gop_send,
    gop,
    gres_send,
    gres,
    beside_send,
    beside,
    edge_send,
    edge_in,
    tail,
    tail_send,
    tail_in,
    out_buf,
    agg,
    resid_two,
    side_x,
    side_y,
    late_send_x,
    late_send_y,
    late_x,
    late_y,
    blocks_x,
    blocks_y,
    sizes,
    load_sem,
    store_sem,
    face_send_sem,
    face_recv_sem,
    ends_sem,
    gop_sem,
    gres_sem,
    beside_sem,
    edge_sem,
    tail_sem,
    agg_sem,
    more_sem,
    near_sem,
    end_sem,
):
    index_x = lax.axis_index("gx")
    index_y = lax.axis_index("gy")
    rank = lax.rem(index_x, GROUP)
    base = index_x - rank
    next_x = (lax.rem(index_x + 1, count_x), index_y)
    prev_x = (lax.rem(index_x + count_x - 1, count_x), index_y)
    next_y = (index_x, lax.rem(index_y + 1, count_y))
    prev_y = (index_x, lax.rem(index_y + count_y - 1, count_y))
    sides = (next_x, prev_x, next_y, prev_y)
    steps = sorted(range(GROUP), key=lambda step: -min(step % 8, -step % 8))
    members = [base + lax.rem(rank + step, GROUP) for step in steps]
    mates = [(member, index_y) for step, member in zip(steps, members) if step > 0]
    upper_group = [(member, next_y[1]) for member in members]
    lower_group = [(member, prev_y[1]) for member in members]
    has_next = index_x < count_x - 1
    has_prev = index_x > 0
    group_after = base + GROUP < count_x
    group_before = base > 0
    last_member = group_after & (rank == GROUP - 1)
    first_member = group_before & (rank == 0)
    send_if = (has_next, has_prev, None, None)

    loads = [
        pltpu.make_async_copy(src, dst, load_sem.at[place])
        for place, (src, dst) in enumerate(
            (
                (inv_any, inv_in),
                (rhs_any, fields_in.at[0]),
                (tx_any, fields_in.at[1]),
                (ty_any, fields_in.at[2]),
                (tz_any, fields_in.at[3]),
                (acc_any, fields_in.at[4]),
                (map_any, map_in),
                (cells_any, cells),
                (flags_any, flags),
                (rates_any, rates),
                (index_any, well_index),
            )
        )
    ]
    for load in loads:
        load.start()
    halo_x[...] = jnp.zeros_like(halo_x)
    ends_in[...] = jnp.zeros_like(ends_in)
    edge_in[...] = jnp.zeros_like(edge_in)
    tail_in[...] = jnp.zeros_like(tail_in)
    side_x[...] = jnp.zeros_like(side_x)
    late_x[...] = jnp.zeros_like(late_x)

    barrier = pltpu.get_barrier_semaphore()

    def member(step_z, step_y):
        place = lax.rem(rank // 8 + step_y, 2) * 8 + lax.rem(lax.rem(rank, 8) + step_z + 8, 8)
        return base + place

    near = []
    for step_z in (2, -2, 1, -1, 0):
        near.append((member(step_z, 1), index_y))
        near.append((member(step_z, 0), next_y[1]))
        near.append((member(step_z, 0), prev_y[1]))
        if step_z != 0:
            near.append((member(step_z, 0), index_y))

    def announce(semaphore):
        for device in near:
            pl.semaphore_signal(semaphore, inc=1, device_id=device, device_id_type=MESH)
        announce_end(semaphore)

    def announce_end(semaphore):
        for condition, device in ((last_member, next_x), (first_member, prev_x)):
            only_if(
                condition,
                lambda device=device: pl.semaphore_signal(
                    semaphore, inc=1, device_id=device, device_id_type=MESH
                ),
            )

    group_end = last_member.astype(jnp.int32) + first_member.astype(jnp.int32)
    announced = len(near) + group_end
    announce(barrier)

    row = iota((DEPTH, DEPTH), 0)
    col = iota((DEPTH, DEPTH), 1)
    to_inside = (row == 4 * (col & 63) + (col >> 6)).astype(F32).astype(BF16)
    lane = iota(FIELD, 3)
    second = iota(FIELD, 2)
    first = iota(FIELD, 1)
    half = iota(FIELD, 0)
    cell_id = ((half * SIZE + first) * SIZE + second) * 128 + lane

    def swapped_offsets(place):
        return (place & ~15) | ((place & 3) << 2) | ((place >> 2) & 3)

    row_k = iota((128, DEPTH), 0)
    col_k = iota((128, DEPTH), 1)
    take_cols = ((row_k & 63) == swapped_offsets(col_k & 63)) & ((row_k < 64) == (col_k < 128))
    take_cols = take_cols.astype(F32).astype(BF16)
    loads[0].wait()
    tiles = [
        (OMEGA * inv_in[pl.ds(third, KINDS * 16, stride=4), :]).reshape(KINDS * 2, 8, 64)
        for third in range(4)
    ]
    upper_half = iota((KINDS * 2, 8, 64), 1) >= 4
    rows = jnp.concatenate(
        [
            tile[:, None]
            for tile in (
                jnp.where(upper_half, roll(tiles[1], 4, 1), tiles[0]),
                jnp.where(upper_half, roll(tiles[3], 4, 1), tiles[2]),
                jnp.where(upper_half, tiles[1], roll(tiles[0], 4, 1)),
                jnp.where(upper_half, tiles[3], roll(tiles[2], 4, 1)),
            )
        ],
        axis=1,
    ).reshape(KINDS * 64, 64)
    high, low = split_two(rows)
    blocks[...] = jnp.dot(
        jnp.concatenate([high, low], axis=1), take_cols, preferred_element_type=F32
    ).astype(BF16)

    for place in range(7, 11):
        loads[place].wait()
    plane_cells = SIZE * count_y * DEPTH
    well_ids = []
    for well in range(WELLS):
        cell = cells[well]
        pos_x = cell // plane_cells - index_x * SIZE
        left = lax.rem(cell, plane_cells)
        pos_y = left // DEPTH - index_y * SIZE
        pos_z = lax.rem(left, DEPTH)
        place = lax.rem(pos_z, 4) * 64 + pos_z // 4
        well_ids.append(
            ((place // 128 * SIZE + pos_x) * SIZE + pos_y) * 128 + lax.rem(place, 128)
        )
    signed = [
        jnp.where(flags[well] == 1, rates[well], -rates[well]) for well in range(WELLS)
    ]

    loads[1].wait()
    well_source = jnp.zeros(FIELD, F32)
    for well in range(WELLS):
        well_source = well_source + jnp.where(cell_id == well_ids[well], signed[well], 0.0)
    source[...] = (
        unflat(times_ones(fields_in[0].reshape(SIZE * SIZE, DEPTH), to_inside)) + well_source
    )

    loads[6].wait()
    kinds = []
    for part in range(2):
        kind = map_in[part]
        kinds.append(jnp.concatenate([kind[0:1], kind[1:2]], axis=1))
    kind_ids = jnp.broadcast_to(jnp.concatenate(kinds, axis=1), (8, 256))

    def products(field, operators, rows, kind_row):
        tiles = turned(field)
        columns = jnp.concatenate(
            [
                jnp.concatenate(
                    [
                        tiles[half_id, 4 * part + offset]
                        for offset in range(4)
                        for half_id in range(2)
                    ],
                    axis=0,
                )
                for part in range(2)
            ],
            axis=1,
        )
        high, low = split_two(columns)
        product = jnp.dot(
            operators[...],
            jnp.concatenate([high, low, high, low], axis=0),
            preferred_element_type=F32,
        )
        chosen = product[0:rows]
        for kind in range(1, KINDS):
            mask = jnp.broadcast_to((kind_row == kind)[None], (rows // 8, 8, 256))
            chosen = jnp.where(
                mask.reshape(rows, 256), product[rows * kind : rows * kind + rows], chosen
            )
        return chosen

    def smooth(resid, operators=blocks, kind_row=kind_ids):
        chosen = products(resid, operators, 64, kind_row)
        back = [
            [
                chosen[8 * (2 * offset + half_id) : 8 * (2 * offset + half_id) + 8,
                       128 * part : 128 * part + 128][None]
                for part in range(2)
                for offset in range(4)
            ]
            for half_id in range(2)
        ]
        field = jnp.concatenate(
            [jnp.concatenate(tiles, axis=0)[None] for tiles in back], axis=0
        )
        return turned(field)

    def send_faces(step, field):
        face_x[step, 0] = field[:, SIZE - 1]
        face_x[step, 1] = field[:, 0]
        tiles = field.reshape(2 * SIZE, 8, 128)
        face_y[step, 0] = tiles[:, 7:8, :]
        face_y[step, 1] = tiles[:, 0:1, :]
        for side, (out, into) in enumerate(
            ((face_x, halo_x), (face_x, halo_x), (face_y, halo_y), (face_y, halo_y))
        ):
            to_side(
                side,
                out.at[step, side % 2],
                into.at[step, side % 2],
                face_send_sem,
                face_recv_sem.at[step],
            )

    def to_side(side, src, dst, send_sems, recv_sems):
        kind = min(side, 2)
        only_if(
            send_if[side],
            lambda: send(src, dst, send_sems.at[kind], recv_sems.at[kind], sides[side]),
        )

    def wait_sides(buffer_x, buffer_y, sems):
        only_if(has_prev, lambda: wait_bytes(buffer_x[0], sems.at[0]))
        only_if(has_next, lambda: wait_bytes(buffer_x[1], sems.at[1]))
        wait_bytes(buffer_y, sems.at[2])

    def wait_faces(step):
        wait_sides(
            (halo_x.at[step, 0], halo_x.at[step, 1]), halo_y.at[step], face_recv_sem.at[step]
        )

    iterate = smooth(source[...])

    pl.semaphore_wait(barrier, announced)
    announce(near_sem)
    send_faces(0, iterate)

    loads[2].wait()
    loads[3].wait()
    ends_send[0, 0] = fields_in[1, SIZE - 1]
    for place in range(SIZE):
        ends_send[0, 1, place : place + 1] = fields_in[2, place, SIZE - 1 : SIZE, :]
    for side in range(2):
        to_side(2 * side, ends_send.at[0, side], ends_in.at[0, side], ends_sem.at[0], ends_sem.at[1])
    loads[4].wait()
    loads[5].wait()
    inside = times_ones(
        fields_in[1:5].reshape(4 * SIZE * SIZE, DEPTH), to_inside
    )
    tx, ty, tz, acc = [unflat(inside[64 * place : 64 * place + 64]) for place in range(4)]
    well_diag = jnp.zeros(FIELD, F32)
    for well in range(WELLS):
        well_diag = well_diag + jnp.where(cell_id == well_ids[well], well_index[well], 0.0)
    diag = acc + well_diag
    tx = jnp.where((first == SIZE - 1) & (index_x == count_x - 1), 0.0, tx)
    ty = jnp.where((second == SIZE - 1) & (index_y == count_y - 1), 0.0, ty)
    tz = jnp.where((half == 1) & (lane == 127), 0.0, tz)

    for part in range(2):
        mine = slice(4 * part, 4 * part + 4)
        gop_send[part : part + 1] = agg_rows(diag[:, mine].sum(axis=(0, 1)))
        gop_send[2 + part : 3 + part] = agg_rows(tx[:, 4 * part + 3].sum(axis=0))
        tile = ty[:, mine].sum(axis=(0, 1))
        tile = tile + roll(tile, 64, 1)
        gop_send[4 + part : 5 + part] = jnp.where(
            iota((1, 128), 1) < 64, tile[3:4], tile[7:8]
        )
        tile = tz[1, mine].sum(axis=0)
        gop_send[6 + part : 7 + part] = agg_rows(
            jnp.where(iota((8, 128), 1) >= 64, tile, 0.0)
        )

    tz_down = jnp.where((half == 0) & (lane == 0), 0.0, z_neighbours(tz)[1])
    agg[0] = diag
    agg[1] = jnp.zeros(FIELD, F32)
    for place, layer in ((3, 3), (4, 3), (7, 7)):
        agg[1, :, place] = tx[:, layer]
    for part in range(2):
        agg[1, 0, 4 * part + 1] = kind_ids[:, 128 * part : 128 * part + 128].astype(F32)
    agg[2] = jnp.where(
        (second & 3) == 3, ty, jnp.where(second == 4, row_roll(ty, 1), 0.0)
    )
    agg[3] = jnp.where(
        (half == 0) & (lane < 64), tz_down, jnp.where((half == 1) & (lane >= 64), tz, 0.0)
    )


    def to_all(devices, mine, target, sems):
        for device in devices:
            send(mine, target, sems.at[0], sems.at[1], device)

    for side, part in enumerate((slice(4, 8), slice(0, 4))):
        to_side(side, agg.at[:, :, part], side_x.at[side, 0:4], agg_sem.at[0], agg_sem.at[1])
        to_side(2 + side, agg, side_y.at[side, 0:4], agg_sem.at[0], agg_sem.at[1])

    for kind in range(KINDS):
        blocks_x[32 * kind : 32 * kind + 16, :] = blocks[64 * kind : 64 * kind + 16, :]
        blocks_x[32 * kind + 16 : 32 * kind + 32, :] = blocks[64 * kind + 48 : 64 * kind + 64, :]
    mirror = (col == (row ^ 3)).astype(F32).astype(BF16)
    for part in range(KINDS // 4):
        here = slice(part * DEPTH, (part + 1) * DEPTH)
        blocks_y[here, :] = jnp.dot(
            mirror, blocks[here, :], preferred_element_type=F32
        ).astype(BF16)

    pl.semaphore_wait(near_sem, announced)
    announce_end(end_sem)
    to_all(mates, gop_send, gop.at[rank], gop_sem)
    gop[rank] = gop_send[...]

    only_if(has_prev, lambda: wait_bytes(ends_in.at[0, 0], ends_sem.at[1, 0]))
    wait_bytes(ends_in.at[0, 1], ends_sem.at[1, 2])
    end_rows = times_ones(ends_in[0].reshape(2 * SIZE, DEPTH), to_inside)
    end_x = jnp.where(index_x == 0, 0.0, end_rows[0:SIZE])
    end_y = jnp.where(index_y == 0, 0.0, end_rows[SIZE:])
    end_x = jnp.concatenate([end_x[None, None, :, :128], end_x[None, None, :, 128:]], axis=0)
    tx_down = jnp.concatenate([end_x, tx[:, : SIZE - 1]], axis=1)
    for part in range(2):
        for place in range(SIZE):
            late_send_x[SIZE * part + place] = end_y[
                place : place + 1, 128 * part : 128 * part + 128
            ]
    late_send_y[...] = end_x[:, 0]
    end_y = jnp.broadcast_to(late_send_x[...], (2 * SIZE, 8, 128)).reshape(FIELD)
    ty_in = jnp.where(second == SIZE - 1, 0.0, ty)
    ty_down_in = row_roll(ty_in, 1)
    ty_edge = ty - ty_in
    ty_down_edge = jnp.where(second == 0, end_y, 0.0)
    coef[0] = (
        diag + tx + tx_down + ty + ty_down_in + ty_down_edge + tz + tz_down
    )
    coef[1] = tx
    coef[2] = tx_down
    coef[3] = ty_in
    coef[4] = ty_down_in
    coef[5] = tz
    coef[6] = tz_down
    coef[7] = ty_edge
    coef[8] = ty_down_edge
    tx_at = [tx[:, 3], tx[:, 7]]

    def resid_base(field):
        nothing = jnp.zeros((2, 1, SIZE, 128), F32)
        up_z, down_z = z_neighbours(field)
        return (
            source[...]
            - coef[0] * field
            + coef[1] * jnp.concatenate([field[:, 1:], nothing], axis=1)
            + coef[2] * jnp.concatenate([nothing, field[:, : SIZE - 1]], axis=1)
            + coef[3] * row_roll(field, -1)
            + coef[4] * row_roll(field, 1)
            + coef[5] * up_z
            + coef[6] * down_z
        )

    def resid_edges(resid, high_x, low_x, high_y, low_y):
        first_row = resid[:, 0:1] + (coef[2, :, 0] * low_x)[:, None]
        last_row = resid[:, SIZE - 1 :] + (coef[1, :, SIZE - 1] * high_x)[:, None]
        resid = jnp.concatenate([first_row, resid[:, 1 : SIZE - 1], last_row], axis=1)
        return resid + coef[7] * high_y + coef[8] * low_y

    def halos(step):
        spread = [
            jnp.broadcast_to(halo_y[step, side], (2 * SIZE, 8, 128)).reshape(FIELD)
            for side in (1, 0)
        ]
        return halo_x[step, 1], halo_x[step, 0], spread[0], spread[1]

    resid = resid_base(iterate)
    wait_faces(0)
    resid = resid_edges(resid, *halos(0))
    iterate = iterate + smooth(resid)

    send_faces(1, iterate)
    resid = resid_base(iterate)

    for part in range(2):
        mine = slice(4 * part, 4 * part + 4)
        gres_send[:, 128 * part : 128 * part + 128] = agg_rows(resid[:, mine].sum(axis=(0, 1)))
    flux_up = agg_rows((coef[1, :, SIZE - 1] * iterate[:, SIZE - 1]).sum(axis=0))
    flux_down = agg_rows((coef[2, :, 0] * iterate[:, 0]).sum(axis=0))
    gres_send[:, 256:384] = flux_up
    gres_send[:, 384:512] = flux_down
    edge_send[0] = flux_up
    edge_send[1] = flux_down
    for side in range(2):
        flux = coef[7 + side] * iterate
        lines = []
        for part in range(2):
            tile = flux[:, 4 * part : 4 * part + 4].sum(axis=(0, 1))
            tile = tile + roll(tile, 64, 1)
            lines.append(tile[7:8] if side == 0 else tile[0:1])
        beside_send[side] = jnp.where(iota((1, 128), 1) < 64, lines[0], lines[1])
    to_all(mates, gres_send, gres.at[rank], gres_sem)
    to_all(upper_group, beside_send.at[0], beside.at[0, rank], beside_sem)
    to_all(lower_group, beside_send.at[1], beside.at[1, rank], beside_sem)

    def to_edge(side, target):
        for step in range(GROUP):
            send(
                edge_send.at[side],
                edge_in.at[side, 0],
                edge_sem.at[0, side],
                edge_sem.at[1, side],
                (target + step, index_y),
            )

    only_if(last_member | first_member, lambda: pl.semaphore_wait(end_sem, 1))
    only_if(last_member, lambda: to_edge(0, base + GROUP))
    only_if(first_member, lambda: to_edge(1, base - GROUP))
    gres[rank] = gres_send[...]

    wait_bytes(gop.at[1:], gop_sem.at[1])
    shape = (GROUP, 128)
    member = iota(shape, 0)
    lane_c = iota(shape, 1)
    deep = lane_c & 63
    base_a, base_b, tx_a, tx_b, ty_a, ty_b, tz_a, tz_b = [
        gop[:, place, :] for place in range(8)
    ]

    def y_terms(values):
        return jnp.where(lane_c < 64, values, roll(values, 64, 1))

    def z_terms(values, step):
        up = jnp.where(deep < 64 - step, values, 0.0)
        down = jnp.where(deep >= step, roll(values, step, 1), 0.0)
        return up, down

    across_up = jnp.where((member & 1) == 0, tx_b, 0.0)
    across_down = jnp.where((member & 1) == 1, roll(tx_b, 1, 0), 0.0)
    y_a, y_b = y_terms(ty_a), y_terms(ty_b)
    (zu_a, zd_a), (zu_b, zd_b) = z_terms(tz_a, 1), z_terms(tz_b, 1)
    diag_a = base_a + tx_a + across_down + y_a + zu_a + zd_a
    diag_b = base_b + tx_a + across_up + y_b + zu_b + zd_b
    weight_a, weight_b = OMEGA / diag_a, OMEGA / diag_b

    def apply_one(field_a, field_b):
        out_a = (
            diag_a * field_a
            - tx_a * field_b
            - across_down * roll(field_b, 1, 0)
            - y_a * roll(field_a, 64, 1)
            - zu_a * roll(field_a, -1, 1)
            - zd_a * roll(field_a, 1, 1)
        )
        out_b = (
            diag_b * field_b
            - tx_a * field_a
            - across_up * roll(field_a, -1, 0)
            - y_b * roll(field_b, 64, 1)
            - zu_b * roll(field_b, -1, 1)
            - zd_b * roll(field_b, 1, 1)
        )
        return out_a, out_b

    levels = []
    base_k = xor_sum(base_a + base_b, 1, 1)
    tx_k = xor_sum(tx_b, 1, 1)
    ty_k = xor_sum(ty_a + ty_b, 1, 1)
    tz_k = xor_upper(tz_a + tz_b, 1, 1)
    for level in range(2, 5):
        step_x, step_z = 1 << (level - 2), 1 << (level - 1)
        cell_x = member >> (level - 2)
        up_x = jnp.where((cell_x & 3) != 3, tx_k, 0.0)
        down_x = jnp.where((cell_x & 3) != 0, roll(tx_k, step_x, 0), 0.0)
        both_y = y_terms(ty_k)
        up_z, down_z = z_terms(tz_k, step_z)
        diag_k = base_k + up_x + down_x + both_y + up_z + down_z
        levels.append((diag_k, up_x, down_x, both_y, up_z, down_z, step_x, step_z))
        if level < 4:
            base_k = xor_sum(xor_sum(base_k, step_x, 0), step_z, 1)
            ty_k = xor_sum(xor_sum(ty_k, step_x, 0), step_z, 1)
            tx_k = xor_sum(xor_upper(tx_k, step_x, 0), step_z, 1)
            tz_k = xor_upper(xor_sum(tz_k, step_x, 0), step_z, 1)

    def apply_level(field, terms):
        diag_k, up_x, down_x, both_y, up_z, down_z, step_x, step_z = terms
        return (
            diag_k * field
            - up_x * roll(field, -step_x, 0)
            - down_x * roll(field, step_x, 0)
            - both_y * roll(field, 64, 1)
            - up_z * roll(field, -step_z, 1)
            - down_z * roll(field, step_z, 1)
        )

    lane_row = iota((128, 128), 0)
    lane_col = iota((128, 128), 1)
    real = lane_col < 64
    same_place = ((lane_row >> 6) == ((lane_col >> 3) & 1)) & (
        ((lane_row & 63) >> 3) == (lane_col & 7)
    )
    pick_one = (real & same_place & ((lane_row & 7) == 0)).astype(F32).astype(BF16)
    pick_two = (real & same_place & ((lane_row & 3) == 0)).astype(F32).astype(BF16)
    own_x = (member >> 2) == (lane_c >> 4)
    diag_k, up_x, down_x, both_y, up_z, down_z, _, _ = levels[2]
    picked = times_ones(
        jnp.concatenate(
            [1.0 / diag_k, up_x, down_x, both_y, up_z, down_z], axis=0
        ),
        pick_one,
    )
    one_member = own_x & ((member & 3) == 0)
    inverse_diag, up_x, down_x, both_y, up_z, down_z = [
        jnp.sum(
            jnp.where(one_member, picked[GROUP * place : GROUP * place + GROUP], 0.0),
            axis=0,
            keepdims=True,
        )
        for place in range(6)
    ]
    gap = lane_row - lane_col
    upper_y = (lane_col >> 3) & 1
    coupling = jnp.where(gap == 16, up_x, 0.0)
    coupling = jnp.where(gap == -16, down_x, coupling)
    coupling = jnp.where(gap == 8 - 16 * upper_y, both_y, coupling)
    coupling = jnp.where(gap == 1, up_z, coupling)
    coupling = jnp.where(gap == -1, down_z, coupling)
    power = coupling * inverse_diag
    total = jnp.where(gap == 0, 1.0, 0.0)

    def doubled(total, power):
        both = jnp.dot(
            jnp.concatenate([total, power], axis=0),
            power,
            precision=HIGHEST,
            preferred_element_type=F32,
        )
        return total + both[:128], both[128:]

    for _ in range(DOUBLINGS - LATE_DOUBLINGS):
        total, power = doubled(total, power)
    spread = jnp.concatenate(
        [
            ((lane_row >> 4) == part)
            & ((lane_row >> 3 & 1) == (lane_col >> 6))
            & ((lane_row & 7) == ((lane_col & 63) >> 3))
            & (lane_row < 64)
            for part in range(4)
        ],
        axis=1,
    )

    wait_faces(1)
    high_x, low_x, high_y, low_y = halos(1)
    resid = resid_edges(resid, high_x, low_x, high_y, low_y)
    resid_two[...] = resid
    for side, part in enumerate((slice(4, 8), slice(0, 4))):
        to_side(side, resid_two.at[:, part], side_x.at[side, 4], more_sem.at[0], more_sem.at[1])
        to_side(side, late_send_x, late_x.at[side], more_sem.at[0], more_sem.at[1])
        to_side(2 + side, resid_two, side_y.at[side, 4], more_sem.at[0], more_sem.at[1])
        to_side(2 + side, late_send_y, late_y.at[side], more_sem.at[0], more_sem.at[1])

    wait_bytes(gres.at[1:], gres_sem.at[1])
    wait_bytes(beside, beside_sem.at[1])
    only_if(group_before, lambda: wait_bytes(edge_in.at[0, 0], edge_sem.at[1, 0]))
    only_if(group_after, lambda: wait_bytes(edge_in.at[1, 0], edge_sem.at[1, 1]))
    every = gres[:, 0, :]
    first_a, first_b, from_low, from_high = [
        every[:, 128 * part : 128 * part + 128] for part in range(4)
    ]
    from_low = jnp.where(member == 0, edge_in[0, 0], roll(from_low, 1, 0))
    from_high = jnp.where(member == GROUP - 1, edge_in[1, 0], roll(from_high, -1, 0))
    below, above = beside[0, :, 0, :], beside[1, :, 0, :]
    res_a = first_a + from_low + jnp.where(lane_c < 64, below, roll(above, 64, 1))
    res_b = first_b + from_high + jnp.where(lane_c < 64, roll(below, 64, 1), above)

    for _ in range(LATE_DOUBLINGS):
        total, power = doubled(total, power)
    solver = times_ones(total, spread.astype(F32).astype(BF16))

    def descend_one(res_a, res_b):
        cor_a, cor_b = weight_a * res_a, weight_b * res_b
        out_a, out_b = apply_one(cor_a, cor_b)
        cor_a = cor_a + weight_a * (res_a - out_a)
        cor_b = cor_b + weight_b * (res_b - out_b)
        out_a, out_b = apply_one(cor_a, cor_b)
        return cor_a, cor_b, (res_a - out_a) + (res_b - out_b)

    cor_a, cor_b, left = descend_one(res_a, res_b)
    res_k = xor_sum(left, 1, 1)
    cor_k = jnp.zeros(shape, F32)
    for level in (2, 3):
        terms = levels[level - 2]
        weight = OMEGA / terms[0]
        cor = weight * res_k
        cor = cor + weight * (res_k - apply_level(cor, terms))
        left = res_k - apply_level(cor, terms)
        cor_k = cor_k + cor
        if level == 2:
            res_k = xor_sum(xor_sum(left, 1, 0), 2, 1)
    last = times_ones(left, pick_two)
    last = jnp.sum(
        jnp.where(own_x & ((member & 1) == 0), last, 0.0), axis=0, keepdims=True
    )
    last = jnp.broadcast_to(last * inverse_diag, (8, 128))
    solved = jnp.dot(last, solver, precision=HIGHEST, preferred_element_type=F32)
    solved = [jnp.broadcast_to(solved[0:1, 128 * part : 128 * part + 128], (8, 128)) for part in range(4)]
    upper_rows = (iota((8, 128), 0) & 4) != 0
    cor_k = cor_k + jnp.concatenate(
        [
            jnp.where(upper_rows, solved[1], solved[0]),
            jnp.where(upper_rows, solved[3], solved[2]),
        ],
        axis=0,
    )
    tail[0] = cor_a + cor_k
    tail[1] = cor_b + cor_k
    tail_send[0] = tail[0, pl.ds(rank, 1), :]
    tail_send[1] = tail[1, pl.ds(rank, 1), :]
    def tails_to(slot, kind, other_x):
        for step, other_y in enumerate((index_y, next_y[1], prev_y[1])):
            send(
                tail_send,
                tail_in.at[slot + step],
                tail_sem.at[0, kind],
                tail_sem.at[1, kind],
                (other_x, other_y),
            )

    only_if(has_next, lambda: tails_to(0, 0, next_x[0]))
    only_if(has_prev, lambda: tails_to(3, 1, prev_x[0]))
    for side in range(2):
        send(tail_send, tail_in.at[6 + side], tail_sem.at[0, 2], tail_sem.at[1, 2], sides[2 + side])

    def wait_bulk(sem, tiles_x, tiles_y):
        wait_sides(
            (sizes.at[0:tiles_x], sizes.at[0:tiles_x]), sizes.at[0 : 2 * tiles_y], sem
        )

    wait_bulk(agg_sem.at[1], 32, 64)
    wait_bulk(more_sem.at[1], 10, 18)

    def both_x(place):
        return jnp.concatenate([side_x[0, place], side_x[1, place]], axis=1)

    def both_y(low, high):
        shape = low.shape
        low, high = low.reshape(-1, 8, 128), high.reshape(-1, 8, 128)
        return roll(jnp.where(iota(low.shape, 1) < 4, high, low), 4, 1).reshape(shape)

    diag_x, y_x, z_x, resid_x = [both_x(place) for place in (0, 2, 3, 4)]
    diag_y, x_y, y_y, z_y, resid_y = [
        both_y(side_y[0, place], side_y[1, place]) for place in range(5)
    ]
    rows_x = [
        jnp.broadcast_to(late_x[side], (2 * SIZE, 8, 128)).reshape(FIELD) for side in range(2)
    ]
    rows_x = jnp.concatenate([rows_x[0][:, 4:], rows_x[1][:, :4]], axis=1)
    y_x = y_x + jnp.where(second == 0, rows_x, 0.0)
    y_y = y_y + row_roll(coef[7], -3)
    first_x = both_y(late_y[0], late_y[1])
    kinds_x = jnp.concatenate([side_x[0, 1, 0, 1], side_x[1, 1, 0, 1]], axis=1)
    lower = iota((1, 128), 1) < 64

    def swap_halves(line):
        return roll(line, 64, 1)

    kinds_y = jnp.concatenate(
        [
            swap_halves(
                jnp.where(
                    iota((8, 128), 1) < 64,
                    side_y[1, 1, 0, 4 * part + 1],
                    side_y[0, 1, 0, 4 * part + 1],
                )
            )
            for part in range(2)
        ],
        axis=1,
    )

    own = [tail_send[part] for part in range(2)]
    wait_sides((tail_in.at[0:3], tail_in.at[3:6]), tail_in.at[6:8], tail_sem.at[1])
    low_mid, low_from_low, low_from_high = [tail_in[place, 1] for place in (0, 1, 2)]
    low_far = tail_in[0, 0]
    high_mid, high_from_low, high_from_high = [tail_in[place, 0] for place in (3, 4, 5)]
    high_far = tail_in[3, 1]
    below = [tail_in[6, part] for part in range(2)]
    above = [tail_in[7, part] for part in range(2)]

    def y_lines(mid, from_low, from_high):
        return (
            swap_halves(jnp.where(lower, from_high, mid)),
            swap_halves(jnp.where(lower, mid, from_low)),
        )

    def spread_lines(lines):
        return turned(
            jnp.concatenate(
                [jnp.broadcast_to(line, (8, 128))[None] for line in lines], axis=0
            )
        )

    def minus_coarse(resid, diag_f, x_low, x_high, y_f, z_f, mid, x_lines, y_pair):
        up, down = y_pair
        tiles = spread_lines(
            [mid, x_lines[0], x_lines[1], up, down, roll(mid, 1, 1), roll(mid, -1, 1)]
        )
        value = tiles[0]
        across_y = value - jnp.where((iota((8, 128), 0) & 3) == 3, tiles[3], tiles[4])
        across_z = jnp.concatenate(
            [(value - tiles[5])[None, None], (value - tiles[6])[None, None]], axis=0
        )
        resid = resid - diag_f * value - y_f * across_y - z_f * across_z
        first_layer = resid[:, 0:1] - (x_low * (value - tiles[1]))[:, None]
        last_layer = resid[:, 3:4] - (x_high * (value - tiles[2]))[:, None]
        return jnp.concatenate([first_layer, resid[:, 1:3], last_layer], axis=1), value

    def two_rows(resid, fields, x_faces, mids, x_lines, y_pairs):
        parts = [
            minus_coarse(
                resid[:, 4 * part : 4 * part + 4],
                fields[0][:, 4 * part : 4 * part + 4],
                x_faces[part][0],
                x_faces[part][1],
                fields[1][:, 4 * part : 4 * part + 4],
                fields[2][:, 4 * part : 4 * part + 4],
                mids[part],
                x_lines[part],
                y_pairs[part],
            )
            for part in range(2)
        ]
        return jnp.concatenate([parts[0][0], parts[1][0]], axis=1), [part[1] for part in parts]

    resid, own_tiles = two_rows(
        resid,
        (agg[0], agg[2] + coef[8], agg[3]),
        ((coef[2, :, 0], tx_at[0]), (tx_at[0], tx_at[1])),
        own,
        ((low_mid, own[1]), (own[0], high_mid)),
        [y_lines(own[part], below[part], above[part]) for part in range(2)],
    )
    resid_x, tiles_x = two_rows(
        resid_x,
        (diag_x, y_x, z_x),
        ((side_x[0, 1, :, 0], side_x[0, 1, :, 3]), (tx_at[1], side_x[1, 1, :, 3])),
        (low_mid, high_mid),
        ((low_far, own[0]), (own[1], high_far)),
        (
            y_lines(low_mid, low_from_low, low_from_high),
            y_lines(high_mid, high_from_low, high_from_high),
        ),
    )

    def beside_y(low, high):
        return swap_halves(jnp.where(lower, high, low))

    mids_y = [beside_y(below[part], above[part]) for part in range(2)]
    resid_y, tiles_y = two_rows(
        resid_y,
        (diag_y, y_y, z_y),
        ((first_x, x_y[:, 3]), (x_y[:, 4], x_y[:, 7])),
        mids_y,
        (
            (beside_y(low_from_low, low_from_high), mids_y[1]),
            (mids_y[0], beside_y(high_from_low, high_from_high)),
        ),
        [
            (
                jnp.where(lower, own[part], above[part]),
                jnp.where(lower, below[part], own[part]),
            )
            for part in range(2)
        ],
    )

    def over_layers(tiles):
        tiles = jnp.concatenate([tiles[place // 4][None] for place in range(SIZE)], axis=0)
        return jnp.broadcast_to(tiles[None], FIELD)

    iterate = iterate + over_layers(own_tiles) + smooth(resid)
    outer_x = products(resid_x, blocks_x, 32, kinds_x)
    low_x = low_x + tiles_x[0][None] + turned(outer_x[16:32, :128].reshape(2, 8, 128))
    high_x = high_x + tiles_x[1][None] + turned(outer_x[0:16, 128:].reshape(2, 8, 128))
    outer_y = jnp.where(second < 4, low_y, high_y) + over_layers(tiles_y)
    outer_y = outer_y + smooth(resid_y, blocks_y, kinds_y)
    resid = resid_edges(resid_base(iterate), high_x, low_x, outer_y, outer_y)
    iterate = iterate + smooth(resid)

    send_faces(2, iterate)
    out_buf[0] = iterate
    stores = [
        pltpu.make_async_copy(out_buf.at[place], both_any.at[place], store_sem.at[place])
        for place in range(2)
    ]
    stores[0].start()
    resid = resid_base(iterate)
    wait_faces(2)
    out_buf[1] = resid_edges(resid, *halos(2))
    stores[1].start()
    only_if(has_next, lambda: wait_bytes(face_x.at[:, 0], face_send_sem.at[0]))
    only_if(has_prev, lambda: wait_bytes(face_x.at[:, 1], face_send_sem.at[1]))
    wait_bytes(face_y, face_send_sem.at[2])
    only_if(has_next, lambda: wait_bytes(ends_send.at[0, 0], ends_sem.at[0, 0]))
    wait_bytes(ends_send.at[0, 1], ends_sem.at[0, 2])
    wait_bytes(gop.at[1:], gop_sem.at[0])
    wait_bytes(gres.at[1:], gres_sem.at[0])
    wait_bytes(beside, beside_sem.at[0])
    only_if(last_member, lambda: wait_bytes(edge_in.at[0], edge_sem.at[0, 0]))
    only_if(first_member, lambda: wait_bytes(edge_in.at[1], edge_sem.at[0, 1]))
    only_if(has_next, lambda: wait_bytes(tail_in.at[0:3], tail_sem.at[0, 0]))
    only_if(has_prev, lambda: wait_bytes(tail_in.at[3:6], tail_sem.at[0, 1]))
    wait_bytes(tail_in.at[6:8], tail_sem.at[0, 2])
    for sem, tiles_x, tiles_y in ((agg_sem.at[0], 32, 64), (more_sem.at[0], 10, 18)):
        only_if(has_next, lambda: wait_bytes(sizes.at[0:tiles_x], sem.at[0]))
        only_if(has_prev, lambda: wait_bytes(sizes.at[0:tiles_x], sem.at[1]))
        wait_bytes(sizes.at[0 : 2 * tiles_y], sem.at[2])
    for store in stores:
        store.wait()


def to_outer_order(both, pressure, resid):
    row = iota((DEPTH, DEPTH), 0)
    col = iota((DEPTH, DEPTH), 1)
    to_outside = (col == 4 * (row & 63) + (row >> 6)).astype(F32).astype(BF16)
    for place, out in enumerate((pressure, resid)):
        out[...] = times_ones(flat(both[place]), to_outside).reshape(SIZE, SIZE, DEPTH)


def on_device(
    count_x,
    count_y,
    pressure_rhs,
    accumulation,
    trans_x,
    trans_y,
    trans_z,
    well_cells,
    well_flags,
    well_rates,
    well_index,
    block_map,
    block_inverses,
):
    anywhere = pl.BlockSpec(memory_space=pl.ANY)
    dma = pltpu.SemaphoreType.DMA
    out = jax.ShapeDtypeStruct(pressure_rhs.shape, F32)
    both = pl.pallas_call(
        functools.partial(kernel, count_x, count_y),
        out_shape=jax.ShapeDtypeStruct((2,) + FIELD, F32),
        in_specs=[anywhere] * 11,
        out_specs=anywhere,
        scratch_shapes=[
            pltpu.VMEM((5, SIZE, SIZE, DEPTH), F32),
            pltpu.VMEM((2, 2, 64), jnp.int32),
            pltpu.SMEM((WELLS,), jnp.int32),
            pltpu.SMEM((WELLS,), jnp.int32),
            pltpu.SMEM((WELLS,), F32),
            pltpu.SMEM((WELLS,), F32),
            pltpu.VMEM((KINDS * 64, 64), F32),
            pltpu.VMEM((KINDS * 64, DEPTH), BF16),
            pltpu.VMEM(FIELD, F32),
            pltpu.VMEM((9,) + FIELD, F32),
            pltpu.VMEM((3, 2, 2, SIZE, 128), F32),
            pltpu.VMEM((3, 2, 2 * SIZE, 1, 128), F32),
            pltpu.VMEM((3, 2, 2, SIZE, 128), F32),
            pltpu.VMEM((3, 2, 2 * SIZE, 1, 128), F32),
            pltpu.VMEM((1, 2, SIZE, DEPTH), F32),
            pltpu.VMEM((1, 2, SIZE, DEPTH), F32),
            pltpu.VMEM((8, 128), F32),
            pltpu.VMEM((GROUP, 8, 128), F32),
            pltpu.VMEM((1, 512), F32),
            pltpu.VMEM((GROUP, 1, 512), F32),
            pltpu.VMEM((2, 1, 128), F32),
            pltpu.VMEM((2, GROUP, 1, 128), F32),
            pltpu.VMEM((2, 1, 128), F32),
            pltpu.VMEM((2, GROUP, 1, 128), F32),
            pltpu.VMEM((2, GROUP, 128), F32),
            pltpu.VMEM((2, 1, 128), F32),
            pltpu.VMEM((8, 2, 1, 128), F32),
            pltpu.VMEM((2,) + FIELD, F32),
            pltpu.VMEM((4,) + FIELD, F32),
            pltpu.VMEM(FIELD, F32),
            pltpu.VMEM((2, 5, 2, 4, 8, 128), F32),
            pltpu.VMEM((2, 5) + FIELD, F32),
            pltpu.VMEM((2 * SIZE, 1, 128), F32),
            pltpu.VMEM((2, SIZE, 128), F32),
            pltpu.VMEM((2, 2 * SIZE, 1, 128), F32),
            pltpu.VMEM((2, 2, SIZE, 128), F32),
            pltpu.VMEM((KINDS * 32, DEPTH), BF16),
            pltpu.VMEM((KINDS * 64, DEPTH), BF16),
            pltpu.VMEM((128, 8, 128), F32),
            dma((11,)),
            dma((2,)),
            dma((3,)),
            dma((3, 3)),
            dma((2, 3)),
            dma((2,)),
            dma((2,)),
            dma((2,)),
            dma((2, 2)),
            dma((2, 3)),
            dma((2, 3)),
            dma((2, 3)),
            pltpu.SemaphoreType.REGULAR,
            pltpu.SemaphoreType.REGULAR,
        ],
        compiler_params=pltpu.CompilerParams(
            collective_id=0, has_side_effects=True, vmem_limit_bytes=60 * 1024 * 1024
        ),
    )(
        pressure_rhs,
        accumulation,
        trans_x,
        trans_y,
        trans_z,
        well_cells,
        well_flags,
        well_rates,
        well_index,
        block_map,
        block_inverses.reshape(KINDS * 64, 64),
    )
    return pl.pallas_call(to_outer_order, out_shape=(out, out))(both)


def solution(mesh):
    cells = P("gx", "gy", None)
    wells = P(("gx", "gy"))
    return jax.shard_map(
        functools.partial(on_device, mesh.shape["gx"], mesh.shape["gy"]),
        mesh=mesh,
        in_specs=(cells,) * 5 + (wells,) * 4 + (cells, P()),
        out_specs=(cells, cells),
        check_vma=False,
    )
```

```python
import functools

import jax
import jax.numpy as jnp
from jax import lax
from jax.experimental import pallas as pl
from jax.experimental.pallas import tpu as pltpu
from jax.sharding import PartitionSpec as P

OMEGA = 0.8
GROUP = 16
SIZE = 8
DEPTH = 256
KINDS = 16
WELLS = 4
DOUBLINGS = 9
LATE_DOUBLINGS = 4
MESH = pl.DeviceIdType.MESH
HIGHEST = lax.Precision.HIGHEST
F32 = jnp.float32
BF16 = jnp.bfloat16
FIELD = (2, SIZE, SIZE, 128)


def iota(shape, dim):
    return lax.broadcasted_iota(jnp.int32, shape, dim)


def roll(values, shift, axis):
    return pltpu.roll(values, shift % values.shape[axis], axis)


def split_three(values):
    high = values.astype(BF16)
    rest = values - high.astype(F32)
    middle = rest.astype(BF16)
    low = (rest - middle.astype(F32)).astype(BF16)
    return high, middle, low


def split_two(values):
    high = values.astype(BF16)
    low = (values - high.astype(F32)).astype(BF16)
    return high, low


def times_ones(values, ones):
    return sum(jnp.dot(part, ones, preferred_element_type=F32) for part in split_three(values))


def flat(field):
    return jnp.concatenate(
        [field[0].reshape(SIZE * SIZE, 128), field[1].reshape(SIZE * SIZE, 128)], axis=1
    )


def unflat(rows):
    shape = (1, SIZE, SIZE, 128)
    return jnp.concatenate(
        [rows[:, :128].reshape(shape), rows[:, 128:].reshape(shape)], axis=0
    )


def lane_roll(field, shift):
    return roll(field.reshape(-1, 8, 128), shift, 2).reshape(field.shape)


def row_roll(field, shift):
    return roll(field.reshape(-1, 8, 128), shift, 1).reshape(field.shape)


def z_neighbours(field):
    low, high = field[0], field[1]
    lower_lanes = iota(low.shape, 2) < 64
    across = lane_roll(jnp.where(lower_lanes, high, low), 64)
    up = [across, jnp.where(lower_lanes, lane_roll(high, 64), lane_roll(low, 63))]
    down = [jnp.where(lower_lanes, lane_roll(high, 65), lane_roll(low, 64)), across]
    return (
        jnp.concatenate([part[None] for part in up], axis=0),
        jnp.concatenate([part[None] for part in down], axis=0),
    )


def turned(field):
    shape = (field.size // 1024, 8, 128)
    same = (iota(shape, 1) >= 4) == (iota(shape, 2) >= 64)
    tiles = field.reshape(shape)
    return jnp.where(same, tiles, roll(roll(tiles, 4, 1), 64, 2)).reshape(field.shape)


def agg_rows(tile):
    tile = tile + roll(tile, 64, 1)
    tile = tile + roll(tile, -1, 0)
    tile = tile + roll(tile, -2, 0)
    return jnp.where(iota((1, 128), 1) < 64, tile[0:1], tile[4:5])


def xor_sum(values, step, axis):
    place = iota(values.shape, axis)
    return values + jnp.where(
        (place & step) == 0, roll(values, -step, axis), roll(values, step, axis)
    )


def xor_upper(values, step, axis):
    place = iota(values.shape, axis)
    return jnp.where((place & step) == 0, roll(values, -step, axis), values)


def only_if(condition, action):
    if condition is None:
        action()
    else:
        pl.when(condition)(action)


def send(src, dst, send_sem, recv_sem, device):
    pltpu.make_async_remote_copy(
        src_ref=src,
        dst_ref=dst,
        send_sem=send_sem,
        recv_sem=recv_sem,
        device_id=device,
        device_id_type=MESH,
    ).start()


def wait_bytes(like, sem):
    pltpu.make_async_copy(like, like, sem).wait()


def kernel(
    count_x,
    count_y,
    rhs_any,
    acc_any,
    tx_any,
    ty_any,
    tz_any,
    cells_any,
    flags_any,
    rates_any,
    index_any,
    map_any,
    inv_any,
    both_any,
    fields_in,
    map_in,
    cells,
    flags,
    rates,
    well_index,
    inv_in,
    blocks,
    source,
    coef,
    face_x,
    face_y,
    halo_x,
    halo_y,
    ends_in,
    ends_send,
    gop_send,
    gop,
    gres_send,
    gres,
    beside_send,
    beside,
    edge_send,
    edge_in,
    tail,
    tail_send,
    tail_in,
    out_buf,
    agg,
    resid_two,
    side_x,
    side_y,
    late_send_x,
    late_send_y,
    late_x,
    late_y,
    blocks_x,
    blocks_y,
    sizes,
    load_sem,
    store_sem,
    face_send_sem,
    face_recv_sem,
    ends_sem,
    gop_sem,
    gres_sem,
    beside_sem,
    edge_sem,
    tail_sem,
    agg_sem,
    more_sem,
    near_sem,
    end_sem,
):
    index_x = lax.axis_index("gx")
    index_y = lax.axis_index("gy")
    rank = lax.rem(index_x, GROUP)
    base = index_x - rank
    next_x = (lax.rem(index_x + 1, count_x), index_y)
    prev_x = (lax.rem(index_x + count_x - 1, count_x), index_y)
    next_y = (index_x, lax.rem(index_y + 1, count_y))
    prev_y = (index_x, lax.rem(index_y + count_y - 1, count_y))
    sides = (next_x, prev_x, next_y, prev_y)
    steps = sorted(range(GROUP), key=lambda step: -min(step % 8, -step % 8))
    members = [base + lax.rem(rank + step, GROUP) for step in steps]
    mates = [(member, index_y) for step, member in zip(steps, members) if step > 0]
    upper_group = [(member, next_y[1]) for member in members]
    lower_group = [(member, prev_y[1]) for member in members]
    has_next = index_x < count_x - 1
    has_prev = index_x > 0
    group_after = base + GROUP < count_x
    group_before = base > 0
    last_member = group_after & (rank == GROUP - 1)
    first_member = group_before & (rank == 0)
    send_if = (has_next, has_prev, None, None)

    loads = [
        pltpu.make_async_copy(src, dst, load_sem.at[place])
        for place, (src, dst) in enumerate(
            (
                (inv_any, inv_in),
                (rhs_any, fields_in.at[0]),
                (tx_any, fields_in.at[1]),
                (ty_any, fields_in.at[2]),
                (tz_any, fields_in.at[3]),
                (acc_any, fields_in.at[4]),
                (map_any, map_in),
                (cells_any, cells),
                (flags_any, flags),
                (rates_any, rates),
                (index_any, well_index),
            )
        )
    ]
    for load in loads:
        load.start()
    halo_x[...] = jnp.zeros_like(halo_x)
    ends_in[...] = jnp.zeros_like(ends_in)
    edge_in[...] = jnp.zeros_like(edge_in)
    tail_in[...] = jnp.zeros_like(tail_in)
    side_x[...] = jnp.zeros_like(side_x)
    late_x[...] = jnp.zeros_like(late_x)

    barrier = pltpu.get_barrier_semaphore()

    def member(step_z, step_y):
        place = lax.rem(rank // 8 + step_y, 2) * 8 + lax.rem(lax.rem(rank, 8) + step_z + 8, 8)
        return base + place

    near = []
    for step_z in (2, -2, 1, -1, 0):
        near.append((member(step_z, 1), index_y))
        near.append((member(step_z, 0), next_y[1]))
        near.append((member(step_z, 0), prev_y[1]))
        if step_z != 0:
            near.append((member(step_z, 0), index_y))

    def announce(semaphore):
        for device in near:
            pl.semaphore_signal(semaphore, inc=1, device_id=device, device_id_type=MESH)
        announce_end(semaphore)

    def announce_end(semaphore):
        for condition, device in ((last_member, next_x), (first_member, prev_x)):
            only_if(
                condition,
                lambda device=device: pl.semaphore_signal(
                    semaphore, inc=1, device_id=device, device_id_type=MESH
                ),
            )

    group_end = last_member.astype(jnp.int32) + first_member.astype(jnp.int32)
    announced = len(near) + group_end
    announce(barrier)

    row = iota((DEPTH, DEPTH), 0)
    col = iota((DEPTH, DEPTH), 1)
    to_inside = (row == 4 * (col & 63) + (col >> 6)).astype(F32).astype(BF16)
    lane = iota(FIELD, 3)
    second = iota(FIELD, 2)
    first = iota(FIELD, 1)
    half = iota(FIELD, 0)
    cell_id = ((half * SIZE + first) * SIZE + second) * 128 + lane

    def swapped_offsets(place):
        return (place & ~15) | ((place & 3) << 2) | ((place >> 2) & 3)

    row_k = iota((128, DEPTH), 0)
    col_k = iota((128, DEPTH), 1)
    take_cols = ((row_k & 63) == swapped_offsets(col_k & 63)) & ((row_k < 64) == (col_k < 128))
    take_cols = take_cols.astype(F32).astype(BF16)
    loads[0].wait()
    tiles = [
        (OMEGA * inv_in[pl.ds(third, KINDS * 16, stride=4), :]).reshape(KINDS * 2, 8, 64)
        for third in range(4)
    ]
    upper_half = iota((KINDS * 2, 8, 64), 1) >= 4
    rows = jnp.concatenate(
        [
            tile[:, None]
            for tile in (
                jnp.where(upper_half, roll(tiles[1], 4, 1), tiles[0]),
                jnp.where(upper_half, roll(tiles[3], 4, 1), tiles[2]),
                jnp.where(upper_half, tiles[1], roll(tiles[0], 4, 1)),
                jnp.where(upper_half, tiles[3], roll(tiles[2], 4, 1)),
            )
        ],
        axis=1,
    ).reshape(KINDS * 64, 64)
    high, low = split_two(rows)
    blocks[...] = jnp.dot(
        jnp.concatenate([high, low], axis=1), take_cols, preferred_element_type=F32
    ).astype(BF16)

    for place in range(7, 11):
        loads[place].wait()
    plane_cells = SIZE * count_y * DEPTH
    well_ids = []
    for well in range(WELLS):
        cell = cells[well]
        pos_x = cell // plane_cells - index_x * SIZE
        left = lax.rem(cell, plane_cells)
        pos_y = left // DEPTH - index_y * SIZE
        pos_z = lax.rem(left, DEPTH)
        place = lax.rem(pos_z, 4) * 64 + pos_z // 4
        well_ids.append(
            ((place // 128 * SIZE + pos_x) * SIZE + pos_y) * 128 + lax.rem(place, 128)
        )
    signed = [
        jnp.where(flags[well] == 1, rates[well], -rates[well]) for well in range(WELLS)
    ]

    loads[1].wait()
    well_source = jnp.zeros(FIELD, F32)
    for well in range(WELLS):
        well_source = well_source + jnp.where(cell_id == well_ids[well], signed[well], 0.0)
    source[...] = (
        unflat(times_ones(fields_in[0].reshape(SIZE * SIZE, DEPTH), to_inside)) + well_source
    )

    loads[6].wait()
    kinds = []
    for part in range(2):
        kind = map_in[part]
        kinds.append(jnp.concatenate([kind[0:1], kind[1:2]], axis=1))
    kind_ids = jnp.broadcast_to(jnp.concatenate(kinds, axis=1), (8, 256))

    def products(field, operators, rows, kind_row):
        tiles = turned(field)
        columns = jnp.concatenate(
            [
                jnp.concatenate(
                    [
                        tiles[half_id, 4 * part + offset]
                        for offset in range(4)
                        for half_id in range(2)
                    ],
                    axis=0,
                )
                for part in range(2)
            ],
            axis=1,
        )
        high, low = split_two(columns)
        product = jnp.dot(
            operators[...],
            jnp.concatenate([high, low, high, low], axis=0),
            preferred_element_type=F32,
        )
        chosen = product[0:rows]
        for kind in range(1, KINDS):
            mask = jnp.broadcast_to((kind_row == kind)[None], (rows // 8, 8, 256))
            chosen = jnp.where(
                mask.reshape(rows, 256), product[rows * kind : rows * kind + rows], chosen
            )
        return chosen

    def smooth(resid, operators=blocks, kind_row=kind_ids):
        chosen = products(resid, operators, 64, kind_row)
        back = [
            [
                chosen[8 * (2 * offset + half_id) : 8 * (2 * offset + half_id) + 8,
                       128 * part : 128 * part + 128][None]
                for part in range(2)
                for offset in range(4)
            ]
            for half_id in range(2)
        ]
        field = jnp.concatenate(
            [jnp.concatenate(tiles, axis=0)[None] for tiles in back], axis=0
        )
        return turned(field)

    def send_faces(step, field):
        face_x[step, 0] = field[:, SIZE - 1]
        face_x[step, 1] = field[:, 0]
        tiles = field.reshape(2 * SIZE, 8, 128)
        face_y[step, 0] = tiles[:, 7:8, :]
        face_y[step, 1] = tiles[:, 0:1, :]
        for side, (out, into) in enumerate(
            ((face_x, halo_x), (face_x, halo_x), (face_y, halo_y), (face_y, halo_y))
        ):
            to_side(
                side,
                out.at[step, side % 2],
                into.at[step, side % 2],
                face_send_sem,
                face_recv_sem.at[step],
            )

    def to_side(side, src, dst, send_sems, recv_sems):
        kind = min(side, 2)
        only_if(
            send_if[side],
            lambda: send(src, dst, send_sems.at[kind], recv_sems.at[kind], sides[side]),
        )

    def wait_sides(buffer_x, buffer_y, sems):
        only_if(has_prev, lambda: wait_bytes(buffer_x[0], sems.at[0]))
        only_if(has_next, lambda: wait_bytes(buffer_x[1], sems.at[1]))
        wait_bytes(buffer_y, sems.at[2])

    def wait_faces(step):
        wait_sides(
            (halo_x.at[step, 0], halo_x.at[step, 1]), halo_y.at[step], face_recv_sem.at[step]
        )

    iterate = smooth(source[...])

    pl.semaphore_wait(barrier, announced)
    announce(near_sem)
    send_faces(0, iterate)

    loads[2].wait()
    loads[3].wait()
    ends_send[0, 0] = fields_in[1, SIZE - 1]
    for place in range(SIZE):
        ends_send[0, 1, place : place + 1] = fields_in[2, place, SIZE - 1 : SIZE, :]
    for side in range(2):
        to_side(2 * side, ends_send.at[0, side], ends_in.at[0, side], ends_sem.at[0], ends_sem.at[1])
    loads[4].wait()
    loads[5].wait()
    inside = times_ones(
        fields_in[1:5].reshape(4 * SIZE * SIZE, DEPTH), to_inside
    )
    tx, ty, tz, acc = [unflat(inside[64 * place : 64 * place + 64]) for place in range(4)]
    well_diag = jnp.zeros(FIELD, F32)
    for well in range(WELLS):
        well_diag = well_diag + jnp.where(cell_id == well_ids[well], well_index[well], 0.0)
    diag = acc + well_diag
    tx = jnp.where((first == SIZE - 1) & (index_x == count_x - 1), 0.0, tx)
    ty = jnp.where((second == SIZE - 1) & (index_y == count_y - 1), 0.0, ty)
    tz = jnp.where((half == 1) & (lane == 127), 0.0, tz)

    for part in range(2):
        mine = slice(4 * part, 4 * part + 4)
        gop_send[part : part + 1] = agg_rows(diag[:, mine].sum(axis=(0, 1)))
        gop_send[2 + part : 3 + part] = agg_rows(tx[:, 4 * part + 3].sum(axis=0))
        tile = ty[:, mine].sum(axis=(0, 1))
        tile = tile + roll(tile, 64, 1)
        gop_send[4 + part : 5 + part] = jnp.where(
            iota((1, 128), 1) < 64, tile[3:4], tile[7:8]
        )
        tile = tz[1, mine].sum(axis=0)
        gop_send[6 + part : 7 + part] = agg_rows(
            jnp.where(iota((8, 128), 1) >= 64, tile, 0.0)
        )

    tz_down = jnp.where((half == 0) & (lane == 0), 0.0, z_neighbours(tz)[1])
    agg[0] = diag
    agg[1] = jnp.zeros(FIELD, F32)
    for place, layer in ((3, 3), (4, 3), (7, 7)):
        agg[1, :, place] = tx[:, layer]
    for part in range(2):
        agg[1, 0, 4 * part + 1] = kind_ids[:, 128 * part : 128 * part + 128].astype(F32)
    agg[2] = jnp.where(
        (second & 3) == 3, ty, jnp.where(second == 4, row_roll(ty, 1), 0.0)
    )
    agg[3] = jnp.where(
        (half == 0) & (lane < 64), tz_down, jnp.where((half == 1) & (lane >= 64), tz, 0.0)
    )


    def to_all(devices, mine, target, sems):
        for device in devices:
            send(mine, target, sems.at[0], sems.at[1], device)

    for side, part in enumerate((slice(4, 8), slice(0, 4))):
        to_side(side, agg.at[:, :, part], side_x.at[side, 0:4], agg_sem.at[0], agg_sem.at[1])
        to_side(2 + side, agg, side_y.at[side, 0:4], agg_sem.at[0], agg_sem.at[1])

    for kind in range(KINDS):
        blocks_x[32 * kind : 32 * kind + 16, :] = blocks[64 * kind : 64 * kind + 16, :]
        blocks_x[32 * kind + 16 : 32 * kind + 32, :] = blocks[64 * kind + 48 : 64 * kind + 64, :]
    mirror = (col == (row ^ 3)).astype(F32).astype(BF16)
    for part in range(KINDS // 4):
        here = slice(part * DEPTH, (part + 1) * DEPTH)
        blocks_y[here, :] = jnp.dot(
            mirror, blocks[here, :], preferred_element_type=F32
        ).astype(BF16)

    pl.semaphore_wait(near_sem, announced)
    announce_end(end_sem)
    to_all(mates, gop_send, gop.at[rank], gop_sem)
    gop[rank] = gop_send[...]

    only_if(has_prev, lambda: wait_bytes(ends_in.at[0, 0], ends_sem.at[1, 0]))
    wait_bytes(ends_in.at[0, 1], ends_sem.at[1, 2])
    end_rows = times_ones(ends_in[0].reshape(2 * SIZE, DEPTH), to_inside)
    end_x = jnp.where(index_x == 0, 0.0, end_rows[0:SIZE])
    end_y = jnp.where(index_y == 0, 0.0, end_rows[SIZE:])
    end_x = jnp.concatenate([end_x[None, None, :, :128], end_x[None, None, :, 128:]], axis=0)
    tx_down = jnp.concatenate([end_x, tx[:, : SIZE - 1]], axis=1)
    for part in range(2):
        for place in range(SIZE):
            late_send_x[SIZE * part + place] = end_y[
                place : place + 1, 128 * part : 128 * part + 128
            ]
    late_send_y[...] = end_x[:, 0]
    end_y = jnp.broadcast_to(late_send_x[...], (2 * SIZE, 8, 128)).reshape(FIELD)
    ty_in = jnp.where(second == SIZE - 1, 0.0, ty)
    ty_down_in = row_roll(ty_in, 1)
    ty_edge = ty - ty_in
    ty_down_edge = jnp.where(second == 0, end_y, 0.0)
    coef[0] = (
        diag + tx + tx_down + ty + ty_down_in + ty_down_edge + tz + tz_down
    )
    coef[1] = tx
    coef[2] = tx_down
    coef[3] = ty_in
    coef[4] = ty_down_in
    coef[5] = tz
    coef[6] = tz_down
    coef[7] = ty_edge
    coef[8] = ty_down_edge
    tx_at = [tx[:, 3], tx[:, 7]]

    def resid_base(field):
        nothing = jnp.zeros((2, 1, SIZE, 128), F32)
        up_z, down_z = z_neighbours(field)
        return (
            source[...]
            - coef[0] * field
            + coef[1] * jnp.concatenate([field[:, 1:], nothing], axis=1)
            + coef[2] * jnp.concatenate([nothing, field[:, : SIZE - 1]], axis=1)
            + coef[3] * row_roll(field, -1)
            + coef[4] * row_roll(field, 1)
            + coef[5] * up_z
            + coef[6] * down_z
        )

    def resid_edges(resid, high_x, low_x, high_y, low_y):
        first_row = resid[:, 0:1] + (coef[2, :, 0] * low_x)[:, None]
        last_row = resid[:, SIZE - 1 :] + (coef[1, :, SIZE - 1] * high_x)[:, None]
        resid = jnp.concatenate([first_row, resid[:, 1 : SIZE - 1], last_row], axis=1)
        return resid + coef[7] * high_y + coef[8] * low_y

    def halos(step):
        spread = [
            jnp.broadcast_to(halo_y[step, side], (2 * SIZE, 8, 128)).reshape(FIELD)
            for side in (1, 0)
        ]
        return halo_x[step, 1], halo_x[step, 0], spread[0], spread[1]

    resid = resid_base(iterate)
    wait_faces(0)
    resid = resid_edges(resid, *halos(0))
    iterate = iterate + smooth(resid)

    send_faces(1, iterate)
    resid = resid_base(iterate)

    for part in range(2):
        mine = slice(4 * part, 4 * part + 4)
        gres_send[:, 128 * part : 128 * part + 128] = agg_rows(resid[:, mine].sum(axis=(0, 1)))
    flux_up = agg_rows((coef[1, :, SIZE - 1] * iterate[:, SIZE - 1]).sum(axis=0))
    flux_down = agg_rows((coef[2, :, 0] * iterate[:, 0]).sum(axis=0))
    gres_send[:, 256:384] = flux_up
    gres_send[:, 384:512] = flux_down
    edge_send[0] = flux_up
    edge_send[1] = flux_down
    for side in range(2):
        flux = coef[7 + side] * iterate
        lines = []
        for part in range(2):
            tile = flux[:, 4 * part : 4 * part + 4].sum(axis=(0, 1))
            tile = tile + roll(tile, 64, 1)
            lines.append(tile[7:8] if side == 0 else tile[0:1])
        beside_send[side] = jnp.where(iota((1, 128), 1) < 64, lines[0], lines[1])
    to_all(mates, gres_send, gres.at[rank], gres_sem)
    to_all(upper_group, beside_send.at[0], beside.at[0, rank], beside_sem)
    to_all(lower_group, beside_send.at[1], beside.at[1, rank], beside_sem)

    def to_edge(side, target):
        for step in range(GROUP):
            send(
                edge_send.at[side],
                edge_in.at[side, 0],
                edge_sem.at[0, side],
                edge_sem.at[1, side],
                (target + step, index_y),
            )

    only_if(last_member | first_member, lambda: pl.semaphore_wait(end_sem, 1))
    only_if(last_member, lambda: to_edge(0, base + GROUP))
    only_if(first_member, lambda: to_edge(1, base - GROUP))
    gres[rank] = gres_send[...]

    wait_bytes(gop.at[1:], gop_sem.at[1])
    shape = (GROUP, 128)
    member = iota(shape, 0)
    lane_c = iota(shape, 1)
    deep = lane_c & 63
    base_a, base_b, tx_a, tx_b, ty_a, ty_b, tz_a, tz_b = [
        gop[:, place, :] for place in range(8)
    ]

    def y_terms(values):
        return jnp.where(lane_c < 64, values, roll(values, 64, 1))

    def z_terms(values, step):
        up = jnp.where(deep < 64 - step, values, 0.0)
        down = jnp.where(deep >= step, roll(values, step, 1), 0.0)
        return up, down

    across_up = jnp.where((member & 1) == 0, tx_b, 0.0)
    across_down = jnp.where((member & 1) == 1, roll(tx_b, 1, 0), 0.0)
    y_a, y_b = y_terms(ty_a), y_terms(ty_b)
    (zu_a, zd_a), (zu_b, zd_b) = z_terms(tz_a, 1), z_terms(tz_b, 1)
    diag_a = base_a + tx_a + across_down + y_a + zu_a + zd_a
    diag_b = base_b + tx_a + across_up + y_b + zu_b + zd_b
    weight_a, weight_b = OMEGA / diag_a, OMEGA / diag_b

    def apply_one(field_a, field_b):
        out_a = (
            diag_a * field_a
            - tx_a * field_b
            - across_down * roll(field_b, 1, 0)
            - y_a * roll(field_a, 64, 1)
            - zu_a * roll(field_a, -1, 1)
            - zd_a * roll(field_a, 1, 1)
        )
        out_b = (
            diag_b * field_b
            - tx_a * field_a
            - across_up * roll(field_a, -1, 0)
            - y_b * roll(field_b, 64, 1)
            - zu_b * roll(field_b, -1, 1)
            - zd_b * roll(field_b, 1, 1)
        )
        return out_a, out_b

    levels = []
    weights = []
    base_k = xor_sum(base_a + base_b, 1, 1)
    tx_k = xor_sum(tx_b, 1, 1)
    ty_k = xor_sum(ty_a + ty_b, 1, 1)
    tz_k = xor_upper(tz_a + tz_b, 1, 1)
    for level in range(2, 5):
        step_x, step_z = 1 << (level - 2), 1 << (level - 1)
        cell_x = member >> (level - 2)
        up_x = jnp.where((cell_x & 3) != 3, tx_k, 0.0)
        down_x = jnp.where((cell_x & 3) != 0, roll(tx_k, step_x, 0), 0.0)
        both_y = y_terms(ty_k)
        up_z, down_z = z_terms(tz_k, step_z)
        diag_k = base_k + up_x + down_x + both_y + up_z + down_z
        levels.append((diag_k, up_x, down_x, both_y, up_z, down_z, step_x, step_z))
        weights.append(OMEGA / diag_k)
        if level < 4:
            base_k = xor_sum(xor_sum(base_k, step_x, 0), step_z, 1)
            ty_k = xor_sum(xor_sum(ty_k, step_x, 0), step_z, 1)
            tx_k = xor_sum(xor_upper(tx_k, step_x, 0), step_z, 1)
            tz_k = xor_upper(xor_sum(tz_k, step_x, 0), step_z, 1)

    def apply_level(field, terms):
        diag_k, up_x, down_x, both_y, up_z, down_z, step_x, step_z = terms
        return (
            diag_k * field
            - up_x * roll(field, -step_x, 0)
            - down_x * roll(field, step_x, 0)
            - both_y * roll(field, 64, 1)
            - up_z * roll(field, -step_z, 1)
            - down_z * roll(field, step_z, 1)
        )

    lane_row = iota((128, 128), 0)
    lane_col = iota((128, 128), 1)
    real = lane_col < 64
    same_place = ((lane_row >> 6) == ((lane_col >> 3) & 1)) & (
        ((lane_row & 63) >> 3) == (lane_col & 7)
    )
    pick_one = (real & same_place & ((lane_row & 7) == 0)).astype(F32).astype(BF16)
    pick_two = (real & same_place & ((lane_row & 3) == 0)).astype(F32).astype(BF16)
    own_x = (member >> 2) == (lane_c >> 4)
    diag_k, up_x, down_x, both_y, up_z, down_z, _, _ = levels[2]
    picked = times_ones(
        jnp.concatenate(
            [1.0 / diag_k, up_x, down_x, both_y, up_z, down_z], axis=0
        ),
        pick_one,
    )
    one_member = own_x & ((member & 3) == 0)
    inverse_diag, up_x, down_x, both_y, up_z, down_z = [
        jnp.sum(
            jnp.where(one_member, picked[GROUP * place : GROUP * place + GROUP], 0.0),
            axis=0,
            keepdims=True,
        )
        for place in range(6)
    ]
    gap = lane_row - lane_col
    upper_y = (lane_col >> 3) & 1
    coupling = jnp.where(gap == 16, up_x, 0.0)
    coupling = jnp.where(gap == -16, down_x, coupling)
    coupling = jnp.where(gap == 8 - 16 * upper_y, both_y, coupling)
    coupling = jnp.where(gap == 1, up_z, coupling)
    coupling = jnp.where(gap == -1, down_z, coupling)
    power = coupling * inverse_diag
    total = jnp.where(gap == 0, 1.0, 0.0)

    def doubled(total, power):
        both = jnp.dot(
            jnp.concatenate([total, power], axis=0),
            power,
            precision=HIGHEST,
            preferred_element_type=F32,
        )
        return total + both[:128], both[128:]

    for _ in range(DOUBLINGS - LATE_DOUBLINGS):
        total, power = doubled(total, power)
    spread = jnp.concatenate(
        [
            ((lane_row >> 4) == part)
            & ((lane_row >> 3 & 1) == (lane_col >> 6))
            & ((lane_row & 7) == ((lane_col & 63) >> 3))
            & (lane_row < 64)
            for part in range(4)
        ],
        axis=1,
    )

    wait_faces(1)
    high_x, low_x, high_y, low_y = halos(1)
    resid = resid_edges(resid, high_x, low_x, high_y, low_y)
    resid_two[...] = resid
    for side, part in enumerate((slice(4, 8), slice(0, 4))):
        to_side(side, resid_two.at[:, part], side_x.at[side, 4], more_sem.at[0], more_sem.at[1])
        to_side(side, late_send_x, late_x.at[side], more_sem.at[0], more_sem.at[1])
        to_side(2 + side, resid_two, side_y.at[side, 4], more_sem.at[0], more_sem.at[1])
        to_side(2 + side, late_send_y, late_y.at[side], more_sem.at[0], more_sem.at[1])

    wait_bytes(gres.at[1:], gres_sem.at[1])
    wait_bytes(beside, beside_sem.at[1])
    only_if(group_before, lambda: wait_bytes(edge_in.at[0, 0], edge_sem.at[1, 0]))
    only_if(group_after, lambda: wait_bytes(edge_in.at[1, 0], edge_sem.at[1, 1]))
    every = gres[:, 0, :]
    first_a, first_b, from_low, from_high = [
        every[:, 128 * part : 128 * part + 128] for part in range(4)
    ]
    from_low = jnp.where(member == 0, edge_in[0, 0], roll(from_low, 1, 0))
    from_high = jnp.where(member == GROUP - 1, edge_in[1, 0], roll(from_high, -1, 0))
    below, above = beside[0, :, 0, :], beside[1, :, 0, :]
    res_a = first_a + from_low + jnp.where(lane_c < 64, below, roll(above, 64, 1))
    res_b = first_b + from_high + jnp.where(lane_c < 64, roll(below, 64, 1), above)

    for _ in range(LATE_DOUBLINGS):
        total, power = doubled(total, power)

    def descend_one(res_a, res_b):
        cor_a, cor_b = weight_a * res_a, weight_b * res_b
        out_a, out_b = apply_one(cor_a, cor_b)
        cor_a = cor_a + weight_a * (res_a - out_a)
        cor_b = cor_b + weight_b * (res_b - out_b)
        out_a, out_b = apply_one(cor_a, cor_b)
        return cor_a, cor_b, (res_a - out_a) + (res_b - out_b)

    cor_a, cor_b, left = descend_one(res_a, res_b)
    res_k = xor_sum(left, 1, 1)
    cor_k = jnp.zeros(shape, F32)
    for level in (2, 3):
        terms = levels[level - 2]
        weight = weights[level - 2]
        cor = weight * res_k
        cor = cor + weight * (res_k - apply_level(cor, terms))
        left = res_k - apply_level(cor, terms)
        cor_k = cor_k + cor
        if level == 2:
            res_k = xor_sum(xor_sum(left, 1, 0), 2, 1)
    last = times_ones(left, pick_two)
    last = jnp.sum(
        jnp.where(own_x & ((member & 1) == 0), last, 0.0), axis=0, keepdims=True
    )
    last = jnp.broadcast_to(last * inverse_diag, (8, 128))
    solved = jnp.dot(last, total, precision=HIGHEST, preferred_element_type=F32)
    solved = times_ones(solved, spread.astype(F32).astype(BF16))
    solved = [jnp.broadcast_to(solved[0:1, 128 * part : 128 * part + 128], (8, 128)) for part in range(4)]
    upper_rows = (iota((8, 128), 0) & 4) != 0
    cor_k = cor_k + jnp.concatenate(
        [
            jnp.where(upper_rows, solved[1], solved[0]),
            jnp.where(upper_rows, solved[3], solved[2]),
        ],
        axis=0,
    )
    tail[0] = cor_a + cor_k
    tail[1] = cor_b + cor_k
    tail_send[0] = tail[0, pl.ds(rank, 1), :]
    tail_send[1] = tail[1, pl.ds(rank, 1), :]
    def tails_to(slot, kind, other_x):
        for step, other_y in ((1, next_y[1]), (2, prev_y[1]), (0, index_y)):
            send(
                tail_send,
                tail_in.at[slot + step],
                tail_sem.at[0, kind],
                tail_sem.at[1, kind],
                (other_x, other_y),
            )

    only_if(has_next, lambda: tails_to(0, 0, next_x[0]))
    only_if(has_prev, lambda: tails_to(3, 1, prev_x[0]))
    for side in range(2):
        send(tail_send, tail_in.at[6 + side], tail_sem.at[0, 2], tail_sem.at[1, 2], sides[2 + side])

    def wait_bulk(sem, tiles_x, tiles_y):
        wait_sides(
            (sizes.at[0:tiles_x], sizes.at[0:tiles_x]), sizes.at[0 : 2 * tiles_y], sem
        )

    wait_bulk(agg_sem.at[1], 32, 64)
    wait_bulk(more_sem.at[1], 10, 18)

    def both_x(place):
        return jnp.concatenate([side_x[0, place], side_x[1, place]], axis=1)

    def both_y(low, high):
        shape = low.shape
        low, high = low.reshape(-1, 8, 128), high.reshape(-1, 8, 128)
        return roll(jnp.where(iota(low.shape, 1) < 4, high, low), 4, 1).reshape(shape)

    diag_x, y_x, z_x, resid_x = [both_x(place) for place in (0, 2, 3, 4)]
    diag_y, x_y, y_y, z_y, resid_y = [
        both_y(side_y[0, place], side_y[1, place]) for place in range(5)
    ]
    rows_x = [
        jnp.broadcast_to(late_x[side], (2 * SIZE, 8, 128)).reshape(FIELD) for side in range(2)
    ]
    rows_x = jnp.concatenate([rows_x[0][:, 4:], rows_x[1][:, :4]], axis=1)
    y_x = y_x + jnp.where(second == 0, rows_x, 0.0)
    y_y = y_y + row_roll(coef[7], -3)
    first_x = both_y(late_y[0], late_y[1])
    kinds_x = jnp.concatenate([side_x[0, 1, 0, 1], side_x[1, 1, 0, 1]], axis=1)
    lower = iota((1, 128), 1) < 64

    def swap_halves(line):
        return roll(line, 64, 1)

    kinds_y = jnp.concatenate(
        [
            swap_halves(
                jnp.where(
                    iota((8, 128), 1) < 64,
                    side_y[1, 1, 0, 4 * part + 1],
                    side_y[0, 1, 0, 4 * part + 1],
                )
            )
            for part in range(2)
        ],
        axis=1,
    )

    own = [tail_send[part] for part in range(2)]
    wait_sides((tail_in.at[0:3], tail_in.at[3:6]), tail_in.at[6:8], tail_sem.at[1])
    low_mid, low_from_low, low_from_high = [tail_in[place, 1] for place in (0, 1, 2)]
    low_far = tail_in[0, 0]
    high_mid, high_from_low, high_from_high = [tail_in[place, 0] for place in (3, 4, 5)]
    high_far = tail_in[3, 1]
    below = [tail_in[6, part] for part in range(2)]
    above = [tail_in[7, part] for part in range(2)]

    def y_lines(mid, from_low, from_high):
        return (
            swap_halves(jnp.where(lower, from_high, mid)),
            swap_halves(jnp.where(lower, mid, from_low)),
        )

    def spread_lines(lines):
        return turned(
            jnp.concatenate(
                [jnp.broadcast_to(line, (8, 128))[None] for line in lines], axis=0
            )
        )

    def minus_coarse(resid, diag_f, x_low, x_high, y_f, z_f, mid, x_lines, y_pair):
        up, down = y_pair
        tiles = spread_lines(
            [mid, x_lines[0], x_lines[1], up, down, roll(mid, 1, 1), roll(mid, -1, 1)]
        )
        value = tiles[0]
        across_y = value - jnp.where((iota((8, 128), 0) & 3) == 3, tiles[3], tiles[4])
        across_z = jnp.concatenate(
            [(value - tiles[5])[None, None], (value - tiles[6])[None, None]], axis=0
        )
        resid = resid - diag_f * value - y_f * across_y - z_f * across_z
        first_layer = resid[:, 0:1] - (x_low * (value - tiles[1]))[:, None]
        last_layer = resid[:, 3:4] - (x_high * (value - tiles[2]))[:, None]
        return jnp.concatenate([first_layer, resid[:, 1:3], last_layer], axis=1), value

    def two_rows(resid, fields, x_faces, mids, x_lines, y_pairs):
        parts = [
            minus_coarse(
                resid[:, 4 * part : 4 * part + 4],
                fields[0][:, 4 * part : 4 * part + 4],
                x_faces[part][0],
                x_faces[part][1],
                fields[1][:, 4 * part : 4 * part + 4],
                fields[2][:, 4 * part : 4 * part + 4],
                mids[part],
                x_lines[part],
                y_pairs[part],
            )
            for part in range(2)
        ]
        return jnp.concatenate([parts[0][0], parts[1][0]], axis=1), [part[1] for part in parts]

    resid, own_tiles = two_rows(
        resid,
        (agg[0], agg[2] + coef[8], agg[3]),
        ((coef[2, :, 0], tx_at[0]), (tx_at[0], tx_at[1])),
        own,
        ((low_mid, own[1]), (own[0], high_mid)),
        [y_lines(own[part], below[part], above[part]) for part in range(2)],
    )
    resid_x, tiles_x = two_rows(
        resid_x,
        (diag_x, y_x, z_x),
        ((side_x[0, 1, :, 0], side_x[0, 1, :, 3]), (tx_at[1], side_x[1, 1, :, 3])),
        (low_mid, high_mid),
        ((low_far, own[0]), (own[1], high_far)),
        (
            y_lines(low_mid, low_from_low, low_from_high),
            y_lines(high_mid, high_from_low, high_from_high),
        ),
    )

    def beside_y(low, high):
        return swap_halves(jnp.where(lower, high, low))

    mids_y = [beside_y(below[part], above[part]) for part in range(2)]
    resid_y, tiles_y = two_rows(
        resid_y,
        (diag_y, y_y, z_y),
        ((first_x, x_y[:, 3]), (x_y[:, 4], x_y[:, 7])),
        mids_y,
        (
            (beside_y(low_from_low, low_from_high), mids_y[1]),
            (mids_y[0], beside_y(high_from_low, high_from_high)),
        ),
        [
            (
                jnp.where(lower, own[part], above[part]),
                jnp.where(lower, below[part], own[part]),
            )
            for part in range(2)
        ],
    )

    def over_layers(tiles):
        tiles = jnp.concatenate([tiles[place // 4][None] for place in range(SIZE)], axis=0)
        return jnp.broadcast_to(tiles[None], FIELD)

    iterate = iterate + over_layers(own_tiles) + smooth(resid)
    outer_x = products(resid_x, blocks_x, 32, kinds_x)
    low_x = low_x + tiles_x[0][None] + turned(outer_x[16:32, :128].reshape(2, 8, 128))
    high_x = high_x + tiles_x[1][None] + turned(outer_x[0:16, 128:].reshape(2, 8, 128))
    outer_y = jnp.where(second < 4, low_y, high_y) + over_layers(tiles_y)
    outer_y = outer_y + smooth(resid_y, blocks_y, kinds_y)
    resid = resid_edges(resid_base(iterate), high_x, low_x, outer_y, outer_y)
    iterate = iterate + smooth(resid)

    send_faces(2, iterate)
    out_buf[0] = iterate
    stores = [
        pltpu.make_async_copy(out_buf.at[place], both_any.at[place], store_sem.at[place])
        for place in range(2)
    ]
    stores[0].start()
    resid = resid_base(iterate)
    wait_faces(2)
    out_buf[1] = resid_edges(resid, *halos(2))
    stores[1].start()
    only_if(has_next, lambda: wait_bytes(face_x.at[:, 0], face_send_sem.at[0]))
    only_if(has_prev, lambda: wait_bytes(face_x.at[:, 1], face_send_sem.at[1]))
    wait_bytes(face_y, face_send_sem.at[2])
    only_if(has_next, lambda: wait_bytes(ends_send.at[0, 0], ends_sem.at[0, 0]))
    wait_bytes(ends_send.at[0, 1], ends_sem.at[0, 2])
    wait_bytes(gop.at[1:], gop_sem.at[0])
    wait_bytes(gres.at[1:], gres_sem.at[0])
    wait_bytes(beside, beside_sem.at[0])
    only_if(last_member, lambda: wait_bytes(edge_in.at[0], edge_sem.at[0, 0]))
    only_if(first_member, lambda: wait_bytes(edge_in.at[1], edge_sem.at[0, 1]))
    only_if(has_next, lambda: wait_bytes(tail_in.at[0:3], tail_sem.at[0, 0]))
    only_if(has_prev, lambda: wait_bytes(tail_in.at[3:6], tail_sem.at[0, 1]))
    wait_bytes(tail_in.at[6:8], tail_sem.at[0, 2])
    for sem, tiles_x, tiles_y in ((agg_sem.at[0], 32, 64), (more_sem.at[0], 10, 18)):
        only_if(has_next, lambda: wait_bytes(sizes.at[0:tiles_x], sem.at[0]))
        only_if(has_prev, lambda: wait_bytes(sizes.at[0:tiles_x], sem.at[1]))
        wait_bytes(sizes.at[0 : 2 * tiles_y], sem.at[2])
    for store in stores:
        store.wait()


def to_outer_order(both, pressure, resid):
    row = iota((DEPTH, DEPTH), 0)
    col = iota((DEPTH, DEPTH), 1)
    to_outside = (col == 4 * (row & 63) + (row >> 6)).astype(F32).astype(BF16)
    for place, out in enumerate((pressure, resid)):
        out[...] = times_ones(flat(both[place]), to_outside).reshape(SIZE, SIZE, DEPTH)


def on_device(
    count_x,
    count_y,
    pressure_rhs,
    accumulation,
    trans_x,
    trans_y,
    trans_z,
    well_cells,
    well_flags,
    well_rates,
    well_index,
    block_map,
    block_inverses,
):
    anywhere = pl.BlockSpec(memory_space=pl.ANY)
    dma = pltpu.SemaphoreType.DMA
    out = jax.ShapeDtypeStruct(pressure_rhs.shape, F32)
    both = pl.pallas_call(
        functools.partial(kernel, count_x, count_y),
        out_shape=jax.ShapeDtypeStruct((2,) + FIELD, F32),
        in_specs=[anywhere] * 11,
        out_specs=anywhere,
        scratch_shapes=[
            pltpu.VMEM((5, SIZE, SIZE, DEPTH), F32),
            pltpu.VMEM((2, 2, 64), jnp.int32),
            pltpu.SMEM((WELLS,), jnp.int32),
            pltpu.SMEM((WELLS,), jnp.int32),
            pltpu.SMEM((WELLS,), F32),
            pltpu.SMEM((WELLS,), F32),
            pltpu.VMEM((KINDS * 64, 64), F32),
            pltpu.VMEM((KINDS * 64, DEPTH), BF16),
            pltpu.VMEM(FIELD, F32),
            pltpu.VMEM((9,) + FIELD, F32),
            pltpu.VMEM((3, 2, 2, SIZE, 128), F32),
            pltpu.VMEM((3, 2, 2 * SIZE, 1, 128), F32),
            pltpu.VMEM((3, 2, 2, SIZE, 128), F32),
            pltpu.VMEM((3, 2, 2 * SIZE, 1, 128), F32),
            pltpu.VMEM((1, 2, SIZE, DEPTH), F32),
            pltpu.VMEM((1, 2, SIZE, DEPTH), F32),
            pltpu.VMEM((8, 128), F32),
            pltpu.VMEM((GROUP, 8, 128), F32),
            pltpu.VMEM((1, 512), F32),
            pltpu.VMEM((GROUP, 1, 512), F32),
            pltpu.VMEM((2, 1, 128), F32),
            pltpu.VMEM((2, GROUP, 1, 128), F32),
            pltpu.VMEM((2, 1, 128), F32),
            pltpu.VMEM((2, GROUP, 1, 128), F32),
            pltpu.VMEM((2, GROUP, 128), F32),
            pltpu.VMEM((2, 1, 128), F32),
            pltpu.VMEM((8, 2, 1, 128), F32),
            pltpu.VMEM((2,) + FIELD, F32),
            pltpu.VMEM((4,) + FIELD, F32),
            pltpu.VMEM(FIELD, F32),
            pltpu.VMEM((2, 5, 2, 4, 8, 128), F32),
            pltpu.VMEM((2, 5) + FIELD, F32),
            pltpu.VMEM((2 * SIZE, 1, 128), F32),
            pltpu.VMEM((2, SIZE, 128), F32),
            pltpu.VMEM((2, 2 * SIZE, 1, 128), F32),
            pltpu.VMEM((2, 2, SIZE, 128), F32),
            pltpu.VMEM((KINDS * 32, DEPTH), BF16),
            pltpu.VMEM((KINDS * 64, DEPTH), BF16),
            pltpu.VMEM((128, 8, 128), F32),
            dma((11,)),
            dma((2,)),
            dma((3,)),
            dma((3, 3)),
            dma((2, 3)),
            dma((2,)),
            dma((2,)),
            dma((2,)),
            dma((2, 2)),
            dma((2, 3)),
            dma((2, 3)),
            dma((2, 3)),
            pltpu.SemaphoreType.REGULAR,
            pltpu.SemaphoreType.REGULAR,
        ],
        compiler_params=pltpu.CompilerParams(
            collective_id=0, has_side_effects=True, vmem_limit_bytes=60 * 1024 * 1024
        ),
    )(
        pressure_rhs,
        accumulation,
        trans_x,
        trans_y,
        trans_z,
        well_cells,
        well_flags,
        well_rates,
        well_index,
        block_map,
        block_inverses.reshape(KINDS * 64, 64),
    )
    return pl.pallas_call(to_outer_order, out_shape=(out, out))(both)


def solution(mesh):
    cells = P("gx", "gy", None)
    wells = P(("gx", "gy"))
    return jax.shard_map(
        functools.partial(on_device, mesh.shape["gx"], mesh.shape["gy"]),
        mesh=mesh,
        in_specs=(cells,) * 5 + (wells,) * 4 + (cells, P()),
        out_specs=(cells, cells),
        check_vma=False,
    )
```

```python
import functools

import jax
import jax.numpy as jnp
from jax import lax
from jax.experimental import pallas as pl
from jax.experimental.pallas import tpu as pltpu
from jax.sharding import PartitionSpec as P

OMEGA = 0.8
GROUP = 16
SIZE = 8
DEPTH = 256
KINDS = 16
WELLS = 4
DOUBLINGS = 9
LATE_DOUBLINGS = 4
MESH = pl.DeviceIdType.MESH
HIGHEST = lax.Precision.HIGHEST
F32 = jnp.float32
BF16 = jnp.bfloat16
FIELD = (2, SIZE, SIZE, 128)


def iota(shape, dim):
    return lax.broadcasted_iota(jnp.int32, shape, dim)


def roll(values, shift, axis):
    return pltpu.roll(values, shift % values.shape[axis], axis)


def split_three(values):
    high = values.astype(BF16)
    rest = values - high.astype(F32)
    middle = rest.astype(BF16)
    low = (rest - middle.astype(F32)).astype(BF16)
    return high, middle, low


def split_two(values):
    high = values.astype(BF16)
    low = (values - high.astype(F32)).astype(BF16)
    return high, low


def times_ones(values, ones):
    return sum(jnp.dot(part, ones, preferred_element_type=F32) for part in split_three(values))


def flat(field):
    return jnp.concatenate(
        [field[0].reshape(SIZE * SIZE, 128), field[1].reshape(SIZE * SIZE, 128)], axis=1
    )


def unflat(rows):
    shape = (1, SIZE, SIZE, 128)
    return jnp.concatenate(
        [rows[:, :128].reshape(shape), rows[:, 128:].reshape(shape)], axis=0
    )


def lane_roll(field, shift):
    return roll(field.reshape(-1, 8, 128), shift, 2).reshape(field.shape)


def row_roll(field, shift):
    return roll(field.reshape(-1, 8, 128), shift, 1).reshape(field.shape)


def z_neighbours(field):
    low, high = field[0], field[1]
    lower_lanes = iota(low.shape, 2) < 64
    across = lane_roll(jnp.where(lower_lanes, high, low), 64)
    up = [across, jnp.where(lower_lanes, lane_roll(high, 64), lane_roll(low, 63))]
    down = [jnp.where(lower_lanes, lane_roll(high, 65), lane_roll(low, 64)), across]
    return (
        jnp.concatenate([part[None] for part in up], axis=0),
        jnp.concatenate([part[None] for part in down], axis=0),
    )


def turned(field):
    shape = (field.size // 1024, 8, 128)
    same = (iota(shape, 1) >= 4) == (iota(shape, 2) >= 64)
    tiles = field.reshape(shape)
    return jnp.where(same, tiles, roll(roll(tiles, 4, 1), 64, 2)).reshape(field.shape)


def agg_rows(tile):
    tile = tile + roll(tile, 64, 1)
    tile = tile + roll(tile, -1, 0)
    tile = tile + roll(tile, -2, 0)
    return jnp.where(iota((1, 128), 1) < 64, tile[0:1], tile[4:5])


def xor_sum(values, step, axis):
    place = iota(values.shape, axis)
    return values + jnp.where(
        (place & step) == 0, roll(values, -step, axis), roll(values, step, axis)
    )


def xor_upper(values, step, axis):
    place = iota(values.shape, axis)
    return jnp.where((place & step) == 0, roll(values, -step, axis), values)


def only_if(condition, action):
    if condition is None:
        action()
    else:
        pl.when(condition)(action)


def send(src, dst, send_sem, recv_sem, device):
    pltpu.make_async_remote_copy(
        src_ref=src,
        dst_ref=dst,
        send_sem=send_sem,
        recv_sem=recv_sem,
        device_id=device,
        device_id_type=MESH,
    ).start()


def wait_bytes(like, sem):
    pltpu.make_async_copy(like, like, sem).wait()


def kernel(
    count_x,
    count_y,
    rhs_any,
    acc_any,
    tx_any,
    ty_any,
    tz_any,
    cells_any,
    flags_any,
    rates_any,
    index_any,
    map_any,
    inv_any,
    both_any,
    fields_in,
    map_in,
    cells,
    flags,
    rates,
    well_index,
    inv_in,
    blocks,
    source,
    coef,
    face_x,
    face_y,
    halo_x,
    halo_y,
    ends_in,
    ends_send,
    gop_send,
    gop,
    gres_send,
    gres,
    beside_send,
    beside,
    edge_send,
    edge_in,
    tail,
    tail_send,
    tail_in,
    out_buf,
    agg,
    resid_two,
    side_x,
    side_y,
    late_send_x,
    late_send_y,
    late_x,
    late_y,
    blocks_x,
    blocks_y,
    sizes,
    load_sem,
    store_sem,
    face_send_sem,
    face_recv_sem,
    ends_sem,
    gop_sem,
    gres_sem,
    beside_sem,
    edge_sem,
    tail_sem,
    agg_sem,
    more_sem,
    near_sem,
    end_sem,
):
    index_x = lax.axis_index("gx")
    index_y = lax.axis_index("gy")
    rank = lax.rem(index_x, GROUP)
    base = index_x - rank
    next_x = (lax.rem(index_x + 1, count_x), index_y)
    prev_x = (lax.rem(index_x + count_x - 1, count_x), index_y)
    next_y = (index_x, lax.rem(index_y + 1, count_y))
    prev_y = (index_x, lax.rem(index_y + count_y - 1, count_y))
    sides = (next_x, prev_x, next_y, prev_y)
    steps = sorted(range(GROUP), key=lambda step: -min(step % 8, -step % 8))
    members = [base + lax.rem(rank + step, GROUP) for step in steps]
    mates = [(member, index_y) for step, member in zip(steps, members) if step > 0]
    upper_group = [(member, next_y[1]) for member in members]
    lower_group = [(member, prev_y[1]) for member in members]
    has_next = index_x < count_x - 1
    has_prev = index_x > 0
    group_after = base + GROUP < count_x
    group_before = base > 0
    last_member = group_after & (rank == GROUP - 1)
    first_member = group_before & (rank == 0)
    send_if = (has_next, has_prev, None, None)

    loads = [
        pltpu.make_async_copy(src, dst, load_sem.at[place])
        for place, (src, dst) in enumerate(
            (
                (inv_any, inv_in),
                (rhs_any, fields_in.at[0]),
                (tx_any, fields_in.at[1]),
                (ty_any, fields_in.at[2]),
                (tz_any, fields_in.at[3]),
                (acc_any, fields_in.at[4]),
                (map_any, map_in),
                (cells_any, cells),
                (flags_any, flags),
                (rates_any, rates),
                (index_any, well_index),
            )
        )
    ]
    for load in loads:
        load.start()
    halo_x[...] = jnp.zeros_like(halo_x)
    ends_in[...] = jnp.zeros_like(ends_in)
    edge_in[...] = jnp.zeros_like(edge_in)
    tail_in[...] = jnp.zeros_like(tail_in)
    side_x[...] = jnp.zeros_like(side_x)
    late_x[...] = jnp.zeros_like(late_x)

    barrier = pltpu.get_barrier_semaphore()

    def member(step_z, step_y):
        place = lax.rem(rank // 8 + step_y, 2) * 8 + lax.rem(lax.rem(rank, 8) + step_z + 8, 8)
        return base + place

    near = []
    for step_z in (2, -2, 1, -1, 0):
        near.append((member(step_z, 1), index_y))
        near.append((member(step_z, 0), next_y[1]))
        near.append((member(step_z, 0), prev_y[1]))
        if step_z != 0:
            near.append((member(step_z, 0), index_y))

    def announce(semaphore):
        for device in near:
            pl.semaphore_signal(semaphore, inc=1, device_id=device, device_id_type=MESH)
        announce_end(semaphore)

    def announce_end(semaphore):
        for condition, device in ((last_member, next_x), (first_member, prev_x)):
            only_if(
                condition,
                lambda device=device: pl.semaphore_signal(
                    semaphore, inc=1, device_id=device, device_id_type=MESH
                ),
            )

    group_end = last_member.astype(jnp.int32) + first_member.astype(jnp.int32)
    announced = len(near) + group_end
    announce(barrier)

    row = iota((DEPTH, DEPTH), 0)
    col = iota((DEPTH, DEPTH), 1)
    to_inside = (row == 4 * (col & 63) + (col >> 6)).astype(F32).astype(BF16)
    lane = iota(FIELD, 3)
    second = iota(FIELD, 2)
    first = iota(FIELD, 1)
    half = iota(FIELD, 0)
    cell_id = ((half * SIZE + first) * SIZE + second) * 128 + lane

    def swapped_offsets(place):
        return (place & ~15) | ((place & 3) << 2) | ((place >> 2) & 3)

    row_k = iota((128, DEPTH), 0)
    col_k = iota((128, DEPTH), 1)
    take_cols = ((row_k & 63) == swapped_offsets(col_k & 63)) & ((row_k < 64) == (col_k < 128))
    take_cols = take_cols.astype(F32).astype(BF16)
    loads[0].wait()
    tiles = [
        (OMEGA * inv_in[pl.ds(third, KINDS * 16, stride=4), :]).reshape(KINDS * 2, 8, 64)
        for third in range(4)
    ]
    upper_half = iota((KINDS * 2, 8, 64), 1) >= 4
    rows = jnp.concatenate(
        [
            tile[:, None]
            for tile in (
                jnp.where(upper_half, roll(tiles[1], 4, 1), tiles[0]),
                jnp.where(upper_half, roll(tiles[3], 4, 1), tiles[2]),
                jnp.where(upper_half, tiles[1], roll(tiles[0], 4, 1)),
                jnp.where(upper_half, tiles[3], roll(tiles[2], 4, 1)),
            )
        ],
        axis=1,
    ).reshape(KINDS * 64, 64)
    high, low = split_two(rows)
    blocks[...] = jnp.dot(
        jnp.concatenate([high, low], axis=1), take_cols, preferred_element_type=F32
    ).astype(BF16)

    for place in range(7, 11):
        loads[place].wait()
    plane_cells = SIZE * count_y * DEPTH
    well_ids = []
    for well in range(WELLS):
        cell = cells[well]
        pos_x = cell // plane_cells - index_x * SIZE
        left = lax.rem(cell, plane_cells)
        pos_y = left // DEPTH - index_y * SIZE
        pos_z = lax.rem(left, DEPTH)
        place = lax.rem(pos_z, 4) * 64 + pos_z // 4
        well_ids.append(
            ((place // 128 * SIZE + pos_x) * SIZE + pos_y) * 128 + lax.rem(place, 128)
        )
    signed = [
        jnp.where(flags[well] == 1, rates[well], -rates[well]) for well in range(WELLS)
    ]

    loads[1].wait()
    well_source = jnp.zeros(FIELD, F32)
    for well in range(WELLS):
        well_source = well_source + jnp.where(cell_id == well_ids[well], signed[well], 0.0)
    source[...] = (
        unflat(times_ones(fields_in[0].reshape(SIZE * SIZE, DEPTH), to_inside)) + well_source
    )

    loads[6].wait()
    kinds = []
    for part in range(2):
        kind = map_in[part]
        kinds.append(jnp.concatenate([kind[0:1], kind[1:2]], axis=1))
    kind_ids = jnp.broadcast_to(jnp.concatenate(kinds, axis=1), (8, 256))

    def products(field, operators, rows, kind_row):
        tiles = turned(field)
        columns = jnp.concatenate(
            [
                jnp.concatenate(
                    [
                        tiles[half_id, 4 * part + offset]
                        for offset in range(4)
                        for half_id in range(2)
                    ],
                    axis=0,
                )
                for part in range(2)
            ],
            axis=1,
        )
        high, low = split_two(columns)
        product = jnp.dot(
            operators[...],
            jnp.concatenate([high, low, high, low], axis=0),
            preferred_element_type=F32,
        )
        chosen = product[0:rows]
        for kind in range(1, KINDS):
            mask = jnp.broadcast_to((kind_row == kind)[None], (rows // 8, 8, 256))
            chosen = jnp.where(
                mask.reshape(rows, 256), product[rows * kind : rows * kind + rows], chosen
            )
        return chosen

    def smooth(resid, operators=blocks, kind_row=kind_ids):
        chosen = products(resid, operators, 64, kind_row)
        back = [
            [
                chosen[8 * (2 * offset + half_id) : 8 * (2 * offset + half_id) + 8,
                       128 * part : 128 * part + 128][None]
                for part in range(2)
                for offset in range(4)
            ]
            for half_id in range(2)
        ]
        field = jnp.concatenate(
            [jnp.concatenate(tiles, axis=0)[None] for tiles in back], axis=0
        )
        return turned(field)

    def send_faces(step, field):
        face_x[step, 0] = field[:, SIZE - 1]
        face_x[step, 1] = field[:, 0]
        tiles = field.reshape(2 * SIZE, 8, 128)
        face_y[step, 0] = tiles[:, 7:8, :]
        face_y[step, 1] = tiles[:, 0:1, :]
        for side, (out, into) in enumerate(
            ((face_x, halo_x), (face_x, halo_x), (face_y, halo_y), (face_y, halo_y))
        ):
            to_side(
                side,
                out.at[step, side % 2],
                into.at[step, side % 2],
                face_send_sem,
                face_recv_sem.at[step],
            )

    def to_side(side, src, dst, send_sems, recv_sems):
        kind = min(side, 2)
        only_if(
            send_if[side],
            lambda: send(src, dst, send_sems.at[kind], recv_sems.at[kind], sides[side]),
        )

    def wait_sides(buffer_x, buffer_y, sems):
        only_if(has_prev, lambda: wait_bytes(buffer_x[0], sems.at[0]))
        only_if(has_next, lambda: wait_bytes(buffer_x[1], sems.at[1]))
        wait_bytes(buffer_y, sems.at[2])

    def wait_faces(step):
        wait_sides(
            (halo_x.at[step, 0], halo_x.at[step, 1]), halo_y.at[step], face_recv_sem.at[step]
        )

    iterate = smooth(source[...])

    pl.semaphore_wait(barrier, announced)
    announce(near_sem)
    send_faces(0, iterate)

    loads[2].wait()
    loads[3].wait()
    ends_send[0, 0] = fields_in[1, SIZE - 1]
    for place in range(SIZE):
        ends_send[0, 1, place : place + 1] = fields_in[2, place, SIZE - 1 : SIZE, :]
    for side in range(2):
        to_side(2 * side, ends_send.at[0, side], ends_in.at[0, side], ends_sem.at[0], ends_sem.at[1])
    loads[4].wait()
    loads[5].wait()
    inside = times_ones(
        fields_in[1:5].reshape(4 * SIZE * SIZE, DEPTH), to_inside
    )
    tx, ty, tz, acc = [unflat(inside[64 * place : 64 * place + 64]) for place in range(4)]
    well_diag = jnp.zeros(FIELD, F32)
    for well in range(WELLS):
        well_diag = well_diag + jnp.where(cell_id == well_ids[well], well_index[well], 0.0)
    diag = acc + well_diag
    tx = jnp.where((first == SIZE - 1) & (index_x == count_x - 1), 0.0, tx)
    ty = jnp.where((second == SIZE - 1) & (index_y == count_y - 1), 0.0, ty)
    tz = jnp.where((half == 1) & (lane == 127), 0.0, tz)

    for part in range(2):
        mine = slice(4 * part, 4 * part + 4)
        gop_send[part : part + 1] = agg_rows(diag[:, mine].sum(axis=(0, 1)))
        gop_send[2 + part : 3 + part] = agg_rows(tx[:, 4 * part + 3].sum(axis=0))
        tile = ty[:, mine].sum(axis=(0, 1))
        tile = tile + roll(tile, 64, 1)
        gop_send[4 + part : 5 + part] = jnp.where(
            iota((1, 128), 1) < 64, tile[3:4], tile[7:8]
        )
        tile = tz[1, mine].sum(axis=0)
        gop_send[6 + part : 7 + part] = agg_rows(
            jnp.where(iota((8, 128), 1) >= 64, tile, 0.0)
        )

    tz_down = jnp.where((half == 0) & (lane == 0), 0.0, z_neighbours(tz)[1])
    agg[0] = diag
    agg[1] = jnp.zeros(FIELD, F32)
    for place, layer in ((3, 3), (4, 3), (7, 7)):
        agg[1, :, place] = tx[:, layer]
    for part in range(2):
        agg[1, 0, 4 * part + 1] = kind_ids[:, 128 * part : 128 * part + 128].astype(F32)
    agg[2] = jnp.where(
        (second & 3) == 3, ty, jnp.where(second == 4, row_roll(ty, 1), 0.0)
    )
    agg[3] = jnp.where(
        (half == 0) & (lane < 64), tz_down, jnp.where((half == 1) & (lane >= 64), tz, 0.0)
    )


    def to_all(devices, mine, target, sems):
        for device in devices:
            send(mine, target, sems.at[0], sems.at[1], device)

    for side, part in enumerate((slice(4, 8), slice(0, 4))):
        to_side(side, agg.at[:, :, part], side_x.at[side, 0:4], agg_sem.at[0], agg_sem.at[1])
        to_side(2 + side, agg, side_y.at[side, 0:4], agg_sem.at[0], agg_sem.at[1])

    for kind in range(KINDS):
        blocks_x[32 * kind : 32 * kind + 16, :] = blocks[64 * kind : 64 * kind + 16, :]
        blocks_x[32 * kind + 16 : 32 * kind + 32, :] = blocks[64 * kind + 48 : 64 * kind + 64, :]
    mirror = (col == (row ^ 3)).astype(F32).astype(BF16)
    for part in range(KINDS // 4):
        here = slice(part * DEPTH, (part + 1) * DEPTH)
        blocks_y[here, :] = jnp.dot(
            mirror, blocks[here, :], preferred_element_type=F32
        ).astype(BF16)

    pl.semaphore_wait(near_sem, announced)
    announce_end(end_sem)
    to_all(mates, gop_send, gop.at[rank], gop_sem)
    gop[rank] = gop_send[...]

    only_if(has_prev, lambda: wait_bytes(ends_in.at[0, 0], ends_sem.at[1, 0]))
    wait_bytes(ends_in.at[0, 1], ends_sem.at[1, 2])
    end_rows = times_ones(ends_in[0].reshape(2 * SIZE, DEPTH), to_inside)
    end_x = jnp.where(index_x == 0, 0.0, end_rows[0:SIZE])
    end_y = jnp.where(index_y == 0, 0.0, end_rows[SIZE:])
    end_x = jnp.concatenate([end_x[None, None, :, :128], end_x[None, None, :, 128:]], axis=0)
    tx_down = jnp.concatenate([end_x, tx[:, : SIZE - 1]], axis=1)
    for part in range(2):
        for place in range(SIZE):
            late_send_x[SIZE * part + place] = end_y[
                place : place + 1, 128 * part : 128 * part + 128
            ]
    late_send_y[...] = end_x[:, 0]
    end_y = jnp.broadcast_to(late_send_x[...], (2 * SIZE, 8, 128)).reshape(FIELD)
    ty_in = jnp.where(second == SIZE - 1, 0.0, ty)
    ty_down_in = row_roll(ty_in, 1)
    ty_edge = ty - ty_in
    ty_down_edge = jnp.where(second == 0, end_y, 0.0)
    coef[0] = (
        diag + tx + tx_down + ty + ty_down_in + ty_down_edge + tz + tz_down
    )
    coef[1] = tx
    coef[2] = tx_down
    coef[3] = ty_in
    coef[4] = ty_down_in
    coef[5] = tz
    coef[6] = tz_down
    coef[7] = ty_edge
    coef[8] = ty_down_edge
    tx_at = [tx[:, 3], tx[:, 7]]

    def resid_base(field):
        nothing = jnp.zeros((2, 1, SIZE, 128), F32)
        up_z, down_z = z_neighbours(field)
        return (
            source[...]
            - coef[0] * field
            + coef[1] * jnp.concatenate([field[:, 1:], nothing], axis=1)
            + coef[2] * jnp.concatenate([nothing, field[:, : SIZE - 1]], axis=1)
            + coef[3] * row_roll(field, -1)
            + coef[4] * row_roll(field, 1)
            + coef[5] * up_z
            + coef[6] * down_z
        )

    def resid_edges(resid, high_x, low_x, high_y, low_y):
        first_row = resid[:, 0:1] + (coef[2, :, 0] * low_x)[:, None]
        last_row = resid[:, SIZE - 1 :] + (coef[1, :, SIZE - 1] * high_x)[:, None]
        resid = jnp.concatenate([first_row, resid[:, 1 : SIZE - 1], last_row], axis=1)
        return resid + coef[7] * high_y + coef[8] * low_y

    def halos(step):
        spread = [
            jnp.broadcast_to(halo_y[step, side], (2 * SIZE, 8, 128)).reshape(FIELD)
            for side in (1, 0)
        ]
        return halo_x[step, 1], halo_x[step, 0], spread[0], spread[1]

    resid = resid_base(iterate)
    wait_faces(0)
    resid = resid_edges(resid, *halos(0))
    iterate = iterate + smooth(resid)

    send_faces(1, iterate)
    resid = resid_base(iterate)

    for part in range(2):
        mine = slice(4 * part, 4 * part + 4)
        gres_send[:, 128 * part : 128 * part + 128] = agg_rows(resid[:, mine].sum(axis=(0, 1)))
    flux_up = agg_rows((coef[1, :, SIZE - 1] * iterate[:, SIZE - 1]).sum(axis=0))
    flux_down = agg_rows((coef[2, :, 0] * iterate[:, 0]).sum(axis=0))
    gres_send[:, 256:384] = flux_up
    gres_send[:, 384:512] = flux_down
    edge_send[0] = flux_up
    edge_send[1] = flux_down
    for side in range(2):
        flux = coef[7 + side] * iterate
        lines = []
        for part in range(2):
            tile = flux[:, 4 * part : 4 * part + 4].sum(axis=(0, 1))
            tile = tile + roll(tile, 64, 1)
            lines.append(tile[7:8] if side == 0 else tile[0:1])
        beside_send[side] = jnp.where(iota((1, 128), 1) < 64, lines[0], lines[1])
    to_all(mates, gres_send, gres.at[rank], gres_sem)
    to_all(upper_group, beside_send.at[0], beside.at[0, rank], beside_sem)
    to_all(lower_group, beside_send.at[1], beside.at[1, rank], beside_sem)

    def to_edge(side, target):
        for step in range(GROUP):
            send(
                edge_send.at[side],
                edge_in.at[side, 0],
                edge_sem.at[0, side],
                edge_sem.at[1, side],
                (target + step, index_y),
            )

    only_if(last_member | first_member, lambda: pl.semaphore_wait(end_sem, 1))
    only_if(last_member, lambda: to_edge(0, base + GROUP))
    only_if(first_member, lambda: to_edge(1, base - GROUP))
    gres[rank] = gres_send[...]

    wait_faces(1)
    high_x, low_x, high_y, low_y = halos(1)
    resid = resid_edges(resid, high_x, low_x, high_y, low_y)
    resid_two[...] = resid
    for side, part in enumerate((slice(4, 8), slice(0, 4))):
        to_side(side, resid_two.at[:, part], side_x.at[side, 4], more_sem.at[0], more_sem.at[1])
        to_side(side, late_send_x, late_x.at[side], more_sem.at[0], more_sem.at[1])
        to_side(2 + side, resid_two, side_y.at[side, 4], more_sem.at[0], more_sem.at[1])
        to_side(2 + side, late_send_y, late_y.at[side], more_sem.at[0], more_sem.at[1])

    wait_bytes(gop.at[1:], gop_sem.at[1])
    shape = (GROUP, 128)
    member = iota(shape, 0)
    lane_c = iota(shape, 1)
    deep = lane_c & 63
    base_a, base_b, tx_a, tx_b, ty_a, ty_b, tz_a, tz_b = [
        gop[:, place, :] for place in range(8)
    ]

    def y_terms(values):
        return jnp.where(lane_c < 64, values, roll(values, 64, 1))

    def z_terms(values, step):
        up = jnp.where(deep < 64 - step, values, 0.0)
        down = jnp.where(deep >= step, roll(values, step, 1), 0.0)
        return up, down

    across_up = jnp.where((member & 1) == 0, tx_b, 0.0)
    across_down = jnp.where((member & 1) == 1, roll(tx_b, 1, 0), 0.0)
    y_a, y_b = y_terms(ty_a), y_terms(ty_b)
    (zu_a, zd_a), (zu_b, zd_b) = z_terms(tz_a, 1), z_terms(tz_b, 1)
    diag_a = base_a + tx_a + across_down + y_a + zu_a + zd_a
    diag_b = base_b + tx_a + across_up + y_b + zu_b + zd_b
    weight_a, weight_b = OMEGA / diag_a, OMEGA / diag_b

    def apply_one(field_a, field_b):
        out_a = (
            diag_a * field_a
            - tx_a * field_b
            - across_down * roll(field_b, 1, 0)
            - y_a * roll(field_a, 64, 1)
            - zu_a * roll(field_a, -1, 1)
            - zd_a * roll(field_a, 1, 1)
        )
        out_b = (
            diag_b * field_b
            - tx_a * field_a
            - across_up * roll(field_a, -1, 0)
            - y_b * roll(field_b, 64, 1)
            - zu_b * roll(field_b, -1, 1)
            - zd_b * roll(field_b, 1, 1)
        )
        return out_a, out_b

    levels = []
    weights = []
    base_k = xor_sum(base_a + base_b, 1, 1)
    tx_k = xor_sum(tx_b, 1, 1)
    ty_k = xor_sum(ty_a + ty_b, 1, 1)
    tz_k = xor_upper(tz_a + tz_b, 1, 1)
    for level in range(2, 5):
        step_x, step_z = 1 << (level - 2), 1 << (level - 1)
        cell_x = member >> (level - 2)
        up_x = jnp.where((cell_x & 3) != 3, tx_k, 0.0)
        down_x = jnp.where((cell_x & 3) != 0, roll(tx_k, step_x, 0), 0.0)
        both_y = y_terms(ty_k)
        up_z, down_z = z_terms(tz_k, step_z)
        diag_k = base_k + up_x + down_x + both_y + up_z + down_z
        levels.append((diag_k, up_x, down_x, both_y, up_z, down_z, step_x, step_z))
        weights.append(OMEGA / diag_k)
        if level < 4:
            base_k = xor_sum(xor_sum(base_k, step_x, 0), step_z, 1)
            ty_k = xor_sum(xor_sum(ty_k, step_x, 0), step_z, 1)
            tx_k = xor_sum(xor_upper(tx_k, step_x, 0), step_z, 1)
            tz_k = xor_upper(xor_sum(tz_k, step_x, 0), step_z, 1)

    def apply_level(field, terms):
        diag_k, up_x, down_x, both_y, up_z, down_z, step_x, step_z = terms
        return (
            diag_k * field
            - up_x * roll(field, -step_x, 0)
            - down_x * roll(field, step_x, 0)
            - both_y * roll(field, 64, 1)
            - up_z * roll(field, -step_z, 1)
            - down_z * roll(field, step_z, 1)
        )

    lane_row = iota((128, 128), 0)
    lane_col = iota((128, 128), 1)
    real = lane_col < 64
    same_place = ((lane_row >> 6) == ((lane_col >> 3) & 1)) & (
        ((lane_row & 63) >> 3) == (lane_col & 7)
    )
    pick_one = (real & same_place & ((lane_row & 7) == 0)).astype(F32).astype(BF16)
    pick_two = (real & same_place & ((lane_row & 3) == 0)).astype(F32).astype(BF16)
    own_x = (member >> 2) == (lane_c >> 4)
    diag_k, up_x, down_x, both_y, up_z, down_z, _, _ = levels[2]
    picked = times_ones(
        jnp.concatenate(
            [1.0 / diag_k, up_x, down_x, both_y, up_z, down_z], axis=0
        ),
        pick_one,
    )
    one_member = own_x & ((member & 3) == 0)
    inverse_diag, up_x, down_x, both_y, up_z, down_z = [
        jnp.sum(
            jnp.where(one_member, picked[GROUP * place : GROUP * place + GROUP], 0.0),
            axis=0,
            keepdims=True,
        )
        for place in range(6)
    ]
    gap = lane_row - lane_col
    upper_y = (lane_col >> 3) & 1
    coupling = jnp.where(gap == 16, up_x, 0.0)
    coupling = jnp.where(gap == -16, down_x, coupling)
    coupling = jnp.where(gap == 8 - 16 * upper_y, both_y, coupling)
    coupling = jnp.where(gap == 1, up_z, coupling)
    coupling = jnp.where(gap == -1, down_z, coupling)
    power = coupling * inverse_diag
    total = jnp.where(gap == 0, 1.0, 0.0)

    def doubled(total, power):
        both = jnp.dot(
            jnp.concatenate([total, power], axis=0),
            power,
            precision=HIGHEST,
            preferred_element_type=F32,
        )
        return total + both[:128], both[128:]

    for _ in range(DOUBLINGS - LATE_DOUBLINGS):
        total, power = doubled(total, power)
    spread = jnp.concatenate(
        [
            ((lane_row >> 4) == part)
            & ((lane_row >> 3 & 1) == (lane_col >> 6))
            & ((lane_row & 7) == ((lane_col & 63) >> 3))
            & (lane_row < 64)
            for part in range(4)
        ],
        axis=1,
    )

    wait_bytes(gres.at[1:], gres_sem.at[1])
    wait_bytes(beside, beside_sem.at[1])
    only_if(group_before, lambda: wait_bytes(edge_in.at[0, 0], edge_sem.at[1, 0]))
    only_if(group_after, lambda: wait_bytes(edge_in.at[1, 0], edge_sem.at[1, 1]))
    every = gres[:, 0, :]
    first_a, first_b, from_low, from_high = [
        every[:, 128 * part : 128 * part + 128] for part in range(4)
    ]
    from_low = jnp.where(member == 0, edge_in[0, 0], roll(from_low, 1, 0))
    from_high = jnp.where(member == GROUP - 1, edge_in[1, 0], roll(from_high, -1, 0))
    below, above = beside[0, :, 0, :], beside[1, :, 0, :]
    res_a = first_a + from_low + jnp.where(lane_c < 64, below, roll(above, 64, 1))
    res_b = first_b + from_high + jnp.where(lane_c < 64, roll(below, 64, 1), above)

    for _ in range(LATE_DOUBLINGS):
        total, power = doubled(total, power)

    def descend_one(res_a, res_b):
        cor_a, cor_b = weight_a * res_a, weight_b * res_b
        out_a, out_b = apply_one(cor_a, cor_b)
        cor_a = cor_a + weight_a * (res_a - out_a)
        cor_b = cor_b + weight_b * (res_b - out_b)
        out_a, out_b = apply_one(cor_a, cor_b)
        return cor_a, cor_b, (res_a - out_a) + (res_b - out_b)

    cor_a, cor_b, left = descend_one(res_a, res_b)
    res_k = xor_sum(left, 1, 1)
    cor_k = jnp.zeros(shape, F32)
    for level in (2, 3):
        terms = levels[level - 2]
        weight = weights[level - 2]
        cor = weight * res_k
        cor = cor + weight * (res_k - apply_level(cor, terms))
        left = res_k - apply_level(cor, terms)
        cor_k = cor_k + cor
        if level == 2:
            res_k = xor_sum(xor_sum(left, 1, 0), 2, 1)
    last = times_ones(left, pick_two)
    last = jnp.sum(
        jnp.where(own_x & ((member & 1) == 0), last, 0.0), axis=0, keepdims=True
    )
    last = jnp.broadcast_to(last * inverse_diag, (8, 128))
    solved = jnp.dot(last, total, precision=HIGHEST, preferred_element_type=F32)
    solved = times_ones(solved, spread.astype(F32).astype(BF16))
    solved = [jnp.broadcast_to(solved[0:1, 128 * part : 128 * part + 128], (8, 128)) for part in range(4)]
    upper_rows = (iota((8, 128), 0) & 4) != 0
    cor_k = cor_k + jnp.concatenate(
        [
            jnp.where(upper_rows, solved[1], solved[0]),
            jnp.where(upper_rows, solved[3], solved[2]),
        ],
        axis=0,
    )
    tail[0] = cor_a + cor_k
    tail[1] = cor_b + cor_k
    tail_send[0] = tail[0, pl.ds(rank, 1), :]
    tail_send[1] = tail[1, pl.ds(rank, 1), :]
    def tails_to(slot, kind, other_x):
        for step, other_y in ((1, next_y[1]), (2, prev_y[1]), (0, index_y)):
            send(
                tail_send,
                tail_in.at[slot + step],
                tail_sem.at[0, kind],
                tail_sem.at[1, kind],
                (other_x, other_y),
            )

    only_if(has_next, lambda: tails_to(0, 0, next_x[0]))
    only_if(has_prev, lambda: tails_to(3, 1, prev_x[0]))
    for side in range(2):
        send(tail_send, tail_in.at[6 + side], tail_sem.at[0, 2], tail_sem.at[1, 2], sides[2 + side])

    def wait_bulk(sem, tiles_x, tiles_y):
        wait_sides(
            (sizes.at[0:tiles_x], sizes.at[0:tiles_x]), sizes.at[0 : 2 * tiles_y], sem
        )

    wait_bulk(agg_sem.at[1], 32, 64)
    wait_bulk(more_sem.at[1], 10, 18)

    def both_x(place):
        return jnp.concatenate([side_x[0, place], side_x[1, place]], axis=1)

    def both_y(low, high):
        shape = low.shape
        low, high = low.reshape(-1, 8, 128), high.reshape(-1, 8, 128)
        return roll(jnp.where(iota(low.shape, 1) < 4, high, low), 4, 1).reshape(shape)

    diag_x, y_x, z_x, resid_x = [both_x(place) for place in (0, 2, 3, 4)]
    diag_y, x_y, y_y, z_y, resid_y = [
        both_y(side_y[0, place], side_y[1, place]) for place in range(5)
    ]
    rows_x = [
        jnp.broadcast_to(late_x[side], (2 * SIZE, 8, 128)).reshape(FIELD) for side in range(2)
    ]
    rows_x = jnp.concatenate([rows_x[0][:, 4:], rows_x[1][:, :4]], axis=1)
    y_x = y_x + jnp.where(second == 0, rows_x, 0.0)
    y_y = y_y + row_roll(coef[7], -3)
    first_x = both_y(late_y[0], late_y[1])
    kinds_x = jnp.concatenate([side_x[0, 1, 0, 1], side_x[1, 1, 0, 1]], axis=1)
    lower = iota((1, 128), 1) < 64

    def swap_halves(line):
        return roll(line, 64, 1)

    kinds_y = jnp.concatenate(
        [
            swap_halves(
                jnp.where(
                    iota((8, 128), 1) < 64,
                    side_y[1, 1, 0, 4 * part + 1],
                    side_y[0, 1, 0, 4 * part + 1],
                )
            )
            for part in range(2)
        ],
        axis=1,
    )

    own = [tail_send[part] for part in range(2)]
    wait_sides((tail_in.at[0:3], tail_in.at[3:6]), tail_in.at[6:8], tail_sem.at[1])
    low_mid, low_from_low, low_from_high = [tail_in[place, 1] for place in (0, 1, 2)]
    low_far = tail_in[0, 0]
    high_mid, high_from_low, high_from_high = [tail_in[place, 0] for place in (3, 4, 5)]
    high_far = tail_in[3, 1]
    below = [tail_in[6, part] for part in range(2)]
    above = [tail_in[7, part] for part in range(2)]

    def y_lines(mid, from_low, from_high):
        return (
            swap_halves(jnp.where(lower, from_high, mid)),
            swap_halves(jnp.where(lower, mid, from_low)),
        )

    def spread_lines(lines):
        return turned(
            jnp.concatenate(
                [jnp.broadcast_to(line, (8, 128))[None] for line in lines], axis=0
            )
        )

    def minus_coarse(resid, diag_f, x_low, x_high, y_f, z_f, mid, x_lines, y_pair):
        up, down = y_pair
        tiles = spread_lines(
            [mid, x_lines[0], x_lines[1], up, down, roll(mid, 1, 1), roll(mid, -1, 1)]
        )
        value = tiles[0]
        across_y = value - jnp.where((iota((8, 128), 0) & 3) == 3, tiles[3], tiles[4])
        across_z = jnp.concatenate(
            [(value - tiles[5])[None, None], (value - tiles[6])[None, None]], axis=0
        )
        resid = resid - diag_f * value - y_f * across_y - z_f * across_z
        first_layer = resid[:, 0:1] - (x_low * (value - tiles[1]))[:, None]
        last_layer = resid[:, 3:4] - (x_high * (value - tiles[2]))[:, None]
        return jnp.concatenate([first_layer, resid[:, 1:3], last_layer], axis=1), value

    def two_rows(resid, fields, x_faces, mids, x_lines, y_pairs):
        parts = [
            minus_coarse(
                resid[:, 4 * part : 4 * part + 4],
                fields[0][:, 4 * part : 4 * part + 4],
                x_faces[part][0],
                x_faces[part][1],
                fields[1][:, 4 * part : 4 * part + 4],
                fields[2][:, 4 * part : 4 * part + 4],
                mids[part],
                x_lines[part],
                y_pairs[part],
            )
            for part in range(2)
        ]
        return jnp.concatenate([parts[0][0], parts[1][0]], axis=1), [part[1] for part in parts]

    resid, own_tiles = two_rows(
        resid,
        (agg[0], agg[2] + coef[8], agg[3]),
        ((coef[2, :, 0], tx_at[0]), (tx_at[0], tx_at[1])),
        own,
        ((low_mid, own[1]), (own[0], high_mid)),
        [y_lines(own[part], below[part], above[part]) for part in range(2)],
    )
    resid_x, tiles_x = two_rows(
        resid_x,
        (diag_x, y_x, z_x),
        ((side_x[0, 1, :, 0], side_x[0, 1, :, 3]), (tx_at[1], side_x[1, 1, :, 3])),
        (low_mid, high_mid),
        ((low_far, own[0]), (own[1], high_far)),
        (
            y_lines(low_mid, low_from_low, low_from_high),
            y_lines(high_mid, high_from_low, high_from_high),
        ),
    )

    def beside_y(low, high):
        return swap_halves(jnp.where(lower, high, low))

    mids_y = [beside_y(below[part], above[part]) for part in range(2)]
    resid_y, tiles_y = two_rows(
        resid_y,
        (diag_y, y_y, z_y),
        ((first_x, x_y[:, 3]), (x_y[:, 4], x_y[:, 7])),
        mids_y,
        (
            (beside_y(low_from_low, low_from_high), mids_y[1]),
            (mids_y[0], beside_y(high_from_low, high_from_high)),
        ),
        [
            (
                jnp.where(lower, own[part], above[part]),
                jnp.where(lower, below[part], own[part]),
            )
            for part in range(2)
        ],
    )

    def over_layers(tiles):
        tiles = jnp.concatenate([tiles[place // 4][None] for place in range(SIZE)], axis=0)
        return jnp.broadcast_to(tiles[None], FIELD)

    iterate = iterate + over_layers(own_tiles) + smooth(resid)
    outer_x = products(resid_x, blocks_x, 32, kinds_x)
    low_x = low_x + tiles_x[0][None] + turned(outer_x[16:32, :128].reshape(2, 8, 128))
    high_x = high_x + tiles_x[1][None] + turned(outer_x[0:16, 128:].reshape(2, 8, 128))
    outer_y = jnp.where(second < 4, low_y, high_y) + over_layers(tiles_y)
    outer_y = outer_y + smooth(resid_y, blocks_y, kinds_y)
    resid = resid_edges(resid_base(iterate), high_x, low_x, outer_y, outer_y)
    iterate = iterate + smooth(resid)

    send_faces(2, iterate)
    out_buf[0] = iterate
    stores = [
        pltpu.make_async_copy(out_buf.at[place], both_any.at[place], store_sem.at[place])
        for place in range(2)
    ]
    stores[0].start()
    resid = resid_base(iterate)
    wait_faces(2)
    out_buf[1] = resid_edges(resid, *halos(2))
    stores[1].start()
    only_if(has_next, lambda: wait_bytes(face_x.at[:, 0], face_send_sem.at[0]))
    only_if(has_prev, lambda: wait_bytes(face_x.at[:, 1], face_send_sem.at[1]))
    wait_bytes(face_y, face_send_sem.at[2])
    only_if(has_next, lambda: wait_bytes(ends_send.at[0, 0], ends_sem.at[0, 0]))
    wait_bytes(ends_send.at[0, 1], ends_sem.at[0, 2])
    wait_bytes(gop.at[1:], gop_sem.at[0])
    wait_bytes(gres.at[1:], gres_sem.at[0])
    wait_bytes(beside, beside_sem.at[0])
    only_if(last_member, lambda: wait_bytes(edge_in.at[0], edge_sem.at[0, 0]))
    only_if(first_member, lambda: wait_bytes(edge_in.at[1], edge_sem.at[0, 1]))
    only_if(has_next, lambda: wait_bytes(tail_in.at[0:3], tail_sem.at[0, 0]))
    only_if(has_prev, lambda: wait_bytes(tail_in.at[3:6], tail_sem.at[0, 1]))
    wait_bytes(tail_in.at[6:8], tail_sem.at[0, 2])
    for sem, tiles_x, tiles_y in ((agg_sem.at[0], 32, 64), (more_sem.at[0], 10, 18)):
        only_if(has_next, lambda: wait_bytes(sizes.at[0:tiles_x], sem.at[0]))
        only_if(has_prev, lambda: wait_bytes(sizes.at[0:tiles_x], sem.at[1]))
        wait_bytes(sizes.at[0 : 2 * tiles_y], sem.at[2])
    for store in stores:
        store.wait()


def to_outer_order(both, pressure, resid):
    row = iota((DEPTH, DEPTH), 0)
    col = iota((DEPTH, DEPTH), 1)
    to_outside = (col == 4 * (row & 63) + (row >> 6)).astype(F32).astype(BF16)
    for place, out in enumerate((pressure, resid)):
        out[...] = times_ones(flat(both[place]), to_outside).reshape(SIZE, SIZE, DEPTH)


def on_device(
    count_x,
    count_y,
    pressure_rhs,
    accumulation,
    trans_x,
    trans_y,
    trans_z,
    well_cells,
    well_flags,
    well_rates,
    well_index,
    block_map,
    block_inverses,
):
    anywhere = pl.BlockSpec(memory_space=pl.ANY)
    dma = pltpu.SemaphoreType.DMA
    out = jax.ShapeDtypeStruct(pressure_rhs.shape, F32)
    both = pl.pallas_call(
        functools.partial(kernel, count_x, count_y),
        out_shape=jax.ShapeDtypeStruct((2,) + FIELD, F32),
        in_specs=[anywhere] * 11,
        out_specs=anywhere,
        scratch_shapes=[
            pltpu.VMEM((5, SIZE, SIZE, DEPTH), F32),
            pltpu.VMEM((2, 2, 64), jnp.int32),
            pltpu.SMEM((WELLS,), jnp.int32),
            pltpu.SMEM((WELLS,), jnp.int32),
            pltpu.SMEM((WELLS,), F32),
            pltpu.SMEM((WELLS,), F32),
            pltpu.VMEM((KINDS * 64, 64), F32),
            pltpu.VMEM((KINDS * 64, DEPTH), BF16),
            pltpu.VMEM(FIELD, F32),
            pltpu.VMEM((9,) + FIELD, F32),
            pltpu.VMEM((3, 2, 2, SIZE, 128), F32),
            pltpu.VMEM((3, 2, 2 * SIZE, 1, 128), F32),
            pltpu.VMEM((3, 2, 2, SIZE, 128), F32),
            pltpu.VMEM((3, 2, 2 * SIZE, 1, 128), F32),
            pltpu.VMEM((1, 2, SIZE, DEPTH), F32),
            pltpu.VMEM((1, 2, SIZE, DEPTH), F32),
            pltpu.VMEM((8, 128), F32),
            pltpu.VMEM((GROUP, 8, 128), F32),
            pltpu.VMEM((1, 512), F32),
            pltpu.VMEM((GROUP, 1, 512), F32),
            pltpu.VMEM((2, 1, 128), F32),
            pltpu.VMEM((2, GROUP, 1, 128), F32),
            pltpu.VMEM((2, 1, 128), F32),
            pltpu.VMEM((2, GROUP, 1, 128), F32),
            pltpu.VMEM((2, GROUP, 128), F32),
            pltpu.VMEM((2, 1, 128), F32),
            pltpu.VMEM((8, 2, 1, 128), F32),
            pltpu.VMEM((2,) + FIELD, F32),
            pltpu.VMEM((4,) + FIELD, F32),
            pltpu.VMEM(FIELD, F32),
            pltpu.VMEM((2, 5, 2, 4, 8, 128), F32),
            pltpu.VMEM((2, 5) + FIELD, F32),
            pltpu.VMEM((2 * SIZE, 1, 128), F32),
            pltpu.VMEM((2, SIZE, 128), F32),
            pltpu.VMEM((2, 2 * SIZE, 1, 128), F32),
            pltpu.VMEM((2, 2, SIZE, 128), F32),
            pltpu.VMEM((KINDS * 32, DEPTH), BF16),
            pltpu.VMEM((KINDS * 64, DEPTH), BF16),
            pltpu.VMEM((128, 8, 128), F32),
            dma((11,)),
            dma((2,)),
            dma((3,)),
            dma((3, 3)),
            dma((2, 3)),
            dma((2,)),
            dma((2,)),
            dma((2,)),
            dma((2, 2)),
            dma((2, 3)),
            dma((2, 3)),
            dma((2, 3)),
            pltpu.SemaphoreType.REGULAR,
            pltpu.SemaphoreType.REGULAR,
        ],
        compiler_params=pltpu.CompilerParams(
            collective_id=0, has_side_effects=True, vmem_limit_bytes=60 * 1024 * 1024
        ),
    )(
        pressure_rhs,
        accumulation,
        trans_x,
        trans_y,
        trans_z,
        well_cells,
        well_flags,
        well_rates,
        well_index,
        block_map,
        block_inverses.reshape(KINDS * 64, 64),
    )
    return pl.pallas_call(to_outer_order, out_shape=(out, out))(both)


def solution(mesh):
    cells = P("gx", "gy", None)
    wells = P(("gx", "gy"))
    return jax.shard_map(
        functools.partial(on_device, mesh.shape["gx"], mesh.shape["gy"]),
        mesh=mesh,
        in_specs=(cells,) * 5 + (wells,) * 4 + (cells, P()),
        out_specs=(cells, cells),
        check_vma=False,
    )
```
